32 devices in a mesh: rep: 2 (over y), yz: 4 (over z), gx: 4 (over x, core).
Axes of the slice: x: 2, y: 2, z: 4, core: 2. Of those that a mesh axis runs over, the one named last changes fastest.
Arguments:
- saved_input: bfloat16 [8192, 9, 128], P(('rep', 'yz', 'gx')), parts along dimension 0, may hold values from -6 to 6
- cotangent: bfloat16 [4096, 9, 128], P(('rep', 'yz', 'gx')), parts along dimension 0, may hold values from -6 to 6
- neighbours: int32 [4096, 8], P(('rep', 'yz', 'gx')), parts along dimension 0, may hold values from 0 to 255
- rot_zero: float32 [32768], P(('rep', 'yz', 'gx')), parts along dimension 0, may hold values from -4 to 4
- rot_one: float32 [3, 3, 32768], P(None, None, ('rep', 'yz', 'gx')), parts along dimension 2, may hold values from -3 to 3
- rot_two: float32 [5, 5, 32768], P(None, None, ('rep', 'yz', 'gx')), parts along dimension 2, may hold values from -2.5 to 2.5
- send_index: int32 [128, 32], P(('rep', 'yz', 'gx')), parts along dimension 0, may hold values from 0 to 127
- atom_class: int32 [4096], P(('rep', 'yz', 'gx')), parts along dimension 0, may hold values from 0 to 1
- live_blocks: int32 [32], P(('rep', 'yz', 'gx')), parts along dimension 0, may hold values from 1 to 2, as said below
- merge_coef: float32 [2, 32], replicated, may hold values from 0.05 to 0.3
- experts: bfloat16 [32, 278528], P(None, 'yz'), may hold values from -0.375 to 0.375
Outputs:
- input_grad: bfloat16 [4096, 9, 128], P(('rep', 'yz', 'gx')), parts along dimension 0
- expert_grad: float32 [64, 278528], P(('rep', 'gx'), 'yz'), parts along dimension 0
The draws below stay inside these ranges and needn't reach their ends.
There are 2 independent parts, one for each index of `rep`. The reference program is written for one: setup_inputs(seed, part) draws one part's arguments, and reference() takes and returns one part's arrays. A program takes and returns all parts, laid end to end along the dimension named above; an argument that names none is the same for every part. Nothing has to cross between parts.
Inputs may be any that keep to these rules, and one draw needn't show every extreme that they name: `neighbours`: rows of the tile's own block: below 128 its atoms, the rest its ghosts. `send_index`: own atom slots of the tile; repeats may occur. Tile t's live atoms are slots 0 to 64 * live_blocks[t] - 1; in every draw some tile has all 2 blocks live.
All inputs are finite; a program needn't handle non-finite values.
Results may differ from the reference program's by a relative error of at most 0.0065.
Values may be sent and summed in bfloat16 or wider, within the bound.
No kernel may reach another device: no remote copies, remote signals or barrier semaphores. Data moves between devices by JAX's collectives and lax.ppermute only.
A program may use at most 128 MiB of HBM per device.

```python
import math
import jax
import jax.numpy as jnp
from jax import lax

C = 128
NEIGH = 8
EXPERTS = 32
CLASSES = 2
ATOM_DEV = 128
ATOM_BLOCK = 64
FACE = 32
TILES = 16
ATOMS = 2048
EDGES = 16384
SLOTS = 4096
BLOCKS = 2
PARAMS = 278528
N_YZ = 4
N_GX = 4


def draw_live_blocks(key, part):
    key = jax.random.fold_in(key, 7)
    first_key, second_key = jax.random.split(key)
    counts = jax.random.randint(first_key, (TILES,), 1, BLOCKS // 2 + 1)
    busiest = jax.random.randint(second_key, (), 0, TILES)
    return jnp.where(jnp.arange(TILES) == busiest, BLOCKS, counts).astype(jnp.int32)


def plant(result, stream_key, low, high):
    place = [jax.random.randint(jax.random.fold_in(stream_key, axis), (), 0, length) for axis, length in enumerate(result.shape)]
    widest = result.shape.index(max(result.shape))
    beside = place[:widest] + [(place[widest] + 1) % result.shape[widest]] + place[widest + 1:]
    return result.at[tuple(place)].set(low).at[tuple(beside)].set(high)


def block_levels(stream_key, shape, cuts, low, top_value):
    gain, own = 1.0, jax.random.fold_in(stream_key, 6)
    for axis_at, blocks in cuts:
        draws = jnp.exp(jax.random.uniform(jax.random.fold_in(own, axis_at), (blocks,), jnp.float32, low / len(cuts), top_value / len(cuts)))
        gain = gain * jnp.repeat(draws, shape[axis_at] // blocks).reshape([-1 if axis == axis_at else 1 for axis in range(len(shape))])
    return gain


def normal_values(stream_key, dims, deviation, most, cuts=(), held_as=jnp.bfloat16):
    drawn = deviation * jax.random.normal(stream_key, dims, jnp.float32)
    if cuts:
        drawn = drawn * block_levels(stream_key, dims, cuts, -0.22, 0.18)
    return jnp.clip(drawn, -most, most).astype(held_as)


def setup_inputs(seed: int = 0, part: int = 0) -> dict:
    streams_of = jax.random.split(jax.random.key(seed), 12)
    part_splits = jax.random.split(jax.random.fold_in(streams_of[11], part), 12)
    saved_input = normal_values(part_splits[0], (SLOTS, 9, C), 1.0, 6.0, ((0, 16),))
    cotangent = normal_values(part_splits[1], (ATOMS, 9, C), 1.0, 6.0, ((0, 16),))
    neighbours = plant(jax.random.randint(part_splits[2], (ATOMS, NEIGH), 0, ATOM_DEV + 4 * FACE), jax.random.fold_in(part_splits[2], 1), 0, (ATOM_DEV + 4 * FACE) - 1).astype(jnp.int32)
    rot_zero = normal_values(part_splits[3], (EDGES,), 1.0, 4.0, ((0, 16),), jnp.float32)
    rot_one = normal_values(part_splits[4], (3, 3, EDGES), 0.6, 3.0, ((2, 16),), jnp.float32)
    rot_two = normal_values(part_splits[5], (5, 5, EDGES), 0.45, 2.5, ((2, 16),), jnp.float32)
    send_index = plant(jax.random.randint(part_splits[6], (4 * TILES, FACE), 0, ATOM_DEV), jax.random.fold_in(part_splits[6], 1), 0, ATOM_DEV - 1).astype(jnp.int32)
    atom_class = plant(jax.random.randint(part_splits[7], (ATOMS,), 0, CLASSES), jax.random.fold_in(part_splits[7], 1), 0, CLASSES - 1).astype(jnp.int32)
    live_blocks = draw_live_blocks(jax.random.fold_in(jax.random.fold_in(streams_of[11], part), 71), part)
    merge_coef = jnp.clip(jax.random.uniform(streams_of[9], (CLASSES, EXPERTS), jnp.float32, 0.05, 0.3), 0.05, 0.3)
    experts = normal_values(streams_of[10], (EXPERTS, PARAMS), (2 * C) ** -0.5, 0.375, ((1, 4),))
    return {"saved_input": saved_input, "cotangent": cotangent, "neighbours": neighbours, "rot_zero": rot_zero, "rot_one": rot_one, "rot_two": rot_two, "send_index": send_index, "atom_class": atom_class, "live_blocks": live_blocks, "merge_coef": merge_coef, "experts": experts}


highest = lax.Precision.HIGHEST
zero_rows = (0, 2, 6)
pair_rows = (3, 7, 1, 5)

def rotate(field, turn_zero, turn_one, turn_two):
    first_part = turn_zero[:, None, None] * field[:, 0:1]
    second_part = jnp.einsum('abe,ebc->eac', turn_one, field[:, 1:4], precision=highest)
    third_part = jnp.einsum('abe,ebc->eac', turn_two, field[:, 4:9], precision=highest)
    return jnp.concatenate([first_part, second_part, third_part], axis=1)

def rotate_back(field, turn_zero, turn_one, turn_two):
    first_part = turn_zero[:, None, None] * field[:, 0:1]
    second_part = jnp.einsum('bae,ebc->eac', turn_one, field[:, 1:4], precision=highest)
    third_part = jnp.einsum('bae,ebc->eac', turn_two, field[:, 4:9], precision=highest)
    return jnp.concatenate([first_part, second_part, third_part], axis=1)

def pick_rows(field, positions):
    return jnp.concatenate([field[:, position] for position in positions], axis=1)

def class_weights(merged, channels):
    zero_width = 3 * channels
    pair_width = 2 * channels
    zero_parts = []
    pair_parts = []
    for member in range(merged.shape[0]):
        vector = merged[member]
        zero_parts.append(vector[:zero_width * zero_width].reshape(zero_width, zero_width))
        coupled = vector[zero_width * zero_width:zero_width * zero_width + pair_width * pair_width].reshape(pair_width, pair_width)
        crossed = vector[zero_width * zero_width + pair_width * pair_width:].reshape(pair_width, pair_width)
        top_rows = jnp.concatenate([coupled, crossed], axis=1)
        bottom_rows = jnp.concatenate([-crossed, coupled], axis=1)
        pair_parts.append(jnp.concatenate([top_rows, bottom_rows], axis=0))
    return (jnp.concatenate(zero_parts, axis=1), jnp.concatenate(pair_parts, axis=1))

def class_gradients(grad_zero, grad_pair, channels):
    zero_width = 3 * channels
    pair_width = 2 * channels
    members = grad_zero.shape[1] // zero_width
    vectors = []
    for member in range(members):
        zero_part = grad_zero[:, member * zero_width:(member + 1) * zero_width]
        pair_block = grad_pair[:, member * 2 * pair_width:(member + 1) * 2 * pair_width]
        coupled = pair_block[:pair_width, :pair_width] + pair_block[pair_width:, pair_width:]
        crossed = pair_block[:pair_width, pair_width:] - pair_block[pair_width:, :pair_width]
        vectors.append(jnp.concatenate([zero_part.reshape(-1), coupled.reshape(-1), crossed.reshape(-1)]))
    return jnp.stack(vectors)

def edge_terms(sources, targets, turn_zero, turn_one, turn_two, class_mask, zero_weight, pair_weight, fanout):
    channels = sources.shape[2]
    rotated = rotate(sources.astype(jnp.float32), turn_zero, turn_one, turn_two).astype(jnp.bfloat16)
    pulled = (rotate(targets.astype(jnp.float32), turn_zero, turn_one, turn_two) / math.sqrt(fanout)).astype(jnp.bfloat16)
    masks = class_mask.astype(jnp.bfloat16)
    members = class_mask.shape[1]
    zero_in = pick_rows(rotated, zero_rows)
    pair_in = pick_rows(rotated, pair_rows)
    zero_pulled = pick_rows(pulled, zero_rows)
    pair_pulled = pick_rows(pulled, pair_rows)
    zero_out = jnp.concatenate([zero_pulled * masks[:, member:member + 1] for member in range(members)], axis=1)
    pair_out = jnp.concatenate([pair_pulled * masks[:, member:member + 1] for member in range(members)], axis=1)
    over_edges = (((0,), (0,)), ((), ()))
    over_last = (((1,), (1,)), ((), ()))
    grad_zero = lax.dot_general(zero_in, zero_out, over_edges, preferred_element_type=jnp.float32)
    grad_pair = lax.dot_general(pair_in, pair_out, over_edges, preferred_element_type=jnp.float32)
    back_zero = lax.dot_general(zero_out, zero_weight, over_last, preferred_element_type=jnp.float32)
    back_pair = lax.dot_general(pair_out, pair_weight, over_last, preferred_element_type=jnp.float32)
    empty_part = jnp.zeros_like(back_zero[:, :channels])
    pieces = [empty_part] * 9
    for position, component in enumerate(zero_rows):
        pieces[component] = back_zero[:, position * channels:(position + 1) * channels]
    for position, component in enumerate(pair_rows):
        pieces[component] = back_pair[:, position * channels:(position + 1) * channels]
    turned = rotate_back(jnp.stack(pieces, axis=1), turn_zero, turn_one, turn_two)
    return (turned, grad_zero, grad_pair)

def reference(saved_input, cotangent, neighbours, rot_zero, rot_one, rot_two, send_index, atom_class, live_blocks, merge_coef, experts):
    merged = jnp.dot(merge_coef, experts.astype(jnp.float32), precision=highest).astype(jnp.bfloat16)
    zero_weight, pair_weight = class_weights(merged, C)
    rows_ext = ATOM_DEV + 4 * FACE
    edges_dev = ATOM_DEV * NEIGH
    inputs_tiled = saved_input.reshape(TILES, rows_ext, 9, C)
    targets_tiled = cotangent.reshape(TILES, ATOM_DEV, 9, C)
    sources_tiled = neighbours.reshape(TILES, edges_dev)
    zero_tiled = rot_zero.reshape(TILES, edges_dev)
    one_tiled = jnp.moveaxis(rot_one.reshape(3, 3, TILES, edges_dev), 2, 0)
    two_tiled = jnp.moveaxis(rot_two.reshape(5, 5, TILES, edges_dev), 2, 0)
    class_tiled = atom_class.reshape(TILES, ATOM_DEV)
    slot_ids = jnp.arange(ATOM_DEV, dtype=jnp.int32)
    member_ids = jnp.arange(CLASSES, dtype=jnp.int32)

    def tile_step(summed, tile):
        ext_rows, targets, source_rows, turn_zero, turn_one, turn_two, classes_here, live_count = tile
        alive = (slot_ids < live_count * ATOM_BLOCK).astype(jnp.float32)
        class_mask = (classes_here[:, None] == member_ids[None, :]).astype(jnp.float32) * alive[:, None]
        class_mask = jnp.repeat(class_mask, NEIGH, axis=0)
        expanded = jnp.repeat(targets, NEIGH, axis=0)
        turned, grad_zero, grad_pair = edge_terms(ext_rows[source_rows], expanded, turn_zero, turn_one, turn_two, class_mask, zero_weight, pair_weight, NEIGH)
        grad_ext = jnp.zeros((rows_ext, 9, C), jnp.float32).at[source_rows].add(turned)
        return (summed + class_gradients(grad_zero, grad_pair, C), grad_ext)
    summed, grad_ext = lax.scan(tile_step, jnp.zeros((CLASSES, PARAMS), jnp.float32), (inputs_tiled, targets_tiled, sources_tiled, zero_tiled, one_tiled, two_tiled, class_tiled, live_blocks))
    grid = grad_ext.reshape(N_YZ, N_GX, rows_ext, 9, C)
    owned = grid[:, :, :ATOM_DEV].reshape(TILES, ATOM_DEV, 9, C)
    ghosts = grid[:, :, ATOM_DEV:].reshape(N_YZ, N_GX, 4, FACE, 9, C)
    returned = jnp.stack([jnp.roll(ghosts[:, :, 1], 1, axis=1), jnp.roll(ghosts[:, :, 0], -1, axis=1), jnp.roll(ghosts[:, :, 3], 1, axis=0), jnp.roll(ghosts[:, :, 2], -1, axis=0)], axis=2)
    returned = returned.reshape(TILES, 4 * FACE, 9, C)
    face_rows = send_index.reshape(TILES, 4 * FACE)

    def add_faces(owned_rows, face_ids, face_grads):
        return owned_rows.at[face_ids].add(face_grads)
    input_grad = jax.vmap(add_faces)(owned, face_rows, returned).reshape(ATOMS, 9, C).astype(jnp.bfloat16)
    expert_grad = math.sqrt(NEIGH / ATOMS) * jnp.dot(merge_coef.T, summed, precision=highest)
    return (input_grad, expert_grad)
```

```python
import functools
import math

import jax
import jax.numpy as jnp
from jax import lax
from jax.experimental import pallas as pl
from jax.experimental.pallas import tpu as pltpu
from jax.sharding import PartitionSpec as P

LIVE_BLOCK = 64
CHUNK = 256
SUB = 16
F32 = jnp.float32
BF16 = jnp.bfloat16

STACK = (0, 2, 6, 3, 7, 1, 5)
SLOT = {component: place for place, component in enumerate(STACK)}

VMEM = pl.BlockSpec(memory_space=pltpu.VMEM)
SMEM = pl.BlockSpec(memory_space=pltpu.SMEM)
PARAMS = pltpu.CompilerParams(vmem_limit_bytes=56 * 1024 * 1024)


def nn(left, right):
    return lax.dot_general(left, right, (((1,), (0,)), ((), ())), preferred_element_type=F32)


def nt(left, right):
    return lax.dot_general(left, right, (((1,), (1,)), ((), ())), preferred_element_type=F32)


def split3(value):
    high = value.astype(BF16)
    rest = value - high.astype(F32)
    middle = rest.astype(BF16)
    low = (rest - middle.astype(F32)).astype(BF16)
    return high, middle, low


def merge_kernel(coef_ref, experts_ref, out_ref):
    members, wide = coef_ref.shape
    experts = experts_ref.shape[0]
    rows = out_ref.shape[1]
    row = lax.broadcasted_iota(jnp.int32, (8, wide), 0)
    col = lax.broadcasted_iota(jnp.int32, (8, wide), 1)
    diagonal = row == col // experts
    pieces = []
    for member in range(members):
        pieces.append(jnp.where(diagonal, coef_ref[member : member + 1, :], 0.0))
    left = jnp.concatenate(pieces, axis=0)
    lefts = jnp.concatenate(split3(left), axis=0)
    height = 8 * members
    for block in range(rows // 16):
        right = jnp.concatenate(
            [
                jnp.concatenate(
                    [
                        experts_ref[:, (block * 16 + half * 8 + g) * 128 : (block * 16 + half * 8 + g + 1) * 128]
                        for g in range(8)
                    ],
                    axis=0,
                )
                for half in range(2)
            ],
            axis=1,
        )
        product = nn(lefts, right)
        total = product[:height] + product[height : 2 * height] + product[2 * height :]
        for member in range(members):
            part = total[member * 8 : member * 8 + 8]
            out_ref[member, block * 16 : block * 16 + 16, :] = jnp.concatenate(
                [part[:, :128], part[:, 128:]], axis=0
            ).astype(BF16)


def merge(coef, experts, core, parts):
    members, count = coef.shape
    columns = experts.shape[1] // parts
    rows = columns // 128
    return pl.pallas_call(
        lambda ids_ref, coef_ref, experts_ref, out_ref: merge_kernel(coef_ref, experts_ref, out_ref),
        grid_spec=pltpu.PrefetchScalarGridSpec(
            num_scalar_prefetch=1,
            grid=(1,),
            in_specs=[
                pl.BlockSpec((members, 8 * count), lambda i, ids: (0, 0)),
                pl.BlockSpec((count, columns), lambda i, ids: (0, ids[0])),
            ],
            out_specs=pl.BlockSpec((members, rows, 128), lambda i, ids: (0, 0, 0)),
        ),
        out_shape=jax.ShapeDtypeStruct((members, rows, 128), BF16),
        compiler_params=PARAMS,
        name="merge",
    )(core, jnp.tile(coef, (1, 8)), experts)


def features_kernel(
    ids_ref, live_ref, near_ref, class_ref, zero_ref, one_ref, two_ref, source_ref, target_ref,
    other_ref, own_ref, pulled_ref, edge_ref,
    source_t, target_t, moved, spread, rotated, grads,
    *, fanout,
):
    slots, channels = source_ref.shape[1:]
    atoms = target_ref.shape[1]
    edges = atoms * fanout
    for c in range(9):
        source_t[c * channels : (c + 1) * channels, :] = source_ref[c].T
        target_t[c * channels : (c + 1) * channels, :] = target_ref[c].T
    near = near_ref[...].astype(F32).astype(BF16)
    classes = class_ref[...].astype(F32).astype(BF16)
    live_edges = live_ref[0] * LIVE_BLOCK * fanout
    scale = 1.0 / math.sqrt(fanout)

    def chunk_step(chunk, carry):
        start = pl.multiple_of(chunk * CHUNK, CHUNK)
        here = pl.ds(start, CHUNK)
        edge = lax.broadcasted_iota(jnp.int32, (atoms, CHUNK), 1) + start
        atom = lax.broadcasted_iota(jnp.int32, (atoms, CHUNK), 0)
        repeat = (edge // fanout == atom).astype(F32).astype(BF16)
        edge8 = lax.broadcasted_iota(jnp.int32, (fanout, CHUNK), 1) + start
        lane8 = lax.broadcasted_iota(jnp.int32, (fanout, CHUNK), 0)
        picked = jnp.where(edge8 % fanout == lane8, nn(near, repeat), 0.0)
        near_row = jnp.sum(picked, axis=0, keepdims=True)
        class_row = nn(classes, repeat)
        edge_ref[0:1, here] = near_row
        edge_ref[1:2, here] = jnp.where(edge8[0:1] < live_edges, class_row, -1.0)
        slot = lax.broadcasted_iota(jnp.int32, (slots, CHUNK), 0).astype(F32)
        pick = (slot == near_row).astype(F32).astype(BF16)
        moved[...] = nn(source_t[...], pick)
        spread[...] = nn(target_t[...], repeat)

        def sub_step(sub, inner):
            at = pl.multiple_of(sub * SUB, SUB)

            def turn(field, write):
                def part(c):
                    return field[pl.ds(c * channels + at, SUB), :]

                write(0, zero_ref[0:1, here] * part(0))
                values = [part(c) for c in (1, 2, 3)]
                for a in range(3):
                    total = one_ref[a, 0:1, here] * values[0]
                    for b in range(1, 3):
                        total += one_ref[a, b : b + 1, here] * values[b]
                    write(1 + a, total)
                values = [part(c) for c in (4, 5, 6, 7, 8)]
                for a in range(1, 4):
                    total = two_ref[a, 0:1, here] * values[0]
                    for b in range(1, 5):
                        total += two_ref[a, b : b + 1, here] * values[b]
                    write(4 + a, total)

            def write_rotated(c, value):
                rotated[pl.ds(SLOT[c] * channels + at, SUB), here] = value.astype(BF16)

            def write_pulled(c, value):
                pulled_ref[pl.ds(SLOT[c] * channels + at, SUB), here] = (value * scale).astype(BF16)

            turn(moved, write_rotated)
            turn(spread, write_pulled)
            return inner

        lax.fori_loop(0, channels // SUB, sub_step, 0)
        return carry

    lax.fori_loop(0, edges // CHUNK, chunk_step, 0)
    zw, pw = 3 * channels, 2 * channels
    first = zw * zw // 128
    second = first + pw * pw // 128
    own = ids_ref[1].astype(F32)
    for out_ref, wanted in ((other_ref, 1.0 - own), (own_ref, own)):
        mask = (edge_ref[1:2, :] == wanted).astype(F32).astype(BF16)
        qz = pulled_ref[0:zw, :] * mask
        qp = pulled_ref[zw : zw + pw, :] * mask
        qn = pulled_ref[zw + pw : zw + 2 * pw, :] * mask
        z, p, n = rotated[0:zw, :], rotated[zw : zw + pw, :], rotated[zw + pw : zw + 2 * pw, :]
        whole = nt(z, qz)
        for j in range(zw // 128):
            grads[pl.ds(j, zw, stride=zw // 128), :] = whole[:, j * 128 : (j + 1) * 128]
        coupled = nt(p, qp) + nt(n, qn)
        crossed = nt(p, qn) - nt(n, qp)
        for j in range(pw // 128):
            grads[pl.ds(first + j, pw, stride=pw // 128), :] = coupled[:, j * 128 : (j + 1) * 128]
            grads[pl.ds(second + j, pw, stride=pw // 128), :] = crossed[:, j * 128 : (j + 1) * 128]
        out_ref[...] = grads[...].astype(BF16)


def features(ids, live, near, classes, zero, one, two, source, target, rows, fanout):
    slots, channels = source.shape[1:]
    atoms = target.shape[1]
    edges = atoms * fanout
    shape = jax.ShapeDtypeStruct
    return pl.pallas_call(
        functools.partial(features_kernel, fanout=fanout),
        in_specs=[SMEM, SMEM] + [VMEM] * 7,
        out_specs=[VMEM] * 4,
        out_shape=[
            shape((rows, 128), BF16),
            shape((rows, 128), BF16),
            shape((7 * channels, edges), BF16),
            shape((8, edges), F32),
        ],
        scratch_shapes=[
            pltpu.VMEM((9 * channels, slots), BF16),
            pltpu.VMEM((9 * channels, atoms), BF16),
            pltpu.VMEM((9 * channels, CHUNK), F32),
            pltpu.VMEM((9 * channels, CHUNK), F32),
            pltpu.VMEM((7 * channels, edges), BF16),
            pltpu.VMEM((rows, 128), F32),
        ],
        compiler_params=PARAMS,
        name="features",
    )(ids, live, near, classes, zero, one, two, source, target)


def back_kernel(
    places_ref, edge_ref, zero_ref, one_ref, two_ref, pulled_ref, *rest, pieces, members, atoms, face,
):
    piece_refs = rest[:pieces]
    own_ref, ghost_ref, flat, weight_zero, weight_pair, field, turned, pick_all = rest[pieces:]
    rows = flat.shape[1]
    channels = own_ref.shape[2]
    slots = pick_all.shape[0]
    edges = pulled_ref.shape[1]
    zw, pw = 3 * channels, 2 * channels
    first = zw * zw // 128
    second = first + pw * pw // 128
    for index, piece in enumerate(piece_refs):
        height = piece.shape[1]
        at = pl.ds(pl.multiple_of(places_ref[index], 16), height)
        for k in range(members):
            flat[k, at, :] = piece[k].astype(F32)
    for k in range(members):
        for j in range(zw // 128):
            weight_zero[:, k * zw + j * 128 : k * zw + (j + 1) * 128] = flat[
                k, pl.ds(j, zw, stride=zw // 128), :
            ].astype(BF16)
        for j in range(pw // 128):
            at = k * 2 * pw + j * 128
            weight_pair[:, at : at + 128] = flat[k, pl.ds(first + j, pw, stride=pw // 128), :].astype(BF16)
            weight_pair[:, at + pw : at + pw + 128] = flat[
                k, pl.ds(second + j, pw, stride=pw // 128), :
            ].astype(BF16)

    def chunk_step(chunk, carry):
        start = pl.multiple_of(chunk * CHUNK, CHUNK)
        here = pl.ds(start, CHUNK)
        slot = lax.broadcasted_iota(jnp.int32, (slots, CHUNK), 0).astype(F32)
        pick_all[:, here] = (slot == edge_ref[0:1, here]).astype(F32).astype(BF16)
        qz, qpn, qnp = [], [], []
        for k in range(members):
            mask = (edge_ref[1:2, here] == float(k)).astype(F32).astype(BF16)
            qz.append(pulled_ref[0:zw, here] * mask)
            qp = pulled_ref[zw : zw + pw, here] * mask
            qn = pulled_ref[zw + pw : zw + 2 * pw, here] * mask
            qpn += [qp, qn]
            qnp += [qn, -qp]
        field[0:zw, :] = nn(weight_zero[...], jnp.concatenate(qz, axis=0))
        field[zw : zw + pw, :] = nn(weight_pair[...], jnp.concatenate(qpn, axis=0))
        field[zw + pw : zw + 2 * pw, :] = nn(weight_pair[...], jnp.concatenate(qnp, axis=0))

        def sub_step(sub, inner):
            at = pl.multiple_of(sub * SUB, SUB)

            def part(c):
                return field[pl.ds(SLOT[c] * channels + at, SUB), :]

            def write(c, value):
                turned[pl.ds(c * channels + at, SUB), here] = value.astype(BF16)

            write(0, zero_ref[0:1, here] * part(0))
            values = [part(c) for c in (1, 2, 3)]
            for b in range(3):
                total = one_ref[0, b : b + 1, here] * values[0]
                for a in range(1, 3):
                    total += one_ref[a, b : b + 1, here] * values[a]
                write(1 + b, total)
            values = [part(c) for c in (5, 6, 7)]
            for b in range(5):
                total = two_ref[1, b : b + 1, here] * values[0]
                for a in range(2, 4):
                    total += two_ref[a, b : b + 1, here] * values[a - 1]
                write(4 + b, total)
            return inner

        lax.fori_loop(0, channels // SUB, sub_step, 0)
        return carry

    lax.fori_loop(0, edges // CHUNK, chunk_step, 0)
    for c in range(9):
        summed = nt(pick_all[...], turned[c * channels : (c + 1) * channels, :])
        own_ref[c] = summed[:atoms]
        for block in range(4):
            at = atoms + block * face
            ghost_ref[block, c] = summed[at : at + face].astype(BF16)


def back(places, edge, zero, one, two, pulled, pieces, rows, atoms, slots, face):
    members = pieces[0].shape[0]
    edges = pulled.shape[1]
    channels = pulled.shape[0] // 7
    shape = jax.ShapeDtypeStruct
    return pl.pallas_call(
        functools.partial(back_kernel, pieces=len(pieces), members=members, atoms=atoms, face=face),
        in_specs=[SMEM] + [VMEM] * (5 + len(pieces)),
        out_specs=[VMEM] * 2,
        out_shape=[shape((9, atoms, channels), F32), shape((4, 9, face, channels), BF16)],
        scratch_shapes=[
            pltpu.VMEM((members, rows, 128), F32),
            pltpu.VMEM((3 * channels, members * 3 * channels), BF16),
            pltpu.VMEM((2 * channels, members * 4 * channels), BF16),
            pltpu.VMEM((7 * channels, CHUNK), F32),
            pltpu.VMEM((9 * channels, edges), BF16),
            pltpu.VMEM((slots, edges), BF16),
        ],
        compiler_params=PARAMS,
        name="back",
    )(places, edge, zero, one, two, pulled, *pieces)


def pair_kernel(places_ref, own_ref, came_ref, *out_refs):
    height = out_refs[0].shape[0]
    for index, out_ref in enumerate(out_refs):
        at = pl.ds(pl.multiple_of(places_ref[index], 16), height)
        out_ref[...] = (own_ref[at, :].astype(F32) + came_ref[at, :].astype(F32)).astype(BF16)


def pair_sum(places, own, came, count):
    height = own.shape[0] // count
    return pl.pallas_call(
        pair_kernel,
        in_specs=[SMEM, VMEM, VMEM],
        out_specs=[VMEM] * count,
        out_shape=[jax.ShapeDtypeStruct((height, 128), BF16)] * count,
        compiler_params=PARAMS,
        name="pair_sum",
    )(places, own, came)


def total_kernel(*refs):
    total = refs[0][...].astype(F32)
    for ref in refs[1:-1]:
        total += ref[...].astype(F32)
    refs[-1][...] = total.astype(BF16)


def total_sum(parts):
    return pl.pallas_call(
        total_kernel,
        in_specs=[VMEM] * len(parts),
        out_specs=VMEM,
        out_shape=jax.ShapeDtypeStruct(parts[0].shape, BF16),
        compiler_params=PARAMS,
        name="total_sum",
    )(*parts)


def expert_kernel(coef_ref, *refs):
    sums, out_ref, summed = refs[:-2], refs[-2], refs[-1]
    half = len(sums) // 2
    for side in range(2):
        total = sums[side * half][...].astype(F32)
        for ref in sums[side * half + 1 : (side + 1) * half]:
            total += ref[...].astype(F32)
        summed[side] = total
    owned = coef_ref.shape[0]
    first = jnp.broadcast_to(coef_ref[:, 0:1], (owned, 128))
    second = jnp.broadcast_to(coef_ref[:, 1:2], (owned, 128))
    for row in range(summed.shape[1]):
        out_ref[:, row * 128 : (row + 1) * 128] = (
            first * summed[0, row : row + 1, :] + second * summed[1, row : row + 1, :]
        )


def expert_product(coef, sums):
    rows = sums[0].shape[0]
    owned = coef.shape[0]
    return pl.pallas_call(
        expert_kernel,
        in_specs=[VMEM] * (1 + len(sums)),
        out_specs=VMEM,
        out_shape=jax.ShapeDtypeStruct((owned, rows * 128), F32),
        scratch_shapes=[pltpu.VMEM((2, rows, 128), F32)],
        compiler_params=PARAMS,
        name="expert_product",
    )(coef, *sums)


def finish_kernel(send_ref, own_ref, a_ref, b_ref, c_ref, d_ref, out_ref):
    atoms = own_ref.shape[1]
    face = send_ref.shape[1]
    row = lax.broadcasted_iota(jnp.int32, (atoms, face), 0)
    picks = [(row == send_ref[b : b + 1, :]).astype(F32).astype(BF16) for b in range(4)]
    for c in range(9):
        total = own_ref[c]
        for pick, ref in zip(picks, (a_ref, b_ref, c_ref, d_ref)):
            total += nn(pick, ref[c])
        out_ref[c] = total.astype(BF16)


def finish(send, own, returned):
    return pl.pallas_call(
        finish_kernel,
        in_specs=[VMEM] * 6,
        out_specs=VMEM,
        out_shape=jax.ShapeDtypeStruct(own.shape, BF16),
        compiler_params=PARAMS,
        name="finish",
    )(send, own, *returned)


def swap(value, axis, bit):
    return lax.ppermute(value, axis, [(i, i ^ bit) for i in range(lax.axis_size(axis))])


def shift(value, axis, step):
    count = lax.axis_size(axis)
    return lax.ppermute(value, axis, [(i, (i + step) % count) for i in range(count)])


def local(
    saved_input, cotangent, neighbours, rot_zero, rot_one, rot_two, send_index, atom_class, live_blocks,
    merge_coef, experts,
):
    atoms, fanout = neighbours.shape
    slots = saved_input.shape[0]
    channels = cotangent.shape[2]
    face = send_index.shape[1]
    count_yz, count_gx = lax.axis_size("yz"), lax.axis_size("gx")
    row, column = lax.axis_index("yz"), lax.axis_index("gx")
    core = column % 2
    height = experts.shape[1] // 128
    rows = height * count_yz
    direct = height % 32 == 0 and count_yz & (count_yz - 1) == 0 and count_gx == 4

    zero = rot_zero.reshape(1, -1)
    source = jnp.transpose(saved_input, (1, 0, 2))
    target = jnp.transpose(cotangent, (1, 0, 2))
    ids = jnp.stack([core, core]).astype(jnp.int32)

    if direct:
        half = height // 2
        mine = merge(merge_coef, experts, core.reshape(1).astype(jnp.int32), 2)
        held = [mine] + [swap(mine, "yz", k) for k in range(1, count_yz)]
        facing = [swap(piece, "gx", 1) for piece in held]
        pieces = held + facing
        starts = jnp.stack([(row ^ k) * height for k in range(count_yz)])
        places = jnp.concatenate([starts + core * half, starts + (1 - core) * half]).astype(jnp.int32)
    else:
        part = jnp.dot(merge_coef, experts.astype(F32), precision=lax.Precision.HIGHEST).astype(BF16)
        merged = lax.all_gather(part, "yz", axis=1, tiled=True)
        pieces = [merged.reshape(merged.shape[0], rows, 128)]
        places = jnp.zeros((1,), jnp.int32)

    other, own, pulled, edge = features(
        ids, live_blocks, neighbours.T, atom_class.reshape(1, -1), zero, rot_one, rot_two, source, target,
        rows, fanout,
    )
    per_owner = merge_coef.shape[1] // count_gx
    owned = lax.dynamic_slice_in_dim(merge_coef, column * per_owner, per_owner, 1)
    grad_scale = math.sqrt(fanout / (atoms * count_yz * count_gx))
    owned = owned.T * grad_scale
    owned = jnp.where(core == 0, owned, owned[:, ::-1])
    if direct:
        came = swap(other, "gx", 1)
        parts = pair_sum(starts.astype(jnp.int32), own, came, count_yz)
        gathered = [parts[0]] + [swap(parts[k], "yz", k) for k in range(1, count_yz)]
    grad_own, ghosts = back(
        places, edge, zero, rot_one, rot_two, pulled, pieces, rows, atoms, slots, face
    )
    if direct:
        summed = total_sum(gathered)
        across = swap(summed, "gx", 2)
        sums = [summed, across, swap(summed, "gx", 1), swap(across, "gx", 1)]
    else:
        mixed = jnp.stack([own, other]).astype(F32)
        mixed = jnp.where(core == 0, mixed, mixed[::-1])
        whole = lax.psum(mixed, ("yz", "gx"))
        piece = lax.dynamic_slice_in_dim(whole, row * height, height, 1)
        piece = jnp.where(core == 0, piece, piece[::-1])
        sums = [piece[0], piece[1]]
    returned = [
        shift(ghosts[1], "gx", 1), shift(ghosts[0], "gx", -1), shift(ghosts[3], "yz", 1), shift(ghosts[2], "yz", -1),
    ]
    expert_grad = expert_product(owned, sums)
    input_grad = finish(send_index, grad_own, returned)
    return (jnp.transpose(input_grad, (1, 0, 2)), expert_grad)


def solution(mesh):
    tiles = ("rep", "yz", "gx")
    in_specs = (
        P(tiles, None, None),
        P(tiles, None, None),
        P(tiles, None),
        P(tiles),
        P(None, None, tiles),
        P(None, None, tiles),
        P(tiles, None),
        P(tiles),
        P(tiles),
        P(),
        P(None, "yz"),
    )
    out_specs = (P(tiles, None, None), P(("rep", "gx"), "yz"))
    return jax.shard_map(local, mesh=mesh, in_specs=in_specs, out_specs=out_specs, check_vma=False)
```

```python
import functools
import math

import jax
import jax.numpy as jnp
from jax import lax
from jax.experimental import pallas as pl
from jax.experimental.pallas import tpu as pltpu
from jax.sharding import PartitionSpec as P

LIVE_BLOCK = 64
CHUNK = 256
SUB = 16
F32 = jnp.float32
BF16 = jnp.bfloat16

STACK = (0, 2, 6, 3, 7, 1, 5)
SLOT = {component: place for place, component in enumerate(STACK)}

VMEM = pl.BlockSpec(memory_space=pltpu.VMEM)
SMEM = pl.BlockSpec(memory_space=pltpu.SMEM)
HBM = pl.BlockSpec(memory_space=pltpu.HBM)


def limits(mebibytes):
    return pltpu.CompilerParams(vmem_limit_bytes=mebibytes * 1024 * 1024)


def cost(flops, moved):
    return pl.CostEstimate(flops=flops, bytes_accessed=moved, transcendentals=0)


def nn(left, right):
    return lax.dot_general(left, right, (((1,), (0,)), ((), ())), preferred_element_type=F32)


def nt(left, right):
    return lax.dot_general(left, right, (((1,), (1,)), ((), ())), preferred_element_type=F32)


def split3(value):
    high = value.astype(BF16)
    rest = value - high.astype(F32)
    middle = rest.astype(BF16)
    low = (rest - middle.astype(F32)).astype(BF16)
    return high, middle, low


def merge_kernel(coef_ref, experts_ref, out_ref, held, arrived):
    members, experts = coef_ref.shape
    rows = out_ref.shape[1]
    start = pl.multiple_of(lax.rem(lax.axis_index("gx"), 2) * rows * 128, 128)
    stripes = arrived.shape[0]
    blocks = rows // 16
    edges = [blocks * stripe // stripes for stripe in range(stripes + 1)]
    copies = []
    for stripe in range(stripes):
        at, wide = edges[stripe] * 2048, (edges[stripe + 1] - edges[stripe]) * 2048
        copies.append(
            pltpu.make_async_copy(
                experts_ref.at[:, pl.ds(start + at, wide)], held.at[:, pl.ds(at, wide)], arrived.at[stripe]
            )
        )
        copies[-1].start()
    wide = 8 * experts
    row = lax.broadcasted_iota(jnp.int32, (8, wide), 0)
    col = lax.broadcasted_iota(jnp.int32, (8, wide), 1)
    diagonal = row == col // experts
    source = lax.broadcasted_iota(jnp.int32, (experts, wide), 0)
    target = lax.broadcasted_iota(jnp.int32, (experts, wide), 1)
    tile = (source == target % experts).astype(F32).astype(BF16)
    lefts = []
    for term in split3(coef_ref[...]):
        tiled = nn(term, tile)
        for member in range(members):
            lefts.append(jnp.where(diagonal, tiled[member : member + 1, :], 0.0).astype(BF16))
    lefts = jnp.concatenate(lefts, axis=0)
    height = 8 * members
    for block in range(blocks):
        if block in edges:
            copies[edges.index(block)].wait()
        halves = []
        for half in range(2):
            first = block * 16 + half * 8
            groups = [held[:, (first + g) * 128 : (first + g + 1) * 128] for g in range(8)]
            halves.append(jnp.concatenate(groups, axis=0))
        product = nn(lefts, jnp.concatenate(halves, axis=1))
        total = product[:height] + product[height : 2 * height] + product[2 * height :]
        for member in range(members):
            part = total[member * 8 : member * 8 + 8]
            out_ref[member, block * 16 : block * 16 + 16, :] = jnp.concatenate(
                [part[:, :128], part[:, 128:]], axis=0
            ).astype(BF16)


def merge(coef, experts, parts):
    members, count = coef.shape
    columns = experts.shape[1] // parts
    rows = columns // 128
    return pl.pallas_call(
        merge_kernel,
        in_specs=[VMEM, HBM],
        out_specs=VMEM,
        out_shape=jax.ShapeDtypeStruct((members, rows, 128), BF16),
        scratch_shapes=[pltpu.VMEM((count, columns), BF16), pltpu.SemaphoreType.DMA((4,))],
        compiler_params=limits(60),
        cost_estimate=cost(96 * 16 * columns, 2 * count * columns),
        name="merge",
    )(coef, experts)


def features_kernel(
    live_ref, near_ref, class_ref, zero_ref, one_ref, two_ref, source_ref, target_ref,
    other_ref, own_ref, pulled_ref, edge_ref,
    source_t, target_t, moved, spread, rotated, grads,
    *, fanout,
):
    slots, channels = source_ref.shape[1:]
    atoms = target_ref.shape[1]
    edges = atoms * fanout
    for c in range(9):
        source_t[c * channels : (c + 1) * channels, :] = source_ref[c].T
        target_t[c * channels : (c + 1) * channels, :] = target_ref[c].T
    near = near_ref[...].astype(F32).astype(BF16)
    classes = class_ref[...].astype(F32).astype(BF16)
    live_edges = live_ref[0] * LIVE_BLOCK * fanout
    scale = 1.0 / math.sqrt(fanout)

    def chunk_step(chunk, carry):
        start = pl.multiple_of(chunk * CHUNK, CHUNK)
        here = pl.ds(start, CHUNK)
        edge = lax.broadcasted_iota(jnp.int32, (atoms, CHUNK), 1) + start
        atom = lax.broadcasted_iota(jnp.int32, (atoms, CHUNK), 0)
        repeat = (edge // fanout == atom).astype(F32).astype(BF16)
        edge8 = lax.broadcasted_iota(jnp.int32, (fanout, CHUNK), 1) + start
        lane8 = lax.broadcasted_iota(jnp.int32, (fanout, CHUNK), 0)
        picked = jnp.where(edge8 % fanout == lane8, nn(near, repeat), 0.0)
        near_row = jnp.sum(picked, axis=0, keepdims=True)
        class_row = nn(classes, repeat)
        edge_ref[0:1, here] = near_row
        edge_ref[1:2, here] = jnp.where(edge8[0:1] < live_edges, class_row, -1.0)
        slot = lax.broadcasted_iota(jnp.int32, (slots, CHUNK), 0).astype(F32)
        pick = (slot == near_row).astype(F32).astype(BF16)
        moved[...] = nn(source_t[...], pick)
        spread[...] = nn(target_t[...], repeat)

        def sub_step(sub, inner):
            at = pl.multiple_of(sub * SUB, SUB)

            def turn(field, write):
                def part(c):
                    return field[pl.ds(c * channels + at, SUB), :]

                write(0, zero_ref[0:1, here] * part(0))
                values = [part(c) for c in (1, 2, 3)]
                for a in range(3):
                    total = one_ref[a, 0:1, here] * values[0]
                    for b in range(1, 3):
                        total += one_ref[a, b : b + 1, here] * values[b]
                    write(1 + a, total)
                values = [part(c) for c in (4, 5, 6, 7, 8)]
                for a in range(1, 4):
                    total = two_ref[a, 0:1, here] * values[0]
                    for b in range(1, 5):
                        total += two_ref[a, b : b + 1, here] * values[b]
                    write(4 + a, total)

            def write_rotated(c, value):
                rotated[pl.ds(SLOT[c] * channels + at, SUB), here] = value.astype(BF16)

            def write_pulled(c, value):
                pulled_ref[pl.ds(SLOT[c] * channels + at, SUB), here] = (value * scale).astype(BF16)

            turn(moved, write_rotated)
            turn(spread, write_pulled)
            return inner

        lax.fori_loop(0, channels // SUB, sub_step, 0)
        return carry

    lax.fori_loop(0, edges // CHUNK, chunk_step, 0)
    zw, pw = 3 * channels, 2 * channels
    first = zw * zw // 128
    second = first + pw * pw // 128
    own = lax.rem(lax.axis_index("gx"), 2).astype(F32)
    for out_ref, wanted in ((other_ref, 1.0 - own), (own_ref, own)):
        mask = (edge_ref[1:2, :] == wanted).astype(F32).astype(BF16)
        qz = pulled_ref[0:zw, :] * mask
        qp = pulled_ref[zw : zw + pw, :] * mask
        qn = pulled_ref[zw + pw : zw + 2 * pw, :] * mask
        z, p, n = rotated[0:zw, :], rotated[zw : zw + pw, :], rotated[zw + pw : zw + 2 * pw, :]
        whole = nt(z, qz)
        for j in range(zw // 128):
            grads[pl.ds(j, zw, stride=zw // 128), :] = whole[:, j * 128 : (j + 1) * 128]
        coupled = nt(p, qp) + nt(n, qn)
        crossed = nt(p, qn) - nt(n, qp)
        for j in range(pw // 128):
            grads[pl.ds(first + j, pw, stride=pw // 128), :] = coupled[:, j * 128 : (j + 1) * 128]
            grads[pl.ds(second + j, pw, stride=pw // 128), :] = crossed[:, j * 128 : (j + 1) * 128]
        out_ref[...] = grads[...].astype(BF16)


def features(live, near, classes, zero, one, two, source, target, rows, fanout):
    slots, channels = source.shape[1:]
    atoms = target.shape[1]
    edges = atoms * fanout
    shape = jax.ShapeDtypeStruct
    return pl.pallas_call(
        functools.partial(features_kernel, fanout=fanout),
        in_specs=[SMEM] + [VMEM] * 7,
        out_specs=[VMEM] * 4,
        out_shape=[
            shape((rows, 128), BF16),
            shape((rows, 128), BF16),
            shape((7 * channels, edges), BF16),
            shape((8, edges), F32),
        ],
        scratch_shapes=[
            pltpu.VMEM((9 * channels, slots), BF16),
            pltpu.VMEM((9 * channels, atoms), BF16),
            pltpu.VMEM((9 * channels, CHUNK), F32),
            pltpu.VMEM((9 * channels, CHUNK), F32),
            pltpu.VMEM((7 * channels, edges), BF16),
            pltpu.VMEM((rows, 128), F32),
        ],
        compiler_params=limits(24),
        cost_estimate=cost(9 * 10**9, 7 * 10**6),
        name="features",
    )(live, near, classes, zero, one, two, source, target)


def back_kernel(
    edge_ref, zero_ref, one_ref, two_ref, pulled_ref, *rest, pieces, members, atoms, face, places,
):
    piece_refs = rest[:pieces]
    own_ref, *ghost_refs = rest[pieces : pieces + 5]
    flat, weight_zero, weight_pair, field, turned, pick_all = rest[pieces + 5 :]
    rows = flat.shape[1]
    channels = own_ref.shape[2]
    slots = pick_all.shape[0]
    edges = pulled_ref.shape[1]
    zw, pw = 3 * channels, 2 * channels
    first = zw * zw // 128
    second = first + pw * pw // 128
    for piece, place in zip(piece_refs, places()):
        height = piece.shape[1]
        at = pl.ds(pl.multiple_of(place, 16), height)
        for k in range(members):
            flat[k, at, :] = piece[k].astype(F32)
    for k in range(members):
        for j in range(zw // 128):
            weight_zero[:, k * zw + j * 128 : k * zw + (j + 1) * 128] = flat[
                k, pl.ds(j, zw, stride=zw // 128), :
            ].astype(BF16)
        for j in range(pw // 128):
            at = k * 2 * pw + j * 128
            weight_pair[:, at : at + 128] = flat[k, pl.ds(first + j, pw, stride=pw // 128), :].astype(BF16)
            weight_pair[:, at + pw : at + pw + 128] = flat[
                k, pl.ds(second + j, pw, stride=pw // 128), :
            ].astype(BF16)

    def chunk_step(chunk, carry):
        start = pl.multiple_of(chunk * CHUNK, CHUNK)
        here = pl.ds(start, CHUNK)
        slot = lax.broadcasted_iota(jnp.int32, (slots, CHUNK), 0).astype(F32)
        pick_all[:, here] = (slot == edge_ref[0:1, here]).astype(F32).astype(BF16)
        qz, qpn, qnp = [], [], []
        for k in range(members):
            mask = (edge_ref[1:2, here] == float(k)).astype(F32).astype(BF16)
            qz.append(pulled_ref[0:zw, here] * mask)
            qp = pulled_ref[zw : zw + pw, here] * mask
            qn = pulled_ref[zw + pw : zw + 2 * pw, here] * mask
            qpn += [qp, qn]
            qnp += [qn, -qp]
        field[0:zw, :] = nn(weight_zero[...], jnp.concatenate(qz, axis=0))
        field[zw : zw + pw, :] = nn(weight_pair[...], jnp.concatenate(qpn, axis=0))
        field[zw + pw : zw + 2 * pw, :] = nn(weight_pair[...], jnp.concatenate(qnp, axis=0))

        def sub_step(sub, inner):
            at = pl.multiple_of(sub * SUB, SUB)

            def part(c):
                return field[pl.ds(SLOT[c] * channels + at, SUB), :]

            def write(c, value):
                turned[pl.ds(c * channels + at, SUB), here] = value.astype(BF16)

            write(0, zero_ref[0:1, here] * part(0))
            values = [part(c) for c in (1, 2, 3)]
            for b in range(3):
                total = one_ref[0, b : b + 1, here] * values[0]
                for a in range(1, 3):
                    total += one_ref[a, b : b + 1, here] * values[a]
                write(1 + b, total)
            values = [part(c) for c in (5, 6, 7)]
            for b in range(5):
                total = two_ref[1, b : b + 1, here] * values[0]
                for a in range(2, 4):
                    total += two_ref[a, b : b + 1, here] * values[a - 1]
                write(4 + b, total)
            return inner

        lax.fori_loop(0, channels // SUB, sub_step, 0)
        return carry

    lax.fori_loop(0, edges // CHUNK, chunk_step, 0)
    for c in range(9):
        summed = nt(pick_all[...], turned[c * channels : (c + 1) * channels, :])
        own_ref[c] = summed[:atoms]
        for block in range(4):
            at = atoms + block * face
            ghost_refs[block][c] = summed[at : at + face].astype(BF16)


def back(edge, zero, one, two, pulled, pieces, places, rows, atoms, slots, face):
    members = pieces[0].shape[0]
    edges = pulled.shape[1]
    channels = pulled.shape[0] // 7
    shape = jax.ShapeDtypeStruct
    return pl.pallas_call(
        functools.partial(
            back_kernel, pieces=len(pieces), members=members, atoms=atoms, face=face, places=places
        ),
        in_specs=[VMEM] * (5 + len(pieces)),
        out_specs=[VMEM] * 5,
        out_shape=[shape((9, atoms, channels), F32), *[shape((9, face, channels), BF16)] * 4],
        scratch_shapes=[
            pltpu.VMEM((members, rows, 128), F32),
            pltpu.VMEM((3 * channels, members * 3 * channels), BF16),
            pltpu.VMEM((2 * channels, members * 4 * channels), BF16),
            pltpu.VMEM((7 * channels, CHUNK), F32),
            pltpu.VMEM((9 * channels, edges), BF16),
            pltpu.VMEM((slots, edges), BF16),
        ],
        compiler_params=limits(24),
        cost_estimate=cost(9 * 10**9, 7 * 10**6),
        name="back",
    )(edge, zero, one, two, pulled, *pieces)


def pair_kernel(own_ref, came_ref, *out_refs):
    height = out_refs[0].shape[0]
    row = lax.axis_index("yz")
    for index, out_ref in enumerate(out_refs):
        at = pl.ds(pl.multiple_of((row ^ index) * height, 16), height)
        out_ref[...] = (own_ref[at, :].astype(F32) + came_ref[at, :].astype(F32)).astype(BF16)


def pair_sum(own, came, count):
    height = own.shape[0] // count
    return pl.pallas_call(
        pair_kernel,
        in_specs=[VMEM, VMEM],
        out_specs=[VMEM] * count,
        out_shape=[jax.ShapeDtypeStruct((height, 128), BF16)] * count,
        compiler_params=limits(6),
        cost_estimate=cost(10**6, 2 * 10**6),
        name="pair_sum",
    )(own, came)


def total_kernel(*refs):
    total = refs[0][...].astype(F32)
    for ref in refs[1:-1]:
        total += ref[...].astype(F32)
    refs[-1][...] = total.astype(BF16)


def total_sum(parts):
    return pl.pallas_call(
        total_kernel,
        in_specs=[VMEM] * len(parts),
        out_specs=VMEM,
        out_shape=jax.ShapeDtypeStruct(parts[0].shape, BF16),
        compiler_params=limits(6),
        cost_estimate=cost(10**6, 10**6),
        name="total_sum",
    )(*parts)


def expert_kernel(coef_ref, *refs, scale):
    sums, out_ref, summed = refs[:-2], refs[-2], refs[-1]
    owned = out_ref.shape[0]
    place = lax.axis_index("gx")
    row = lax.broadcasted_iota(jnp.int32, (owned, coef_ref.shape[1]), 0)
    col = lax.broadcasted_iota(jnp.int32, (owned, coef_ref.shape[1]), 1)
    chosen = col == row + place * owned
    picked = [
        jnp.sum(jnp.where(chosen, coef_ref[k : k + 1, :], 0.0), axis=1, keepdims=True) * scale for k in range(2)
    ]
    even = lax.rem(place, 2) == 0
    first = jnp.broadcast_to(jnp.where(even, picked[0], picked[1]), (owned, 128))
    second = jnp.broadcast_to(jnp.where(even, picked[1], picked[0]), (owned, 128))
    half = len(sums) // 2
    for side in range(2):
        total = sums[side * half][...].astype(F32)
        for ref in sums[side * half + 1 : (side + 1) * half]:
            total += ref[...].astype(F32)
        summed[side] = total
    for row in range(summed.shape[1]):
        out_ref[:, row * 128 : (row + 1) * 128] = (
            first * summed[0, row : row + 1, :] + second * summed[1, row : row + 1, :]
        )


def expert_product(coef, sums, owned, scale):
    rows = sums[0].shape[0]
    return pl.pallas_call(
        functools.partial(expert_kernel, scale=scale),
        in_specs=[VMEM] * (1 + len(sums)),
        out_specs=VMEM,
        out_shape=jax.ShapeDtypeStruct((owned, rows * 128), F32),
        scratch_shapes=[pltpu.VMEM((2, rows, 128), F32)],
        compiler_params=limits(8),
        cost_estimate=cost(10**6, 4 * 10**6),
        name="expert_product",
    )(coef, *sums)


def finish_kernel(send_ref, own_ref, a_ref, b_ref, c_ref, d_ref, out_ref):
    atoms = own_ref.shape[1]
    face = send_ref.shape[1]
    row = lax.broadcasted_iota(jnp.int32, (atoms, face), 0)
    picks = [(row == send_ref[b : b + 1, :]).astype(F32).astype(BF16) for b in range(4)]
    for c in range(9):
        total = own_ref[c]
        for pick, ref in zip(picks, (a_ref, b_ref, c_ref, d_ref)):
            total += nn(pick, ref[c])
        out_ref[c] = total.astype(BF16)


def finish(send, own, returned):
    return pl.pallas_call(
        finish_kernel,
        in_specs=[VMEM] * 6,
        out_specs=VMEM,
        out_shape=jax.ShapeDtypeStruct(own.shape, BF16),
        compiler_params=limits(6),
        cost_estimate=cost(10**8, 2 * 10**6),
        name="finish",
    )(send, own, *returned)


def swap(value, axis, bit):
    return lax.ppermute(value, axis, [(i, i ^ bit) for i in range(lax.axis_size(axis))])


def shift(value, axis, step):
    count = lax.axis_size(axis)
    return lax.ppermute(value, axis, [(i, (i + step) % count) for i in range(count)])


def local(
    saved_input, cotangent, neighbours, rot_zero, rot_one, rot_two, send_index, atom_class, live_blocks,
    merge_coef, experts,
):
    atoms, fanout = neighbours.shape
    slots = saved_input.shape[0]
    channels = cotangent.shape[2]
    face = send_index.shape[1]
    count_yz, count_gx = lax.axis_size("yz"), lax.axis_size("gx")
    row, column = lax.axis_index("yz"), lax.axis_index("gx")
    core = column % 2
    height = experts.shape[1] // 128
    rows = height * count_yz
    direct = height % 32 == 0 and count_yz & (count_yz - 1) == 0 and count_gx == 4

    zero = rot_zero.reshape(1, -1)
    source = jnp.transpose(saved_input, (1, 0, 2))
    target = jnp.transpose(cotangent, (1, 0, 2))

    if direct:
        half = height // 2
        mine = merge(merge_coef, experts, 2)
        held = [mine] + [swap(mine, "yz", k) for k in range(1, count_yz)]
        source, target, mine = lax.optimization_barrier((source, target, mine))

        def places():
            here, side = lax.axis_index("yz"), lax.rem(lax.axis_index("gx"), 2)
            starts = [(here ^ k) * height for k in range(count_yz)]
            return [at + side * half for at in starts] + [at + (1 - side) * half for at in starts]
    else:
        part = jnp.dot(merge_coef, experts.astype(F32), precision=lax.Precision.HIGHEST).astype(BF16)
        merged = lax.all_gather(part, "yz", axis=1, tiled=True)
        pieces = [merged.reshape(merged.shape[0], rows, 128)]

        def places():
            return [0]

    other, own, pulled, edge = features(
        live_blocks, neighbours.T, atom_class.reshape(1, -1), zero, rot_one, rot_two, source, target, rows, fanout
    )
    if direct:
        other, *held = lax.optimization_barrier((other, *held))
        came = swap(other, "gx", 1)
        parts = pair_sum(own, came, count_yz)
        gathered = [parts[0]] + [swap(parts[k], "yz", k) for k in range(1, count_yz)]
        pieces = held + [swap(piece, "gx", 1) for piece in held]
    grad_own, *ghosts = back(edge, zero, rot_one, rot_two, pulled, pieces, places, rows, atoms, slots, face)
    if direct:
        grad_own, *gathered = lax.optimization_barrier((grad_own, *gathered))
        summed = total_sum(gathered)
        across = swap(summed, "gx", 2)
        sums = [summed, across, swap(summed, "gx", 1), swap(across, "gx", 1)]
    else:
        mixed = jnp.stack([own, other]).astype(F32)
        mixed = jnp.where(core == 0, mixed, mixed[::-1])
        whole = lax.psum(mixed, ("yz", "gx"))
        piece = lax.dynamic_slice_in_dim(whole, row * height, height, 1)
        piece = jnp.where(core == 0, piece, piece[::-1])
        sums = [piece[0], piece[1]]
    returned = [
        shift(ghosts[1], "gx", 1), shift(ghosts[0], "gx", -1), shift(ghosts[3], "yz", 1), shift(ghosts[2], "yz", -1),
    ]
    grad_scale = math.sqrt(fanout / (atoms * count_yz * count_gx))
    expert_grad = expert_product(merge_coef, sums, merge_coef.shape[1] // count_gx, grad_scale)
    input_grad = finish(send_index, grad_own, returned)
    return (jnp.transpose(input_grad, (1, 0, 2)), expert_grad)


def solution(mesh):
    tiles = ("rep", "yz", "gx")
    in_specs = (
        P(tiles, None, None),
        P(tiles, None, None),
        P(tiles, None),
        P(tiles),
        P(None, None, tiles),
        P(None, None, tiles),
        P(tiles, None),
        P(tiles),
        P(tiles),
        P(),
        P(None, "yz"),
    )
    out_specs = (P(tiles, None, None), P(("rep", "gx"), "yz"))
    return jax.shard_map(local, mesh=mesh, in_specs=in_specs, out_specs=out_specs, check_vma=False)
```

```python
import functools
import math

import jax
import jax.numpy as jnp
from jax import lax
from jax.experimental import pallas as pl
from jax.experimental.pallas import tpu as pltpu
from jax.sharding import PartitionSpec as P

LIVE_BLOCK = 64
CHUNK = 256
SUB = 16
F32 = jnp.float32
BF16 = jnp.bfloat16

STACK = (0, 2, 6, 3, 7, 1, 5)
SLOT = {component: place for place, component in enumerate(STACK)}

VMEM = pl.BlockSpec(memory_space=pltpu.VMEM)
SMEM = pl.BlockSpec(memory_space=pltpu.SMEM)
HBM = pl.BlockSpec(memory_space=pltpu.HBM)


def limits(mebibytes):
    return pltpu.CompilerParams(vmem_limit_bytes=mebibytes * 1024 * 1024)


def cost(flops, moved):
    return pl.CostEstimate(flops=flops, bytes_accessed=moved, transcendentals=0)


def nn(left, right):
    return lax.dot_general(left, right, (((1,), (0,)), ((), ())), preferred_element_type=F32)


def nt(left, right):
    return lax.dot_general(left, right, (((1,), (1,)), ((), ())), preferred_element_type=F32)


def split3(value):
    high = value.astype(BF16)
    rest = value - high.astype(F32)
    middle = rest.astype(BF16)
    low = (rest - middle.astype(F32)).astype(BF16)
    return high, middle, low


def merge_kernel(coef_ref, experts_ref, out_ref, held, arrived):
    members, experts = coef_ref.shape
    rows = out_ref.shape[1]
    start = pl.multiple_of(lax.rem(lax.axis_index("gx"), 2) * rows * 128, 128)
    stripes = arrived.shape[0]
    blocks = rows // 16
    edges = [blocks * stripe // stripes for stripe in range(stripes + 1)]
    copies = []
    for stripe in range(stripes):
        at, wide = edges[stripe] * 2048, (edges[stripe + 1] - edges[stripe]) * 2048
        copies.append(
            pltpu.make_async_copy(
                experts_ref.at[:, pl.ds(start + at, wide)], held.at[:, pl.ds(at, wide)], arrived.at[stripe]
            )
        )
        copies[-1].start()
    wide = 8 * experts
    row = lax.broadcasted_iota(jnp.int32, (8, wide), 0)
    col = lax.broadcasted_iota(jnp.int32, (8, wide), 1)
    diagonal = row == col // experts
    source = lax.broadcasted_iota(jnp.int32, (experts, wide), 0)
    target = lax.broadcasted_iota(jnp.int32, (experts, wide), 1)
    tile = (source == target % experts).astype(F32).astype(BF16)
    lefts = []
    for term in split3(coef_ref[...]):
        tiled = nn(term, tile)
        for member in range(members):
            lefts.append(jnp.where(diagonal, tiled[member : member + 1, :], 0.0).astype(BF16))
    lefts = jnp.concatenate(lefts, axis=0)
    height = 8 * members
    for block in range(blocks):
        if block in edges:
            copies[edges.index(block)].wait()
        halves = []
        for half in range(2):
            first = block * 16 + half * 8
            groups = [held[:, (first + g) * 128 : (first + g + 1) * 128] for g in range(8)]
            halves.append(jnp.concatenate(groups, axis=0))
        product = nn(lefts, jnp.concatenate(halves, axis=1))
        total = product[:height] + product[height : 2 * height] + product[2 * height :]
        for member in range(members):
            part = total[member * 8 : member * 8 + 8]
            out_ref[member, block * 16 : block * 16 + 16, :] = jnp.concatenate(
                [part[:, :128], part[:, 128:]], axis=0
            ).astype(BF16)


def merge(coef, experts, parts):
    members, count = coef.shape
    columns = experts.shape[1] // parts
    rows = columns // 128
    return pl.pallas_call(
        merge_kernel,
        in_specs=[VMEM, HBM],
        out_specs=VMEM,
        out_shape=jax.ShapeDtypeStruct((members, rows, 128), BF16),
        scratch_shapes=[pltpu.VMEM((count, columns), BF16), pltpu.SemaphoreType.DMA((4,))],
        compiler_params=limits(60),
        cost_estimate=cost(96 * 16 * columns, 2 * count * columns),
        name="merge",
    )(coef, experts)


def features_kernel(
    live_ref, near_ref, class_ref, zero_ref, one_ref, two_ref, source_ref, target_ref,
    other_ref, own_ref, pulled_ref, edge_ref,
    source_t, target_t, moved, spread, rotated, grads,
    *, fanout,
):
    slots, channels = source_ref.shape[1:]
    atoms = target_ref.shape[1]
    edges = atoms * fanout
    for c in range(9):
        source_t[c * channels : (c + 1) * channels, :] = source_ref[c].T
        target_t[c * channels : (c + 1) * channels, :] = target_ref[c].T
    near = near_ref[...].astype(F32).astype(BF16)
    classes = class_ref[...].astype(F32).astype(BF16)
    live_edges = live_ref[0] * LIVE_BLOCK * fanout
    scale = 1.0 / math.sqrt(fanout)

    def chunk_step(chunk, carry):
        start = pl.multiple_of(chunk * CHUNK, CHUNK)
        here = pl.ds(start, CHUNK)
        edge = lax.broadcasted_iota(jnp.int32, (atoms, CHUNK), 1) + start
        atom = lax.broadcasted_iota(jnp.int32, (atoms, CHUNK), 0)
        repeat = (edge // fanout == atom).astype(F32).astype(BF16)
        edge8 = lax.broadcasted_iota(jnp.int32, (fanout, CHUNK), 1) + start
        lane8 = lax.broadcasted_iota(jnp.int32, (fanout, CHUNK), 0)
        picked = jnp.where(edge8 % fanout == lane8, nn(near, repeat), 0.0)
        near_row = jnp.sum(picked, axis=0, keepdims=True)
        class_row = nn(classes, repeat)
        edge_ref[0:1, here] = near_row
        edge_ref[1:2, here] = jnp.where(edge8[0:1] < live_edges, class_row, -1.0)
        slot = lax.broadcasted_iota(jnp.int32, (slots, CHUNK), 0).astype(F32)
        pick = (slot == near_row).astype(F32).astype(BF16)
        moved[...] = nn(source_t[...], pick)
        spread[...] = nn(target_t[...], repeat)

        def sub_step(sub, inner):
            at = pl.multiple_of(sub * SUB, SUB)

            def turn(field, write):
                def part(c):
                    return field[pl.ds(c * channels + at, SUB), :]

                write(0, zero_ref[0:1, here] * part(0))
                values = [part(c) for c in (1, 2, 3)]
                for a in range(3):
                    total = one_ref[a, 0:1, here] * values[0]
                    for b in range(1, 3):
                        total += one_ref[a, b : b + 1, here] * values[b]
                    write(1 + a, total)
                values = [part(c) for c in (4, 5, 6, 7, 8)]
                for a in range(1, 4):
                    total = two_ref[a, 0:1, here] * values[0]
                    for b in range(1, 5):
                        total += two_ref[a, b : b + 1, here] * values[b]
                    write(4 + a, total)

            def write_rotated(c, value):
                rotated[pl.ds(SLOT[c] * channels + at, SUB), here] = value.astype(BF16)

            def write_pulled(c, value):
                pulled_ref[pl.ds(SLOT[c] * channels + at, SUB), here] = (value * scale).astype(BF16)

            turn(moved, write_rotated)
            turn(spread, write_pulled)
            return inner

        lax.fori_loop(0, channels // SUB, sub_step, 0)
        return carry

    lax.fori_loop(0, edges // CHUNK, chunk_step, 0)
    zw, pw = 3 * channels, 2 * channels
    first = zw * zw // 128
    second = first + pw * pw // 128
    own = lax.rem(lax.axis_index("gx"), 2).astype(F32)
    for out_ref, wanted in ((other_ref, 1.0 - own), (own_ref, own)):
        mask = (edge_ref[1:2, :] == wanted).astype(F32).astype(BF16)
        qz = pulled_ref[0:zw, :] * mask
        qp = pulled_ref[zw : zw + pw, :] * mask
        qn = pulled_ref[zw + pw : zw + 2 * pw, :] * mask
        z, p, n = rotated[0:zw, :], rotated[zw : zw + pw, :], rotated[zw + pw : zw + 2 * pw, :]
        whole = nt(z, qz)
        for j in range(zw // 128):
            grads[pl.ds(j, zw, stride=zw // 128), :] = whole[:, j * 128 : (j + 1) * 128]
        coupled = nt(p, qp) + nt(n, qn)
        crossed = nt(p, qn) - nt(n, qp)
        for j in range(pw // 128):
            grads[pl.ds(first + j, pw, stride=pw // 128), :] = coupled[:, j * 128 : (j + 1) * 128]
            grads[pl.ds(second + j, pw, stride=pw // 128), :] = crossed[:, j * 128 : (j + 1) * 128]
        out_ref[...] = grads[...].astype(BF16)


def features(live, near, classes, zero, one, two, source, target, rows, fanout):
    slots, channels = source.shape[1:]
    atoms = target.shape[1]
    edges = atoms * fanout
    shape = jax.ShapeDtypeStruct
    return pl.pallas_call(
        functools.partial(features_kernel, fanout=fanout),
        in_specs=[SMEM] + [VMEM] * 7,
        out_specs=[VMEM] * 4,
        out_shape=[
            shape((rows, 128), BF16),
            shape((rows, 128), BF16),
            shape((7 * channels, edges), BF16),
            shape((8, edges), F32),
        ],
        scratch_shapes=[
            pltpu.VMEM((9 * channels, slots), BF16),
            pltpu.VMEM((9 * channels, atoms), BF16),
            pltpu.VMEM((9 * channels, CHUNK), F32),
            pltpu.VMEM((9 * channels, CHUNK), F32),
            pltpu.VMEM((7 * channels, edges), BF16),
            pltpu.VMEM((rows, 128), F32),
        ],
        compiler_params=limits(24),
        cost_estimate=cost(9 * 10**9, 7 * 10**6),
        name="features",
    )(live, near, classes, zero, one, two, source, target)


def back_kernel(
    edge_ref, zero_ref, one_ref, two_ref, pulled_ref, *rest, pieces, members, atoms, face, places,
):
    piece_refs = rest[:pieces]
    own_ref, *ghost_refs = rest[pieces : pieces + 5]
    flat, weight_zero, weight_pair, field, turned, pick_all = rest[pieces + 5 :]
    rows = flat.shape[1]
    channels = own_ref.shape[2]
    slots = pick_all.shape[0]
    edges = pulled_ref.shape[1]
    zw, pw = 3 * channels, 2 * channels
    first = zw * zw // 128
    second = first + pw * pw // 128
    for piece, place in zip(piece_refs, places()):
        height = piece.shape[1]
        at = pl.ds(pl.multiple_of(place, 16), height)
        for k in range(members):
            flat[k, at, :] = piece[k].astype(F32)
    for k in range(members):
        for j in range(zw // 128):
            weight_zero[:, k * zw + j * 128 : k * zw + (j + 1) * 128] = flat[
                k, pl.ds(j, zw, stride=zw // 128), :
            ].astype(BF16)
        for j in range(pw // 128):
            at = k * 2 * pw + j * 128
            weight_pair[:, at : at + 128] = flat[k, pl.ds(first + j, pw, stride=pw // 128), :].astype(BF16)
            weight_pair[:, at + pw : at + pw + 128] = flat[
                k, pl.ds(second + j, pw, stride=pw // 128), :
            ].astype(BF16)

    def chunk_step(chunk, carry):
        start = pl.multiple_of(chunk * CHUNK, CHUNK)
        here = pl.ds(start, CHUNK)
        slot = lax.broadcasted_iota(jnp.int32, (slots, CHUNK), 0).astype(F32)
        pick_all[:, here] = (slot == edge_ref[0:1, here]).astype(F32).astype(BF16)
        qz, qpn, qnp = [], [], []
        for k in range(members):
            mask = (edge_ref[1:2, here] == float(k)).astype(F32).astype(BF16)
            qz.append(pulled_ref[0:zw, here] * mask)
            qp = pulled_ref[zw : zw + pw, here] * mask
            qn = pulled_ref[zw + pw : zw + 2 * pw, here] * mask
            qpn += [qp, qn]
            qnp += [qn, -qp]
        field[0:zw, :] = nn(weight_zero[...], jnp.concatenate(qz, axis=0))
        field[zw : zw + pw, :] = nn(weight_pair[...], jnp.concatenate(qpn, axis=0))
        field[zw + pw : zw + 2 * pw, :] = nn(weight_pair[...], jnp.concatenate(qnp, axis=0))

        def sub_step(sub, inner):
            at = pl.multiple_of(sub * SUB, SUB)

            def part(c):
                return field[pl.ds(SLOT[c] * channels + at, SUB), :]

            def write(c, value):
                turned[pl.ds(c * channels + at, SUB), here] = value.astype(BF16)

            write(0, zero_ref[0:1, here] * part(0))
            values = [part(c) for c in (1, 2, 3)]
            for b in range(3):
                total = one_ref[0, b : b + 1, here] * values[0]
                for a in range(1, 3):
                    total += one_ref[a, b : b + 1, here] * values[a]
                write(1 + b, total)
            values = [part(c) for c in (5, 6, 7)]
            for b in range(5):
                total = two_ref[1, b : b + 1, here] * values[0]
                for a in range(2, 4):
                    total += two_ref[a, b : b + 1, here] * values[a - 1]
                write(4 + b, total)
            return inner

        lax.fori_loop(0, channels // SUB, sub_step, 0)
        return carry

    lax.fori_loop(0, edges // CHUNK, chunk_step, 0)
    for c in range(9):
        summed = nt(pick_all[...], turned[c * channels : (c + 1) * channels, :])
        own_ref[c] = summed[:atoms]
        blocks = [summed[atoms + block * face : atoms + (block + 1) * face] for block in range(4)]
        for side in range(2):
            even = lax.rem(lax.axis_index(("gx", "yz")[side]), 2) == 0
            low, high = blocks[2 * side], blocks[2 * side + 1]
            ghost_refs[2 * side][c] = jnp.where(even, high, low).astype(BF16)
            ghost_refs[2 * side + 1][c] = jnp.where(even, low, high).astype(BF16)


def back(edge, zero, one, two, pulled, pieces, places, rows, atoms, slots, face):
    members = pieces[0].shape[0]
    edges = pulled.shape[1]
    channels = pulled.shape[0] // 7
    shape = jax.ShapeDtypeStruct
    return pl.pallas_call(
        functools.partial(
            back_kernel, pieces=len(pieces), members=members, atoms=atoms, face=face, places=places
        ),
        in_specs=[VMEM] * (5 + len(pieces)),
        out_specs=[VMEM] * 5,
        out_shape=[shape((9, atoms, channels), F32), *[shape((9, face, channels), BF16)] * 4],
        scratch_shapes=[
            pltpu.VMEM((members, rows, 128), F32),
            pltpu.VMEM((3 * channels, members * 3 * channels), BF16),
            pltpu.VMEM((2 * channels, members * 4 * channels), BF16),
            pltpu.VMEM((7 * channels, CHUNK), F32),
            pltpu.VMEM((9 * channels, edges), BF16),
            pltpu.VMEM((slots, edges), BF16),
        ],
        compiler_params=limits(24),
        cost_estimate=cost(9 * 10**9, 7 * 10**6),
        name="back",
    )(edge, zero, one, two, pulled, *pieces)


def pair_kernel(own_ref, came_ref, *out_refs):
    height = out_refs[0].shape[0]
    row = lax.axis_index("yz")
    for index, out_ref in enumerate(out_refs):
        at = pl.ds(pl.multiple_of((row ^ index) * height, 16), height)
        out_ref[...] = (own_ref[at, :].astype(F32) + came_ref[at, :].astype(F32)).astype(BF16)


def pair_sum(own, came, count):
    height = own.shape[0] // count
    return pl.pallas_call(
        pair_kernel,
        in_specs=[VMEM, VMEM],
        out_specs=[VMEM] * count,
        out_shape=[jax.ShapeDtypeStruct((height, 128), BF16)] * count,
        compiler_params=limits(6),
        cost_estimate=cost(10**6, 2 * 10**6),
        name="pair_sum",
    )(own, came)


def total_kernel(*refs):
    total = refs[0][...].astype(F32)
    for ref in refs[1:-1]:
        total += ref[...].astype(F32)
    refs[-1][...] = total.astype(BF16)


def total_sum(parts):
    return pl.pallas_call(
        total_kernel,
        in_specs=[VMEM] * len(parts),
        out_specs=VMEM,
        out_shape=jax.ShapeDtypeStruct(parts[0].shape, BF16),
        compiler_params=limits(6),
        cost_estimate=cost(10**6, 10**6),
        name="total_sum",
    )(*parts)


def expert_kernel(coef_ref, *refs, scale):
    sums, out_ref, summed = refs[:-2], refs[-2], refs[-1]
    owned = out_ref.shape[0]
    place = lax.axis_index("gx")
    row = lax.broadcasted_iota(jnp.int32, (owned, coef_ref.shape[1]), 0)
    col = lax.broadcasted_iota(jnp.int32, (owned, coef_ref.shape[1]), 1)
    chosen = col == row + place * owned
    picked = [
        jnp.sum(jnp.where(chosen, coef_ref[k : k + 1, :], 0.0), axis=1, keepdims=True) * scale for k in range(2)
    ]
    even = lax.rem(place, 2) == 0
    first = jnp.broadcast_to(jnp.where(even, picked[0], picked[1]), (owned, 128))
    second = jnp.broadcast_to(jnp.where(even, picked[1], picked[0]), (owned, 128))
    half = len(sums) // 2
    for side in range(2):
        total = sums[side * half][...].astype(F32)
        for ref in sums[side * half + 1 : (side + 1) * half]:
            total += ref[...].astype(F32)
        summed[side] = total
    for row in range(summed.shape[1]):
        out_ref[:, row * 128 : (row + 1) * 128] = (
            first * summed[0, row : row + 1, :] + second * summed[1, row : row + 1, :]
        )


def expert_product(coef, sums, owned, scale):
    rows = sums[0].shape[0]
    return pl.pallas_call(
        functools.partial(expert_kernel, scale=scale),
        in_specs=[VMEM] * (1 + len(sums)),
        out_specs=VMEM,
        out_shape=jax.ShapeDtypeStruct((owned, rows * 128), F32),
        scratch_shapes=[pltpu.VMEM((2, rows, 128), F32)],
        compiler_params=limits(8),
        cost_estimate=cost(10**6, 4 * 10**6),
        name="expert_product",
    )(coef, *sums)


def finish_kernel(send_ref, own_ref, a_ref, b_ref, c_ref, d_ref, out_ref):
    atoms = own_ref.shape[1]
    face = send_ref.shape[1]
    row = lax.broadcasted_iota(jnp.int32, (atoms, face), 0)
    picks = []
    for side in range(2):
        even = lax.rem(lax.axis_index(("gx", "yz")[side]), 2) == 0
        below, above = send_ref[2 * side : 2 * side + 1, :], send_ref[2 * side + 1 : 2 * side + 2, :]
        for faces in (jnp.where(even, above, below), jnp.where(even, below, above)):
            picks.append((row == faces).astype(F32).astype(BF16))
    for c in range(9):
        total = own_ref[c]
        for pick, ref in zip(picks, (a_ref, b_ref, c_ref, d_ref)):
            total += nn(pick, ref[c])
        out_ref[c] = total.astype(BF16)


def finish(send, own, returned):
    return pl.pallas_call(
        finish_kernel,
        in_specs=[VMEM] * 6,
        out_specs=VMEM,
        out_shape=jax.ShapeDtypeStruct(own.shape, BF16),
        compiler_params=limits(6),
        cost_estimate=cost(10**8, 2 * 10**6),
        name="finish",
    )(send, own, *returned)


def swap(value, axis, bit):
    return lax.ppermute(value, axis, [(i, i ^ bit) for i in range(lax.axis_size(axis))])


def neighbour_pairs(value, axis, first):
    count = lax.axis_size(axis)
    moves = []
    for low in range(first, count, 2):
        high = (low + 1) % count
        moves += [(low, high), (high, low)]
    return lax.ppermute(value, axis, moves)


def local(
    saved_input, cotangent, neighbours, rot_zero, rot_one, rot_two, send_index, atom_class, live_blocks,
    merge_coef, experts,
):
    atoms, fanout = neighbours.shape
    slots = saved_input.shape[0]
    channels = cotangent.shape[2]
    face = send_index.shape[1]
    count_yz, count_gx = lax.axis_size("yz"), lax.axis_size("gx")
    row, column = lax.axis_index("yz"), lax.axis_index("gx")
    core = column % 2
    height = experts.shape[1] // 128
    rows = height * count_yz
    direct = height % 32 == 0 and count_yz & (count_yz - 1) == 0 and count_gx == 4

    zero = rot_zero.reshape(1, -1)
    source = jnp.transpose(saved_input, (1, 0, 2))
    target = jnp.transpose(cotangent, (1, 0, 2))

    if direct:
        half = height // 2
        mine = merge(merge_coef, experts, 2)
        held = [mine] + [swap(mine, "yz", k) for k in range(1, count_yz)]
        source, target, mine = lax.optimization_barrier((source, target, mine))

        def places():
            here, side = lax.axis_index("yz"), lax.rem(lax.axis_index("gx"), 2)
            starts = [(here ^ k) * height for k in range(count_yz)]
            return [at + side * half for at in starts] + [at + (1 - side) * half for at in starts]
    else:
        part = jnp.dot(merge_coef, experts.astype(F32), precision=lax.Precision.HIGHEST).astype(BF16)
        merged = lax.all_gather(part, "yz", axis=1, tiled=True)
        pieces = [merged.reshape(merged.shape[0], rows, 128)]

        def places():
            return [0]

    other, own, pulled, edge = features(
        live_blocks, neighbours.T, atom_class.reshape(1, -1), zero, rot_one, rot_two, source, target, rows, fanout
    )
    if direct:
        other, *held = lax.optimization_barrier((other, *held))
        came = swap(other, "gx", 1)
        parts = pair_sum(own, came, count_yz)
        gathered = [parts[0]] + [swap(parts[k], "yz", k) for k in range(1, count_yz)]
        pieces = held + [swap(piece, "gx", 1) for piece in held]
    grad_own, *ghosts = back(edge, zero, rot_one, rot_two, pulled, pieces, places, rows, atoms, slots, face)
    returned = [
        neighbour_pairs(ghost, axis, first)
        for ghost, axis, first in zip(ghosts, ("gx", "gx", "yz", "yz"), (0, 1, 0, 1))
    ]
    if direct:
        grad_own, *gathered = lax.optimization_barrier((grad_own, *gathered))
        summed, *returned = lax.optimization_barrier((total_sum(gathered), *returned))
        across = swap(summed, "gx", 2)
        input_grad = finish(send_index, grad_own, returned)
        across, input_grad = lax.optimization_barrier((across, input_grad))
        sums = [summed, across, swap(summed, "gx", 1), swap(across, "gx", 1)]
    else:
        mixed = jnp.stack([own, other]).astype(F32)
        mixed = jnp.where(core == 0, mixed, mixed[::-1])
        whole = lax.psum(mixed, ("yz", "gx"))
        piece = lax.dynamic_slice_in_dim(whole, row * height, height, 1)
        piece = jnp.where(core == 0, piece, piece[::-1])
        sums = [piece[0], piece[1]]
        input_grad = finish(send_index, grad_own, returned)
    grad_scale = math.sqrt(fanout / (atoms * count_yz * count_gx))
    expert_grad = expert_product(merge_coef, sums, merge_coef.shape[1] // count_gx, grad_scale)
    return (jnp.transpose(input_grad, (1, 0, 2)), expert_grad)


def solution(mesh):
    tiles = ("rep", "yz", "gx")
    in_specs = (
        P(tiles, None, None),
        P(tiles, None, None),
        P(tiles, None),
        P(tiles),
        P(None, None, tiles),
        P(None, None, tiles),
        P(tiles, None),
        P(tiles),
        P(tiles),
        P(),
        P(None, "yz"),
    )
    out_specs = (P(tiles, None, None), P(("rep", "gx"), "yz"))
    return jax.shard_map(local, mesh=mesh, in_specs=in_specs, out_specs=out_specs, check_vma=False)
```

```python
import functools
import math

import jax
import jax.numpy as jnp
from jax import lax
from jax.experimental import pallas as pl
from jax.experimental.pallas import tpu as pltpu
from jax.sharding import PartitionSpec as P

LIVE_BLOCK = 64
CHUNK = 256
SUB = 16
F32 = jnp.float32
BF16 = jnp.bfloat16

STACK = (0, 2, 6, 3, 7, 1, 5)
SLOT = {component: place for place, component in enumerate(STACK)}

VMEM = pl.BlockSpec(memory_space=pltpu.VMEM)
SMEM = pl.BlockSpec(memory_space=pltpu.SMEM)
HBM = pl.BlockSpec(memory_space=pltpu.HBM)


def limits(mebibytes):
    return pltpu.CompilerParams(vmem_limit_bytes=mebibytes * 1024 * 1024)


def cost(flops, moved):
    return pl.CostEstimate(flops=flops, bytes_accessed=moved, transcendentals=0)


def nn(left, right):
    return lax.dot_general(left, right, (((1,), (0,)), ((), ())), preferred_element_type=F32)


def nt(left, right):
    return lax.dot_general(left, right, (((1,), (1,)), ((), ())), preferred_element_type=F32)


def split3(value):
    high = value.astype(BF16)
    rest = value - high.astype(F32)
    middle = rest.astype(BF16)
    low = (rest - middle.astype(F32)).astype(BF16)
    return high, middle, low


def merge_kernel(coef_ref, experts_ref, out_ref, held, arrived):
    members, experts = coef_ref.shape
    rows = out_ref.shape[1]
    start = pl.multiple_of(lax.rem(lax.axis_index("gx"), 2) * rows * 128, 128)
    stripes = arrived.shape[0]
    blocks = rows // 16
    edges = [blocks * stripe // stripes for stripe in range(stripes + 1)]
    copies = []
    for stripe in range(stripes):
        at, wide = edges[stripe] * 2048, (edges[stripe + 1] - edges[stripe]) * 2048
        copies.append(
            pltpu.make_async_copy(
                experts_ref.at[:, pl.ds(start + at, wide)], held.at[:, pl.ds(at, wide)], arrived.at[stripe]
            )
        )
        copies[-1].start()
    wide = 8 * experts
    row = lax.broadcasted_iota(jnp.int32, (8, wide), 0)
    col = lax.broadcasted_iota(jnp.int32, (8, wide), 1)
    diagonal = row == col // experts
    source = lax.broadcasted_iota(jnp.int32, (experts, wide), 0)
    target = lax.broadcasted_iota(jnp.int32, (experts, wide), 1)
    tile = (source == target % experts).astype(F32).astype(BF16)
    lefts = []
    for term in split3(coef_ref[...]):
        tiled = nn(term, tile)
        for member in range(members):
            lefts.append(jnp.where(diagonal, tiled[member : member + 1, :], 0.0).astype(BF16))
    lefts = jnp.concatenate(lefts, axis=0)
    height = 8 * members
    for block in range(blocks):
        if block in edges:
            copies[edges.index(block)].wait()
        halves = []
        for half in range(2):
            first = block * 16 + half * 8
            groups = [held[:, (first + g) * 128 : (first + g + 1) * 128] for g in range(8)]
            halves.append(jnp.concatenate(groups, axis=0))
        product = nn(lefts, jnp.concatenate(halves, axis=1))
        total = product[:height] + product[height : 2 * height] + product[2 * height :]
        for member in range(members):
            part = total[member * 8 : member * 8 + 8]
            out_ref[member, block * 16 : block * 16 + 16, :] = jnp.concatenate(
                [part[:, :128], part[:, 128:]], axis=0
            ).astype(BF16)


def merge(coef, experts, parts):
    members, count = coef.shape
    columns = experts.shape[1] // parts
    rows = columns // 128
    return pl.pallas_call(
        merge_kernel,
        in_specs=[VMEM, HBM],
        out_specs=VMEM,
        out_shape=jax.ShapeDtypeStruct((members, rows, 128), BF16),
        scratch_shapes=[pltpu.VMEM((count, columns), BF16), pltpu.SemaphoreType.DMA((4,))],
        compiler_params=limits(60),
        cost_estimate=cost(96 * 16 * columns, 2 * count * columns),
        name="merge",
    )(coef, experts)


def features_kernel(
    live_ref, near_ref, class_ref, zero_ref, one_ref, two_ref, source_ref, target_ref,
    other_ref, own_ref, pulled_ref, edge_ref,
    source_t, target_t, moved, spread, rotated, grads,
    *, fanout,
):
    slots, channels = source_ref.shape[1:]
    atoms = target_ref.shape[1]
    edges = atoms * fanout
    for c in range(9):
        source_t[c * channels : (c + 1) * channels, :] = source_ref[c].T
        target_t[c * channels : (c + 1) * channels, :] = target_ref[c].T
    near = near_ref[...].astype(F32).astype(BF16)
    classes = class_ref[...].astype(F32).astype(BF16)
    live_edges = live_ref[0] * LIVE_BLOCK * fanout
    scale = 1.0 / math.sqrt(fanout)

    def chunk_step(chunk, carry):
        start = pl.multiple_of(chunk * CHUNK, CHUNK)
        here = pl.ds(start, CHUNK)
        edge = lax.broadcasted_iota(jnp.int32, (atoms, CHUNK), 1) + start
        atom = lax.broadcasted_iota(jnp.int32, (atoms, CHUNK), 0)
        repeat = (edge // fanout == atom).astype(F32).astype(BF16)
        edge8 = lax.broadcasted_iota(jnp.int32, (fanout, CHUNK), 1) + start
        lane8 = lax.broadcasted_iota(jnp.int32, (fanout, CHUNK), 0)
        picked = jnp.where(edge8 % fanout == lane8, nn(near, repeat), 0.0)
        near_row = jnp.sum(picked, axis=0, keepdims=True)
        class_row = nn(classes, repeat)
        edge_ref[0:1, here] = near_row
        edge_ref[1:2, here] = jnp.where(edge8[0:1] < live_edges, class_row, -1.0)
        slot = lax.broadcasted_iota(jnp.int32, (slots, CHUNK), 0).astype(F32)
        pick = (slot == near_row).astype(F32).astype(BF16)
        moved[...] = nn(source_t[...], pick)
        spread[...] = nn(target_t[...], repeat)

        def sub_step(sub, inner):
            at = pl.multiple_of(sub * SUB, SUB)

            def turn(field, write):
                def part(c):
                    return field[pl.ds(c * channels + at, SUB), :]

                write(0, zero_ref[0:1, here] * part(0))
                values = [part(c) for c in (1, 2, 3)]
                for a in range(3):
                    total = one_ref[a, 0:1, here] * values[0]
                    for b in range(1, 3):
                        total += one_ref[a, b : b + 1, here] * values[b]
                    write(1 + a, total)
                values = [part(c) for c in (4, 5, 6, 7, 8)]
                for a in range(1, 4):
                    total = two_ref[a, 0:1, here] * values[0]
                    for b in range(1, 5):
                        total += two_ref[a, b : b + 1, here] * values[b]
                    write(4 + a, total)

            def write_rotated(c, value):
                rotated[pl.ds(SLOT[c] * channels + at, SUB), here] = value.astype(BF16)

            def write_pulled(c, value):
                pulled_ref[pl.ds(SLOT[c] * channels + at, SUB), here] = (value * scale).astype(BF16)

            turn(moved, write_rotated)
            turn(spread, write_pulled)
            return inner

        lax.fori_loop(0, channels // SUB, sub_step, 0)
        return carry

    lax.fori_loop(0, edges // CHUNK, chunk_step, 0)
    zw, pw = 3 * channels, 2 * channels
    first = zw * zw // 128
    second = first + pw * pw // 128
    own = lax.rem(lax.axis_index("gx"), 2).astype(F32)
    for out_ref, wanted in ((other_ref, 1.0 - own), (own_ref, own)):
        mask = (edge_ref[1:2, :] == wanted).astype(F32).astype(BF16)
        qz = pulled_ref[0:zw, :] * mask
        qp = pulled_ref[zw : zw + pw, :] * mask
        qn = pulled_ref[zw + pw : zw + 2 * pw, :] * mask
        z, p, n = rotated[0:zw, :], rotated[zw : zw + pw, :], rotated[zw + pw : zw + 2 * pw, :]
        whole = nt(z, qz)
        for j in range(zw // 128):
            grads[pl.ds(j, zw, stride=zw // 128), :] = whole[:, j * 128 : (j + 1) * 128]
        coupled = nt(p, qp) + nt(n, qn)
        crossed = nt(p, qn) - nt(n, qp)
        for j in range(pw // 128):
            grads[pl.ds(first + j, pw, stride=pw // 128), :] = coupled[:, j * 128 : (j + 1) * 128]
            grads[pl.ds(second + j, pw, stride=pw // 128), :] = crossed[:, j * 128 : (j + 1) * 128]
        out_ref[...] = grads[...].astype(BF16)


def features(live, near, classes, zero, one, two, source, target, rows, fanout):
    slots, channels = source.shape[1:]
    atoms = target.shape[1]
    edges = atoms * fanout
    shape = jax.ShapeDtypeStruct
    return pl.pallas_call(
        functools.partial(features_kernel, fanout=fanout),
        in_specs=[SMEM] + [VMEM] * 7,
        out_specs=[VMEM] * 4,
        out_shape=[
            shape((rows, 128), BF16),
            shape((rows, 128), BF16),
            shape((7 * channels, edges), BF16),
            shape((8, edges), F32),
        ],
        scratch_shapes=[
            pltpu.VMEM((9 * channels, slots), BF16),
            pltpu.VMEM((9 * channels, atoms), BF16),
            pltpu.VMEM((9 * channels, CHUNK), F32),
            pltpu.VMEM((9 * channels, CHUNK), F32),
            pltpu.VMEM((7 * channels, edges), BF16),
            pltpu.VMEM((rows, 128), F32),
        ],
        compiler_params=limits(24),
        cost_estimate=cost(9 * 10**9, 7 * 10**6),
        name="features",
    )(live, near, classes, zero, one, two, source, target)


def back_kernel(
    edge_ref, zero_ref, one_ref, two_ref, pulled_ref, *rest, pieces, members, atoms, face, places,
):
    piece_refs = rest[:pieces]
    own_ref, *ghost_refs = rest[pieces : pieces + 5]
    flat, weight_zero, weight_pair, field, turned, pick_all = rest[pieces + 5 :]
    rows = flat.shape[1]
    channels = own_ref.shape[2]
    slots = pick_all.shape[0]
    edges = pulled_ref.shape[1]
    zw, pw = 3 * channels, 2 * channels
    first = zw * zw // 128
    second = first + pw * pw // 128
    placed = [(piece, index) for piece in piece_refs for index in range(piece.shape[0])]
    for (piece, index), place in zip(placed, places()):
        height = piece.shape[2]
        at = pl.ds(pl.multiple_of(place, 16), height)
        for k in range(members):
            flat[k, at, :] = piece[index, k].astype(F32)
    for k in range(members):
        for j in range(zw // 128):
            weight_zero[:, k * zw + j * 128 : k * zw + (j + 1) * 128] = flat[
                k, pl.ds(j, zw, stride=zw // 128), :
            ].astype(BF16)
        for j in range(pw // 128):
            at = k * 2 * pw + j * 128
            weight_pair[:, at : at + 128] = flat[k, pl.ds(first + j, pw, stride=pw // 128), :].astype(BF16)
            weight_pair[:, at + pw : at + pw + 128] = flat[
                k, pl.ds(second + j, pw, stride=pw // 128), :
            ].astype(BF16)

    def chunk_step(chunk, carry):
        start = pl.multiple_of(chunk * CHUNK, CHUNK)
        here = pl.ds(start, CHUNK)
        slot = lax.broadcasted_iota(jnp.int32, (slots, CHUNK), 0).astype(F32)
        pick_all[:, here] = (slot == edge_ref[0:1, here]).astype(F32).astype(BF16)
        qz, qpn, qnp = [], [], []
        for k in range(members):
            mask = (edge_ref[1:2, here] == float(k)).astype(F32).astype(BF16)
            qz.append(pulled_ref[0:zw, here] * mask)
            qp = pulled_ref[zw : zw + pw, here] * mask
            qn = pulled_ref[zw + pw : zw + 2 * pw, here] * mask
            qpn += [qp, qn]
            qnp += [qn, -qp]
        field[0:zw, :] = nn(weight_zero[...], jnp.concatenate(qz, axis=0))
        field[zw : zw + pw, :] = nn(weight_pair[...], jnp.concatenate(qpn, axis=0))
        field[zw + pw : zw + 2 * pw, :] = nn(weight_pair[...], jnp.concatenate(qnp, axis=0))

        def sub_step(sub, inner):
            at = pl.multiple_of(sub * SUB, SUB)

            def part(c):
                return field[pl.ds(SLOT[c] * channels + at, SUB), :]

            def write(c, value):
                turned[pl.ds(c * channels + at, SUB), here] = value.astype(BF16)

            write(0, zero_ref[0:1, here] * part(0))
            values = [part(c) for c in (1, 2, 3)]
            for b in range(3):
                total = one_ref[0, b : b + 1, here] * values[0]
                for a in range(1, 3):
                    total += one_ref[a, b : b + 1, here] * values[a]
                write(1 + b, total)
            values = [part(c) for c in (5, 6, 7)]
            for b in range(5):
                total = two_ref[1, b : b + 1, here] * values[0]
                for a in range(2, 4):
                    total += two_ref[a, b : b + 1, here] * values[a - 1]
                write(4 + b, total)
            return inner

        lax.fori_loop(0, channels // SUB, sub_step, 0)
        return carry

    lax.fori_loop(0, edges // CHUNK, chunk_step, 0)
    for c in range(9):
        summed = nt(pick_all[...], turned[c * channels : (c + 1) * channels, :])
        own_ref[c] = summed[:atoms]
        blocks = [summed[atoms + block * face : atoms + (block + 1) * face] for block in range(4)]
        for side in range(2):
            even = lax.rem(lax.axis_index(("gx", "yz")[side]), 2) == 0
            low, high = blocks[2 * side], blocks[2 * side + 1]
            at = pl.ds(c * face, face)
            ghost_refs[2 * side][at, :] = jnp.where(even, high, low).astype(BF16)
            ghost_refs[2 * side + 1][at, :] = jnp.where(even, low, high).astype(BF16)


def back(edge, zero, one, two, pulled, pieces, places, rows, atoms, slots, face):
    members = pieces[0].shape[1]
    edges = pulled.shape[1]
    channels = pulled.shape[0] // 7
    shape = jax.ShapeDtypeStruct
    return pl.pallas_call(
        functools.partial(
            back_kernel, pieces=len(pieces), members=members, atoms=atoms, face=face, places=places
        ),
        in_specs=[VMEM] * (5 + len(pieces)),
        out_specs=[VMEM] * 5,
        out_shape=[shape((9, atoms, channels), F32), *[shape((9 * face, channels), BF16)] * 4],
        scratch_shapes=[
            pltpu.VMEM((members, rows, 128), F32),
            pltpu.VMEM((3 * channels, members * 3 * channels), BF16),
            pltpu.VMEM((2 * channels, members * 4 * channels), BF16),
            pltpu.VMEM((7 * channels, CHUNK), F32),
            pltpu.VMEM((9 * channels, edges), BF16),
            pltpu.VMEM((slots, edges), BF16),
        ],
        compiler_params=limits(24),
        cost_estimate=cost(9 * 10**9, 7 * 10**6),
        name="back",
    )(edge, zero, one, two, pulled, *pieces)


def core_kernel(own_ref, came_ref, away_ref, keep_ref):
    count = lax.axis_size("yz")
    half = keep_ref.shape[0] // count
    row, side = lax.axis_index("yz"), lax.axis_index("gx") // 2
    for k in range(count):
        start = (row ^ k) * 2 * half
        here = pl.ds(k * half, half)
        near = pl.ds(pl.multiple_of(start + side * half, 16), half)
        far = pl.ds(pl.multiple_of(start + (1 - side) * half, 16), half)
        keep_ref[here, :] = own_ref[near, :].astype(F32) + came_ref[near, :].astype(F32)
        away_ref[here, :] = (own_ref[far, :].astype(F32) + came_ref[far, :].astype(F32)).astype(BF16)


def core_sum(own, came):
    shape = (own.shape[0] // 2, 128)
    return pl.pallas_call(
        core_kernel,
        in_specs=[VMEM] * 2,
        out_specs=[VMEM] * 2,
        out_shape=[jax.ShapeDtypeStruct(shape, BF16), jax.ShapeDtypeStruct(shape, F32)],
        compiler_params=limits(6),
        cost_estimate=cost(10**6, 2 * 10**6),
        name="core_sum",
    )(own, came)


def side_kernel(keep_ref, came_ref, low_ref, high_ref, own_ref, *out_refs):
    half = own_ref.shape[0]
    own_ref[...] = keep_ref[:half] + came_ref[:half].astype(F32)
    for k, out_ref in enumerate(out_refs, 1):
        at = pl.ds(k * half, half)
        out_ref[:half] = (keep_ref[at, :] + came_ref[at, :].astype(F32)).astype(BF16)
    out_refs[0][half:] = low_ref[...]
    out_refs[-1][half:] = high_ref[...]


def side_sum(keep, came, low, high, count):
    half = keep.shape[0] // count
    faces = low.shape[0]
    shape = jax.ShapeDtypeStruct
    sent = [shape((half + (faces if k in (1, count - 1) else 0), 128), BF16) for k in range(1, count)]
    return pl.pallas_call(
        side_kernel,
        in_specs=[VMEM] * 4,
        out_specs=[VMEM] * count,
        out_shape=[shape((half, 128), F32), *sent],
        compiler_params=limits(6),
        cost_estimate=cost(10**6, 2 * 10**6),
        name="side_sum",
    )(keep, came, low, high)


def total_kernel(*refs):
    half = refs[-1].shape[0]
    total = refs[0][...]
    for ref in refs[1:-1]:
        total += ref[:half].astype(F32)
    refs[-1][...] = total.astype(BF16)


def total_sum(parts):
    return pl.pallas_call(
        total_kernel,
        in_specs=[VMEM] * len(parts),
        out_specs=VMEM,
        out_shape=jax.ShapeDtypeStruct(parts[0].shape, BF16),
        compiler_params=limits(6),
        cost_estimate=cost(10**6, 10**6),
        name="total_sum",
    )(*parts)


def pack_kernel(*refs):
    for index, ref in enumerate(refs[:-1]):
        refs[-1][index] = ref[...]


def pack(pieces):
    return pl.pallas_call(
        pack_kernel,
        in_specs=[VMEM] * len(pieces),
        out_specs=VMEM,
        out_shape=jax.ShapeDtypeStruct((len(pieces), *pieces[0].shape), pieces[0].dtype),
        compiler_params=limits(6),
        cost_estimate=cost(10**5, 10**6),
        name="pack",
    )(*pieces)


def expert_kernel(coef_ref, *refs, scale):
    sums, out_ref, summed = refs[:-2], refs[-2], refs[-1]
    owned = out_ref.shape[0]
    place = lax.axis_index("gx")
    row = lax.broadcasted_iota(jnp.int32, (owned, coef_ref.shape[1]), 0)
    col = lax.broadcasted_iota(jnp.int32, (owned, coef_ref.shape[1]), 1)
    chosen = col == row + place * owned
    picked = [
        jnp.sum(jnp.where(chosen, coef_ref[k : k + 1, :], 0.0), axis=1, keepdims=True) * scale for k in range(2)
    ]
    even = lax.rem(place, 2) == 0
    first = jnp.broadcast_to(jnp.where(even, picked[0], picked[1]), (owned, 128))
    second = jnp.broadcast_to(jnp.where(even, picked[1], picked[0]), (owned, 128))
    if len(sums) == 4:
        half = sums[0].shape[0]
        side = place // 2
        for index, ref in enumerate(sums):
            at = (side if index % 2 == 0 else 1 - side) * half
            summed[index // 2, pl.ds(pl.multiple_of(at, 16), half), :] = ref[...].astype(F32)
    else:
        for index, ref in enumerate(sums):
            summed[index] = ref[...].astype(F32)
    for row in range(summed.shape[1]):
        out_ref[:, row * 128 : (row + 1) * 128] = (
            first * summed[0, row : row + 1, :] + second * summed[1, row : row + 1, :]
        )


def expert_product(coef, sums, owned, scale):
    rows = sums[0].shape[0] * len(sums) // 2
    return pl.pallas_call(
        functools.partial(expert_kernel, scale=scale),
        in_specs=[VMEM] * (1 + len(sums)),
        out_specs=VMEM,
        out_shape=jax.ShapeDtypeStruct((owned, rows * 128), F32),
        scratch_shapes=[pltpu.VMEM((2, rows, 128), F32)],
        compiler_params=limits(8),
        cost_estimate=cost(10**6, 4 * 10**6),
        name="expert_product",
    )(coef, *sums)


def finish_kernel(send_ref, own_ref, a_ref, b_ref, c_ref, d_ref, out_ref):
    atoms = own_ref.shape[1]
    face = send_ref.shape[1]
    row = lax.broadcasted_iota(jnp.int32, (atoms, face), 0)
    picks = []
    for side in range(2):
        even = lax.rem(lax.axis_index(("gx", "yz")[side]), 2) == 0
        below, above = send_ref[2 * side : 2 * side + 1, :], send_ref[2 * side + 1 : 2 * side + 2, :]
        for faces in (jnp.where(even, above, below), jnp.where(even, below, above)):
            picks.append((row == faces).astype(F32).astype(BF16))
    for c in range(9):
        total = own_ref[c]
        for pick, ref in zip(picks, (a_ref, b_ref, c_ref, d_ref)):
            at = ref.shape[0] - 9 * face + c * face
            total += nn(pick, ref[at : at + face])
        out_ref[c] = total.astype(BF16)


def finish(send, own, returned):
    return pl.pallas_call(
        finish_kernel,
        in_specs=[VMEM] * 6,
        out_specs=VMEM,
        out_shape=jax.ShapeDtypeStruct(own.shape, BF16),
        compiler_params=limits(6),
        cost_estimate=cost(10**8, 2 * 10**6),
        name="finish",
    )(send, own, *returned)


def swap(value, axis, bit):
    return lax.ppermute(value, axis, [(i, i ^ bit) for i in range(lax.axis_size(axis))])


def neighbour_pairs(value, axis, first):
    count = lax.axis_size(axis)
    moves = []
    for low in range(first, count, 2):
        high = (low + 1) % count
        moves += [(low, high), (high, low)]
    return lax.ppermute(value, axis, moves)


def local(
    saved_input, cotangent, neighbours, rot_zero, rot_one, rot_two, send_index, atom_class, live_blocks,
    merge_coef, experts,
):
    atoms, fanout = neighbours.shape
    slots = saved_input.shape[0]
    channels = cotangent.shape[2]
    face = send_index.shape[1]
    count_yz, count_gx = lax.axis_size("yz"), lax.axis_size("gx")
    row, column = lax.axis_index("yz"), lax.axis_index("gx")
    core = column % 2
    height = experts.shape[1] // 128
    rows = height * count_yz
    direct = height % 32 == 0 and count_yz == 4 and count_gx == 4

    zero = rot_zero.reshape(1, -1)
    source = jnp.transpose(saved_input, (1, 0, 2))
    target = jnp.transpose(cotangent, (1, 0, 2))

    if direct:
        half = height // 2
        mine = merge(merge_coef, experts, 2)
        held = [mine] + [swap(mine, "yz", k) for k in range(1, count_yz)]
        source, target, mine = lax.optimization_barrier((source, target, mine))

        def places():
            here, side = lax.axis_index("yz"), lax.rem(lax.axis_index("gx"), 2)
            starts = [(here ^ k) * height for k in range(count_yz)]
            return [at + side * half for at in starts] + [at + (1 - side) * half for at in starts]
    else:
        part = jnp.dot(merge_coef, experts.astype(F32), precision=lax.Precision.HIGHEST).astype(BF16)
        merged = lax.all_gather(part, "yz", axis=1, tiled=True)
        pieces = [merged.reshape(1, merged.shape[0], rows, 128)]

        def places():
            return [0]

    other, own, pulled, edge = features(
        live_blocks, neighbours.T, atom_class.reshape(1, -1), zero, rot_one, rot_two, source, target, rows, fanout
    )
    if direct:
        other, *held = lax.optimization_barrier((other, *held))
        came = swap(other, "gx", 1)
        away, keep = core_sum(own, came)
        opposite = swap(away, "gx", 2)
        held = pack(held)
        pieces = [held, swap(held, "gx", 1)]
    grad_own, *ghosts = back(edge, zero, rot_one, rot_two, pulled, pieces, places, rows, atoms, slots, face)
    across_gx = [neighbour_pairs(ghosts[first], "gx", first) for first in range(2)]
    if direct:
        parts = side_sum(keep, opposite, ghosts[2], ghosts[3], count_yz)
        gathered = [parts[0]] + [swap(parts[k], "yz", k) for k in range(1, count_yz)]
        summed, *across_gx = lax.optimization_barrier((total_sum(gathered), *across_gx))
        across = swap(summed, "gx", 2)
        input_grad = finish(send_index, grad_own, [*across_gx, gathered[1], gathered[3]])
        across, input_grad = lax.optimization_barrier((across, input_grad))
        sums = [summed, across, swap(summed, "gx", 1), swap(across, "gx", 1)]
    else:
        mixed = jnp.stack([own, other]).astype(F32)
        mixed = jnp.where(core == 0, mixed, mixed[::-1])
        whole = lax.psum(mixed, ("yz", "gx"))
        piece = lax.dynamic_slice_in_dim(whole, row * height, height, 1)
        piece = jnp.where(core == 0, piece, piece[::-1])
        sums = [piece[0], piece[1]]
        across_yz = [neighbour_pairs(ghosts[2 + first], "yz", first) for first in range(2)]
        input_grad = finish(send_index, grad_own, [*across_gx, *across_yz])
    grad_scale = math.sqrt(fanout / (atoms * count_yz * count_gx))
    expert_grad = expert_product(merge_coef, sums, merge_coef.shape[1] // count_gx, grad_scale)
    return (jnp.transpose(input_grad, (1, 0, 2)), expert_grad)


def solution(mesh):
    tiles = ("rep", "yz", "gx")
    in_specs = (
        P(tiles, None, None),
        P(tiles, None, None),
        P(tiles, None),
        P(tiles),
        P(None, None, tiles),
        P(None, None, tiles),
        P(tiles, None),
        P(tiles),
        P(tiles),
        P(),
        P(None, "yz"),
    )
    out_specs = (P(tiles, None, None), P(("rep", "gx"), "yz"))
    return jax.shard_map(local, mesh=mesh, in_specs=in_specs, out_specs=out_specs, check_vma=False)
```

```python
import functools
import math

import jax
import jax.numpy as jnp
from jax import lax
from jax.experimental import pallas as pl
from jax.experimental.pallas import tpu as pltpu
from jax.sharding import PartitionSpec as P

LIVE_BLOCK = 64
CHUNK = 256
SUB = 16
F32 = jnp.float32
BF16 = jnp.bfloat16

STACK = (0, 2, 6, 3, 7, 1, 5)
SLOT = {component: place for place, component in enumerate(STACK)}

VMEM = pl.BlockSpec(memory_space=pltpu.VMEM)
SMEM = pl.BlockSpec(memory_space=pltpu.SMEM)
HBM = pl.BlockSpec(memory_space=pltpu.HBM)


def limits(mebibytes):
    return pltpu.CompilerParams(vmem_limit_bytes=mebibytes * 1024 * 1024)


def cost(flops, moved):
    return pl.CostEstimate(flops=flops, bytes_accessed=moved, transcendentals=0)


def nn(left, right):
    return lax.dot_general(left, right, (((1,), (0,)), ((), ())), preferred_element_type=F32)


def nt(left, right):
    return lax.dot_general(left, right, (((1,), (1,)), ((), ())), preferred_element_type=F32)


def split3(value):
    high = value.astype(BF16)
    rest = value - high.astype(F32)
    middle = rest.astype(BF16)
    low = (rest - middle.astype(F32)).astype(BF16)
    return high, middle, low


def merge_kernel(coef_in_ref, experts_ref, out_ref, held, coef_ref, arrived, coef_arrived):
    members, experts = coef_in_ref.shape
    rows = out_ref.shape[1]
    start = pl.multiple_of(lax.rem(lax.axis_index("gx"), 2) * rows * 128, 128)
    stripes = arrived.shape[0]
    blocks = rows // 16
    edges = [blocks * stripe // stripes for stripe in range(stripes + 1)]
    copies = []
    for stripe in range(stripes):
        at, wide = edges[stripe] * 2048, (edges[stripe + 1] - edges[stripe]) * 2048
        copies.append(
            pltpu.make_async_copy(
                experts_ref.at[:, pl.ds(start + at, wide)], held.at[:, pl.ds(at, wide)], arrived.at[stripe]
            )
        )
        copies[-1].start()
    coef_copy = pltpu.make_async_copy(coef_in_ref, coef_ref, coef_arrived)
    coef_copy.start()
    coef_copy.wait()
    wide = 8 * experts
    row = lax.broadcasted_iota(jnp.int32, (8, wide), 0)
    col = lax.broadcasted_iota(jnp.int32, (8, wide), 1)
    diagonal = row == col // experts
    source = lax.broadcasted_iota(jnp.int32, (experts, wide), 0)
    target = lax.broadcasted_iota(jnp.int32, (experts, wide), 1)
    tile = (source == target % experts).astype(F32).astype(BF16)
    lefts = []
    for term in split3(coef_ref[...]):
        tiled = nn(term, tile)
        for member in range(members):
            lefts.append(jnp.where(diagonal, tiled[member : member + 1, :], 0.0).astype(BF16))
    lefts = jnp.concatenate(lefts, axis=0)
    height = 8 * members
    for block in range(blocks):
        if block in edges:
            copies[edges.index(block)].wait()
        halves = []
        for half in range(2):
            first = block * 16 + half * 8
            groups = [held[:, (first + g) * 128 : (first + g + 1) * 128] for g in range(8)]
            halves.append(jnp.concatenate(groups, axis=0))
        product = nn(lefts, jnp.concatenate(halves, axis=1))
        total = product[:height] + product[height : 2 * height] + product[2 * height :]
        for member in range(members):
            part = total[member * 8 : member * 8 + 8]
            out_ref[member, block * 16 : block * 16 + 16, :] = jnp.concatenate(
                [part[:, :128], part[:, 128:]], axis=0
            ).astype(BF16)


def merge(coef, experts, parts):
    members, count = coef.shape
    columns = experts.shape[1] // parts
    rows = columns // 128
    return pl.pallas_call(
        merge_kernel,
        in_specs=[HBM, HBM],
        out_specs=VMEM,
        out_shape=jax.ShapeDtypeStruct((members, rows, 128), BF16),
        scratch_shapes=[
            pltpu.VMEM((count, columns), BF16),
            pltpu.VMEM((members, count), F32),
            pltpu.SemaphoreType.DMA((2,)),
            pltpu.SemaphoreType.DMA,
        ],
        compiler_params=limits(52),
        cost_estimate=cost(96 * 16 * columns, 2 * count * columns),
        name="merge",
    )(coef, experts)


def features_kernel(
    live_ref, near_ref, class_ref, zero_ref, one_ref, two_ref, source_ref, target_ref,
    other_ref, own_ref, pulled_ref, edge_ref,
    source_t, target_t, moved, spread, rotated, grads,
    *, fanout,
):
    slots, channels = source_ref.shape[1:]
    atoms = target_ref.shape[1]
    edges = atoms * fanout
    for c in range(9):
        source_t[c * channels : (c + 1) * channels, :] = source_ref[c].T
        target_t[c * channels : (c + 1) * channels, :] = target_ref[c].T
    near = near_ref[...].astype(F32).astype(BF16)
    classes = class_ref[...].astype(F32).astype(BF16)
    live_edges = live_ref[0] * LIVE_BLOCK * fanout
    scale = 1.0 / math.sqrt(fanout)

    def chunk_step(chunk, carry):
        start = pl.multiple_of(chunk * CHUNK, CHUNK)
        here = pl.ds(start, CHUNK)
        edge = lax.broadcasted_iota(jnp.int32, (atoms, CHUNK), 1) + start
        atom = lax.broadcasted_iota(jnp.int32, (atoms, CHUNK), 0)
        repeat = (edge // fanout == atom).astype(F32).astype(BF16)
        edge8 = lax.broadcasted_iota(jnp.int32, (fanout, CHUNK), 1) + start
        lane8 = lax.broadcasted_iota(jnp.int32, (fanout, CHUNK), 0)
        picked = jnp.where(edge8 % fanout == lane8, nn(near, repeat), 0.0)
        near_row = jnp.sum(picked, axis=0, keepdims=True)
        class_row = nn(classes, repeat)
        edge_ref[0:1, here] = near_row
        edge_ref[1:2, here] = jnp.where(edge8[0:1] < live_edges, class_row, -1.0)
        slot = lax.broadcasted_iota(jnp.int32, (slots, CHUNK), 0).astype(F32)
        pick = (slot == near_row).astype(F32).astype(BF16)
        moved[...] = nn(source_t[...], pick)
        spread[...] = nn(target_t[...], repeat)

        def sub_step(sub, inner):
            at = pl.multiple_of(sub * SUB, SUB)

            def turn(field, write):
                def part(c):
                    return field[pl.ds(c * channels + at, SUB), :]

                write(0, zero_ref[0:1, here] * part(0))
                values = [part(c) for c in (1, 2, 3)]
                for a in range(3):
                    total = one_ref[a, 0:1, here] * values[0]
                    for b in range(1, 3):
                        total += one_ref[a, b : b + 1, here] * values[b]
                    write(1 + a, total)
                values = [part(c) for c in (4, 5, 6, 7, 8)]
                for a in range(1, 4):
                    total = two_ref[a, 0:1, here] * values[0]
                    for b in range(1, 5):
                        total += two_ref[a, b : b + 1, here] * values[b]
                    write(4 + a, total)

            def write_rotated(c, value):
                rotated[pl.ds(SLOT[c] * channels + at, SUB), here] = value.astype(BF16)

            def write_pulled(c, value):
                pulled_ref[pl.ds(SLOT[c] * channels + at, SUB), here] = (value * scale).astype(BF16)

            turn(moved, write_rotated)
            turn(spread, write_pulled)
            return inner

        lax.fori_loop(0, channels // SUB, sub_step, 0)
        return carry

    lax.fori_loop(0, edges // CHUNK, chunk_step, 0)
    zw, pw = 3 * channels, 2 * channels
    first = zw * zw // 128
    second = first + pw * pw // 128
    own = lax.rem(lax.axis_index("gx"), 2).astype(F32)
    for out_ref, wanted in ((other_ref, 1.0 - own), (own_ref, own)):
        mask = (edge_ref[1:2, :] == wanted).astype(F32).astype(BF16)
        qz = pulled_ref[0:zw, :] * mask
        qp = pulled_ref[zw : zw + pw, :] * mask
        qn = pulled_ref[zw + pw : zw + 2 * pw, :] * mask
        z, p, n = rotated[0:zw, :], rotated[zw : zw + pw, :], rotated[zw + pw : zw + 2 * pw, :]
        whole = nt(z, qz)
        for j in range(zw // 128):
            grads[pl.ds(j, zw, stride=zw // 128), :] = whole[:, j * 128 : (j + 1) * 128]
        coupled = nt(p, qp) + nt(n, qn)
        crossed = nt(p, qn) - nt(n, qp)
        for j in range(pw // 128):
            grads[pl.ds(first + j, pw, stride=pw // 128), :] = coupled[:, j * 128 : (j + 1) * 128]
            grads[pl.ds(second + j, pw, stride=pw // 128), :] = crossed[:, j * 128 : (j + 1) * 128]
        out_ref[...] = grads[...].astype(BF16)


def features(live, near, classes, zero, one, two, source, target, rows, fanout):
    slots, channels = source.shape[1:]
    atoms = target.shape[1]
    edges = atoms * fanout
    shape = jax.ShapeDtypeStruct
    return pl.pallas_call(
        functools.partial(features_kernel, fanout=fanout),
        in_specs=[SMEM] + [VMEM] * 7,
        out_specs=[VMEM] * 4,
        out_shape=[
            shape((rows, 128), BF16),
            shape((rows, 128), BF16),
            shape((7 * channels, edges), BF16),
            shape((8, edges), F32),
        ],
        scratch_shapes=[
            pltpu.VMEM((9 * channels, slots), BF16),
            pltpu.VMEM((9 * channels, atoms), BF16),
            pltpu.VMEM((9 * channels, CHUNK), F32),
            pltpu.VMEM((9 * channels, CHUNK), F32),
            pltpu.VMEM((7 * channels, edges), BF16),
            pltpu.VMEM((rows, 128), F32),
        ],
        compiler_params=limits(24),
        cost_estimate=cost(9 * 10**9, 7 * 10**6),
        name="features",
    )(live, near, classes, zero, one, two, source, target)


def back_kernel(
    edge_ref, zero_ref, one_ref, two_ref, pulled_ref, *rest, pieces, members, atoms, face, places,
):
    piece_refs = rest[:pieces]
    own_ref, *ghost_refs = rest[pieces : pieces + 5]
    flat, weight_zero, weight_pair, field, turned, pick_all = rest[pieces + 5 :]
    rows = flat.shape[1]
    channels = own_ref.shape[2]
    slots = pick_all.shape[0]
    edges = pulled_ref.shape[1]
    zw, pw = 3 * channels, 2 * channels
    first = zw * zw // 128
    second = first + pw * pw // 128
    placed = [(piece, index) for piece in piece_refs for index in range(piece.shape[0])]
    for (piece, index), place in zip(placed, places()):
        height = piece.shape[2]
        at = pl.ds(pl.multiple_of(place, 16), height)
        for k in range(members):
            flat[k, at, :] = piece[index, k].astype(F32)
    for k in range(members):
        for j in range(zw // 128):
            weight_zero[:, k * zw + j * 128 : k * zw + (j + 1) * 128] = flat[
                k, pl.ds(j, zw, stride=zw // 128), :
            ].astype(BF16)
        for j in range(pw // 128):
            at = k * 2 * pw + j * 128
            weight_pair[:, at : at + 128] = flat[k, pl.ds(first + j, pw, stride=pw // 128), :].astype(BF16)
            weight_pair[:, at + pw : at + pw + 128] = flat[
                k, pl.ds(second + j, pw, stride=pw // 128), :
            ].astype(BF16)

    def chunk_step(chunk, carry):
        start = pl.multiple_of(chunk * CHUNK, CHUNK)
        here = pl.ds(start, CHUNK)
        slot = lax.broadcasted_iota(jnp.int32, (slots, CHUNK), 0).astype(F32)
        pick_all[:, here] = (slot == edge_ref[0:1, here]).astype(F32).astype(BF16)
        qz, qpn, qnp = [], [], []
        for k in range(members):
            mask = (edge_ref[1:2, here] == float(k)).astype(F32).astype(BF16)
            qz.append(pulled_ref[0:zw, here] * mask)
            qp = pulled_ref[zw : zw + pw, here] * mask
            qn = pulled_ref[zw + pw : zw + 2 * pw, here] * mask
            qpn += [qp, qn]
            qnp += [qn, -qp]
        field[0:zw, :] = nn(weight_zero[...], jnp.concatenate(qz, axis=0))
        field[zw : zw + pw, :] = nn(weight_pair[...], jnp.concatenate(qpn, axis=0))
        field[zw + pw : zw + 2 * pw, :] = nn(weight_pair[...], jnp.concatenate(qnp, axis=0))

        def sub_step(sub, inner):
            at = pl.multiple_of(sub * SUB, SUB)

            def part(c):
                return field[pl.ds(SLOT[c] * channels + at, SUB), :]

            def write(c, value):
                turned[pl.ds(c * channels + at, SUB), here] = value.astype(BF16)

            write(0, zero_ref[0:1, here] * part(0))
            values = [part(c) for c in (1, 2, 3)]
            for b in range(3):
                total = one_ref[0, b : b + 1, here] * values[0]
                for a in range(1, 3):
                    total += one_ref[a, b : b + 1, here] * values[a]
                write(1 + b, total)
            values = [part(c) for c in (5, 6, 7)]
            for b in range(5):
                total = two_ref[1, b : b + 1, here] * values[0]
                for a in range(2, 4):
                    total += two_ref[a, b : b + 1, here] * values[a - 1]
                write(4 + b, total)
            return inner

        lax.fori_loop(0, channels // SUB, sub_step, 0)
        return carry

    lax.fori_loop(0, edges // CHUNK, chunk_step, 0)
    for c in range(9):
        summed = nt(pick_all[...], turned[c * channels : (c + 1) * channels, :])
        own_ref[c] = summed[:atoms]
        blocks = [summed[atoms + block * face : atoms + (block + 1) * face] for block in range(4)]
        for side in range(2):
            even = lax.rem(lax.axis_index(("gx", "yz")[side]), 2) == 0
            low, high = blocks[2 * side], blocks[2 * side + 1]
            ghost_refs[3 - side][c] = jnp.where(even, high, low).astype(BF16)
            ghost_refs[1 - side][c] = jnp.where(even, low, high).astype(BF16)


def back(edge, zero, one, two, pulled, pieces, places, rows, atoms, slots, face):
    members = pieces[0].shape[1]
    edges = pulled.shape[1]
    channels = pulled.shape[0] // 7
    shape = jax.ShapeDtypeStruct
    return pl.pallas_call(
        functools.partial(
            back_kernel, pieces=len(pieces), members=members, atoms=atoms, face=face, places=places
        ),
        in_specs=[VMEM] * (5 + len(pieces)),
        out_specs=[VMEM] * 5,
        out_shape=[shape((9, atoms, channels), F32), *[shape((9, face, channels), BF16)] * 4],
        scratch_shapes=[
            pltpu.VMEM((members, rows, 128), F32),
            pltpu.VMEM((3 * channels, members * 3 * channels), BF16),
            pltpu.VMEM((2 * channels, members * 4 * channels), BF16),
            pltpu.VMEM((7 * channels, CHUNK), F32),
            pltpu.VMEM((9 * channels, edges), BF16),
            pltpu.VMEM((slots, edges), BF16),
        ],
        compiler_params=limits(24),
        cost_estimate=cost(9 * 10**9, 7 * 10**6),
        name="back",
    )(edge, zero, one, two, pulled, *pieces)


def pair_kernel(own_ref, came_ref, *out_refs):
    height = out_refs[0].shape[0]
    row = lax.axis_index("yz")
    for index, out_ref in enumerate(out_refs):
        at = pl.ds(pl.multiple_of((row ^ index) * height, 16), height)
        out_ref[...] = (own_ref[at, :].astype(F32) + came_ref[at, :].astype(F32)).astype(BF16)


def pair_sum(own, came, count):
    height = own.shape[0] // count
    return pl.pallas_call(
        pair_kernel,
        in_specs=[VMEM, VMEM],
        out_specs=[VMEM] * count,
        out_shape=[jax.ShapeDtypeStruct((height, 128), BF16)] * count,
        compiler_params=limits(6),
        cost_estimate=cost(10**6, 2 * 10**6),
        name="pair_sum",
    )(own, came)


def total_kernel(*refs):
    total = refs[0][...].astype(F32)
    for ref in refs[1:-1]:
        total += ref[...].astype(F32)
    refs[-1][...] = total.astype(BF16)


def total_sum(parts):
    return pl.pallas_call(
        total_kernel,
        in_specs=[VMEM] * len(parts),
        out_specs=VMEM,
        out_shape=jax.ShapeDtypeStruct(parts[0].shape, BF16),
        compiler_params=limits(6),
        cost_estimate=cost(10**6, 10**6),
        name="total_sum",
    )(*parts)


def pack_kernel(*refs):
    for index, ref in enumerate(refs[:-1]):
        refs[-1][index] = ref[...]


def pack(pieces):
    return pl.pallas_call(
        pack_kernel,
        in_specs=[VMEM] * len(pieces),
        out_specs=VMEM,
        out_shape=jax.ShapeDtypeStruct((len(pieces), *pieces[0].shape), pieces[0].dtype),
        compiler_params=limits(6),
        cost_estimate=cost(10**5, 10**6),
        name="pack",
    )(*pieces)


def expert_kernel(coef_ref, *refs, scale):
    sums, out_ref, summed = refs[:-2], refs[-2], refs[-1]
    owned = out_ref.shape[0]
    place = lax.axis_index("gx")
    row = lax.broadcasted_iota(jnp.int32, (owned, coef_ref.shape[1]), 0)
    col = lax.broadcasted_iota(jnp.int32, (owned, coef_ref.shape[1]), 1)
    chosen = col == row + place * owned
    picked = [
        jnp.sum(jnp.where(chosen, coef_ref[k : k + 1, :], 0.0), axis=1, keepdims=True) * scale for k in range(2)
    ]
    even = lax.rem(place, 2) == 0
    first = jnp.broadcast_to(jnp.where(even, picked[0], picked[1]), (owned, 128))
    second = jnp.broadcast_to(jnp.where(even, picked[1], picked[0]), (owned, 128))
    half = len(sums) // 2
    for side in range(2):
        total = sums[side * half][...].astype(F32)
        for ref in sums[side * half + 1 : (side + 1) * half]:
            total += ref[...].astype(F32)
        summed[side] = total
    for row in range(summed.shape[1]):
        out_ref[:, row * 128 : (row + 1) * 128] = (
            first * summed[0, row : row + 1, :] + second * summed[1, row : row + 1, :]
        )


def expert_product(coef, sums, owned, scale):
    rows = sums[0].shape[0]
    return pl.pallas_call(
        functools.partial(expert_kernel, scale=scale),
        in_specs=[VMEM] * (1 + len(sums)),
        out_specs=VMEM,
        out_shape=jax.ShapeDtypeStruct((owned, rows * 128), F32),
        scratch_shapes=[pltpu.VMEM((2, rows, 128), F32)],
        compiler_params=limits(8),
        cost_estimate=cost(10**6, 4 * 10**6),
        name="expert_product",
    )(coef, *sums)


def finish_kernel(send_ref, own_ref, a_ref, b_ref, c_ref, d_ref, out_ref):
    atoms = own_ref.shape[1]
    face = send_ref.shape[1]
    row = lax.broadcasted_iota(jnp.int32, (atoms, face), 0)
    picks = []
    for side in range(2):
        even = lax.rem(lax.axis_index(("gx", "yz")[side]), 2) == 0
        below, above = send_ref[2 * side : 2 * side + 1, :], send_ref[2 * side + 1 : 2 * side + 2, :]
        for faces in (jnp.where(even, above, below), jnp.where(even, below, above)):
            picks.append((row == faces).astype(F32).astype(BF16))
    picks = [picks[3], picks[1], picks[2], picks[0]]
    for c in range(9):
        total = own_ref[c]
        for pick, ref in zip(picks, (a_ref, b_ref, c_ref, d_ref)):
            total += nn(pick, ref[c])
        out_ref[c] = total.astype(BF16)


def finish(send, own, returned):
    return pl.pallas_call(
        finish_kernel,
        in_specs=[VMEM] * 6,
        out_specs=VMEM,
        out_shape=jax.ShapeDtypeStruct(own.shape, BF16),
        compiler_params=limits(6),
        cost_estimate=cost(10**8, 2 * 10**6),
        name="finish",
    )(send, own, *returned)


def swap(value, axis, bit):
    return lax.ppermute(value, axis, [(i, i ^ bit) for i in range(lax.axis_size(axis))])


def neighbour_pairs(value, axis, first):
    count = lax.axis_size(axis)
    moves = []
    for low in range(first, count, 2):
        high = (low + 1) % count
        moves += [(low, high), (high, low)]
    return lax.ppermute(value, axis, moves)


def local(
    saved_input, cotangent, neighbours, rot_zero, rot_one, rot_two, send_index, atom_class, live_blocks,
    merge_coef, experts,
):
    atoms, fanout = neighbours.shape
    slots = saved_input.shape[0]
    channels = cotangent.shape[2]
    face = send_index.shape[1]
    count_yz, count_gx = lax.axis_size("yz"), lax.axis_size("gx")
    row, column = lax.axis_index("yz"), lax.axis_index("gx")
    core = column % 2
    height = experts.shape[1] // 128
    rows = height * count_yz
    direct = height % 32 == 0 and count_yz & (count_yz - 1) == 0 and count_gx == 4

    zero = rot_zero.reshape(1, -1)
    source = jnp.transpose(saved_input, (1, 0, 2))
    target = jnp.transpose(cotangent, (1, 0, 2))

    if direct:
        half = height // 2
        mine = merge(merge_coef, experts, 2)
        held = [mine] + [swap(mine, "yz", k) for k in range(1, count_yz)]
        source, target, mine = lax.optimization_barrier((source, target, mine))

        def places():
            here, side = lax.axis_index("yz"), lax.rem(lax.axis_index("gx"), 2)
            starts = [(here ^ k) * height for k in range(count_yz)]
            return [at + side * half for at in starts] + [at + (1 - side) * half for at in starts]
    else:
        part = jnp.dot(merge_coef, experts.astype(F32), precision=lax.Precision.HIGHEST).astype(BF16)
        merged = lax.all_gather(part, "yz", axis=1, tiled=True)
        pieces = [merged.reshape(1, merged.shape[0], rows, 128)]

        def places():
            return [0]

    other, own, pulled, edge = features(
        live_blocks, neighbours.T, atom_class.reshape(1, -1), zero, rot_one, rot_two, source, target, rows, fanout
    )
    if direct:
        other, *held = lax.optimization_barrier((other, *held))
        came = swap(other, "gx", 1)
        parts = pair_sum(own, came, count_yz)
        gathered = [parts[0]] + [swap(parts[k], "yz", k) for k in reversed(range(1, count_yz))]
        held = pack(held)
        pieces = [held, swap(held, "gx", 1)]
    grad_own, *ghosts = back(edge, zero, rot_one, rot_two, pulled, pieces, places, rows, atoms, slots, face)
    returned = [
        neighbour_pairs(ghost, axis, first)
        for ghost, axis, first in zip(ghosts, ("yz", "gx", "yz", "gx"), (1, 1, 0, 0))
    ]
    if direct:
        grad_own, *gathered = lax.optimization_barrier((grad_own, *gathered))
        summed, *returned = lax.optimization_barrier((total_sum(gathered), *returned))
        across = swap(summed, "gx", 2)
        input_grad = finish(send_index, grad_own, returned)
        across, input_grad = lax.optimization_barrier((across, input_grad))
        sums = [summed, across, swap(summed, "gx", 1), swap(across, "gx", 1)]
    else:
        mixed = jnp.stack([own, other]).astype(F32)
        mixed = jnp.where(core == 0, mixed, mixed[::-1])
        whole = lax.psum(mixed, ("yz", "gx"))
        piece = lax.dynamic_slice_in_dim(whole, row * height, height, 1)
        piece = jnp.where(core == 0, piece, piece[::-1])
        sums = [piece[0], piece[1]]
        input_grad = finish(send_index, grad_own, returned)
    grad_scale = math.sqrt(fanout / (atoms * count_yz * count_gx))
    expert_grad = expert_product(merge_coef, sums, merge_coef.shape[1] // count_gx, grad_scale)
    return (jnp.transpose(input_grad, (1, 0, 2)), expert_grad)


def solution(mesh):
    tiles = ("rep", "yz", "gx")
    in_specs = (
        P(tiles, None, None),
        P(tiles, None, None),
        P(tiles, None),
        P(tiles),
        P(None, None, tiles),
        P(None, None, tiles),
        P(tiles, None),
        P(tiles),
        P(tiles),
        P(),
        P(None, "yz"),
    )
    out_specs = (P(tiles, None, None), P(("rep", "gx"), "yz"))
    return jax.shard_map(local, mesh=mesh, in_specs=in_specs, out_specs=out_specs, check_vma=False)
```

```python
import functools
import math

import jax
import jax.numpy as jnp
from jax import lax
from jax.experimental import pallas as pl
from jax.experimental.pallas import tpu as pltpu
from jax.sharding import PartitionSpec as P

LIVE_BLOCK = 64
CHUNK = 256
SUB = 16
F32 = jnp.float32
BF16 = jnp.bfloat16

STACK = (0, 2, 6, 3, 7, 1, 5)
SLOT = {component: place for place, component in enumerate(STACK)}

VMEM = pl.BlockSpec(memory_space=pltpu.VMEM)
SMEM = pl.BlockSpec(memory_space=pltpu.SMEM)
HBM = pl.BlockSpec(memory_space=pltpu.HBM)


def limits(mebibytes):
    return pltpu.CompilerParams(vmem_limit_bytes=mebibytes * 1024 * 1024)


def cost(flops, moved):
    return pl.CostEstimate(flops=flops, bytes_accessed=moved, transcendentals=0)


def nn(left, right):
    return lax.dot_general(left, right, (((1,), (0,)), ((), ())), preferred_element_type=F32)


def nt(left, right):
    return lax.dot_general(left, right, (((1,), (1,)), ((), ())), preferred_element_type=F32)


def split3(value):
    high = value.astype(BF16)
    rest = value - high.astype(F32)
    middle = rest.astype(BF16)
    low = (rest - middle.astype(F32)).astype(BF16)
    return high, middle, low


def merge_kernel(coef_in_ref, experts_ref, out_ref, held, coef_ref, arrived, coef_arrived):
    members, experts = coef_in_ref.shape
    rows = out_ref.shape[1]
    start = pl.multiple_of(lax.rem(lax.axis_index("gx"), 2) * rows * 128, 128)
    stripes = arrived.shape[0]
    blocks = rows // 16
    edges = [blocks * stripe // stripes for stripe in range(stripes + 1)]
    copies = []
    for stripe in range(stripes):
        at, wide = edges[stripe] * 2048, (edges[stripe + 1] - edges[stripe]) * 2048
        copies.append(
            pltpu.make_async_copy(
                experts_ref.at[:, pl.ds(start + at, wide)], held.at[:, pl.ds(at, wide)], arrived.at[stripe]
            )
        )
        copies[-1].start()
    coef_copy = pltpu.make_async_copy(coef_in_ref, coef_ref, coef_arrived)
    coef_copy.start()
    coef_copy.wait()
    wide = 8 * experts
    row = lax.broadcasted_iota(jnp.int32, (8, wide), 0)
    col = lax.broadcasted_iota(jnp.int32, (8, wide), 1)
    diagonal = row == col // experts
    source = lax.broadcasted_iota(jnp.int32, (experts, wide), 0)
    target = lax.broadcasted_iota(jnp.int32, (experts, wide), 1)
    tile = (source == target % experts).astype(F32).astype(BF16)
    lefts = []
    for term in split3(coef_ref[...]):
        tiled = nn(term, tile)
        for member in range(members):
            lefts.append(jnp.where(diagonal, tiled[member : member + 1, :], 0.0).astype(BF16))
    lefts = jnp.concatenate(lefts, axis=0)
    height = 8 * members
    for block in range(blocks):
        if block in edges:
            copies[edges.index(block)].wait()
        halves = []
        for half in range(2):
            first = block * 16 + half * 8
            groups = [held[:, (first + g) * 128 : (first + g + 1) * 128] for g in range(8)]
            halves.append(jnp.concatenate(groups, axis=0))
        product = nn(lefts, jnp.concatenate(halves, axis=1))
        total = product[:height] + product[height : 2 * height] + product[2 * height :]
        for member in range(members):
            part = total[member * 8 : member * 8 + 8]
            out_ref[member, block * 16 : block * 16 + 16, :] = jnp.concatenate(
                [part[:, :128], part[:, 128:]], axis=0
            ).astype(BF16)


def merge(coef, experts, parts):
    members, count = coef.shape
    columns = experts.shape[1] // parts
    rows = columns // 128
    return pl.pallas_call(
        merge_kernel,
        in_specs=[HBM, HBM],
        out_specs=VMEM,
        out_shape=jax.ShapeDtypeStruct((members, rows, 128), BF16),
        scratch_shapes=[
            pltpu.VMEM((count, columns), BF16),
            pltpu.VMEM((members, count), F32),
            pltpu.SemaphoreType.DMA((2,)),
            pltpu.SemaphoreType.DMA,
        ],
        compiler_params=limits(52),
        cost_estimate=cost(96 * 16 * columns, 2 * count * columns),
        name="merge",
    )(coef, experts)


def features_kernel(
    live_ref, near_ref, class_ref, zero_ref, one_ref, two_ref, source_ref, target_ref,
    rotated, pulled_ref, edge_ref,
    source_t, target_t, moved, spread,
    *, fanout,
):
    slots, channels = source_ref.shape[1:]
    atoms = target_ref.shape[1]
    edges = atoms * fanout
    for c in range(9):
        source_t[c * channels : (c + 1) * channels, :] = source_ref[c].T
        target_t[c * channels : (c + 1) * channels, :] = target_ref[c].T
    near = near_ref[...].astype(F32).astype(BF16)
    classes = class_ref[...].astype(F32).astype(BF16)
    live_edges = live_ref[0] * LIVE_BLOCK * fanout
    scale = 1.0 / math.sqrt(fanout)

    def chunk_step(chunk, carry):
        start = pl.multiple_of(chunk * CHUNK, CHUNK)
        here = pl.ds(start, CHUNK)
        edge = lax.broadcasted_iota(jnp.int32, (atoms, CHUNK), 1) + start
        atom = lax.broadcasted_iota(jnp.int32, (atoms, CHUNK), 0)
        repeat = (edge // fanout == atom).astype(F32).astype(BF16)
        edge8 = lax.broadcasted_iota(jnp.int32, (fanout, CHUNK), 1) + start
        lane8 = lax.broadcasted_iota(jnp.int32, (fanout, CHUNK), 0)
        picked = jnp.where(edge8 % fanout == lane8, nn(near, repeat), 0.0)
        near_row = jnp.sum(picked, axis=0, keepdims=True)
        class_row = nn(classes, repeat)
        edge_ref[0:1, here] = near_row
        edge_ref[1:2, here] = jnp.where(edge8[0:1] < live_edges, class_row, -1.0)
        slot = lax.broadcasted_iota(jnp.int32, (slots, CHUNK), 0).astype(F32)
        pick = (slot == near_row).astype(F32).astype(BF16)
        moved[...] = nn(source_t[...], pick)
        spread[...] = nn(target_t[...], repeat)

        def sub_step(sub, inner):
            at = pl.multiple_of(sub * SUB, SUB)

            def turn(field, write):
                def part(c):
                    return field[pl.ds(c * channels + at, SUB), :]

                write(0, zero_ref[0:1, here] * part(0))
                values = [part(c) for c in (1, 2, 3)]
                for a in range(3):
                    total = one_ref[a, 0:1, here] * values[0]
                    for b in range(1, 3):
                        total += one_ref[a, b : b + 1, here] * values[b]
                    write(1 + a, total)
                values = [part(c) for c in (4, 5, 6, 7, 8)]
                for a in range(1, 4):
                    total = two_ref[a, 0:1, here] * values[0]
                    for b in range(1, 5):
                        total += two_ref[a, b : b + 1, here] * values[b]
                    write(4 + a, total)

            def write_rotated(c, value):
                rotated[pl.ds(SLOT[c] * channels + at, SUB), here] = value.astype(BF16)

            def write_pulled(c, value):
                pulled_ref[pl.ds(SLOT[c] * channels + at, SUB), here] = (value * scale).astype(BF16)

            turn(moved, write_rotated)
            turn(spread, write_pulled)
            return inner

        lax.fori_loop(0, channels // SUB, sub_step, 0)
        return carry

    lax.fori_loop(0, edges // CHUNK, chunk_step, 0)


def class_grad_kernel(rotated, pulled_ref, edge_ref, other_ref, own_ref, grads):
    channels = rotated.shape[0] // 7
    zw, pw = 3 * channels, 2 * channels
    first = zw * zw // 128
    second = first + pw * pw // 128
    own = lax.rem(lax.axis_index("gx"), 2).astype(F32)
    for out_ref, wanted in ((other_ref, 1.0 - own), (own_ref, own)):
        mask = (edge_ref[1:2, :] == wanted).astype(F32).astype(BF16)
        qz = pulled_ref[0:zw, :] * mask
        qp = pulled_ref[zw : zw + pw, :] * mask
        qn = pulled_ref[zw + pw : zw + 2 * pw, :] * mask
        z, p, n = rotated[0:zw, :], rotated[zw : zw + pw, :], rotated[zw + pw : zw + 2 * pw, :]
        whole = nt(z, qz)
        for j in range(zw // 128):
            grads[pl.ds(j, zw, stride=zw // 128), :] = whole[:, j * 128 : (j + 1) * 128]
        coupled = nt(p, qp) + nt(n, qn)
        crossed = nt(p, qn) - nt(n, qp)
        for j in range(pw // 128):
            grads[pl.ds(first + j, pw, stride=pw // 128), :] = coupled[:, j * 128 : (j + 1) * 128]
            grads[pl.ds(second + j, pw, stride=pw // 128), :] = crossed[:, j * 128 : (j + 1) * 128]
        out_ref[...] = grads[...].astype(BF16)


def features(live, near, classes, zero, one, two, source, target, fanout):
    slots, channels = source.shape[1:]
    atoms = target.shape[1]
    edges = atoms * fanout
    shape = jax.ShapeDtypeStruct
    return pl.pallas_call(
        functools.partial(features_kernel, fanout=fanout),
        in_specs=[SMEM] + [VMEM] * 7,
        out_specs=[VMEM] * 3,
        out_shape=[
            shape((7 * channels, edges), BF16),
            shape((7 * channels, edges), BF16),
            shape((8, edges), F32),
        ],
        scratch_shapes=[
            pltpu.VMEM((9 * channels, slots), BF16),
            pltpu.VMEM((9 * channels, atoms), BF16),
            pltpu.VMEM((9 * channels, CHUNK), F32),
            pltpu.VMEM((9 * channels, CHUNK), F32),
        ],
        compiler_params=limits(16),
        cost_estimate=cost(6 * 10**9, 7 * 10**6),
        name="features",
    )(live, near, classes, zero, one, two, source, target)


def class_grads(rotated, pulled, edge, rows):
    shape = jax.ShapeDtypeStruct((rows, 128), BF16)
    return pl.pallas_call(
        class_grad_kernel,
        in_specs=[VMEM] * 3,
        out_specs=[VMEM] * 2,
        out_shape=[shape, shape],
        scratch_shapes=[pltpu.VMEM((rows, 128), F32)],
        compiler_params=limits(16),
        cost_estimate=cost(4 * 10**9, 6 * 10**6),
        name="class_grads",
    )(rotated, pulled, edge)


def back_kernel(
    edge_ref, zero_ref, one_ref, two_ref, pulled_ref, *rest, pieces, members, atoms, face, places,
):
    piece_refs = rest[:pieces]
    own_ref, *ghost_refs = rest[pieces : pieces + 5]
    flat, weight_zero, weight_pair, field, turned, pick_all = rest[pieces + 5 :]
    rows = flat.shape[1]
    channels = own_ref.shape[2]
    slots = pick_all.shape[0]
    edges = pulled_ref.shape[1]
    zw, pw = 3 * channels, 2 * channels
    first = zw * zw // 128
    second = first + pw * pw // 128
    placed = [(piece, index) for piece in piece_refs for index in range(piece.shape[0])]
    for (piece, index), place in zip(placed, places()):
        height = piece.shape[2]
        at = pl.ds(pl.multiple_of(place, 16), height)
        for k in range(members):
            flat[k, at, :] = piece[index, k].astype(F32)
    for k in range(members):
        for j in range(zw // 128):
            weight_zero[:, k * zw + j * 128 : k * zw + (j + 1) * 128] = flat[
                k, pl.ds(j, zw, stride=zw // 128), :
            ].astype(BF16)
        for j in range(pw // 128):
            at = k * 2 * pw + j * 128
            weight_pair[:, at : at + 128] = flat[k, pl.ds(first + j, pw, stride=pw // 128), :].astype(BF16)
            weight_pair[:, at + pw : at + pw + 128] = flat[
                k, pl.ds(second + j, pw, stride=pw // 128), :
            ].astype(BF16)

    def chunk_step(chunk, carry):
        start = pl.multiple_of(chunk * CHUNK, CHUNK)
        here = pl.ds(start, CHUNK)
        slot = lax.broadcasted_iota(jnp.int32, (slots, CHUNK), 0).astype(F32)
        pick_all[:, here] = (slot == edge_ref[0:1, here]).astype(F32).astype(BF16)
        qz, qpn, qnp = [], [], []
        for k in range(members):
            mask = (edge_ref[1:2, here] == float(k)).astype(F32).astype(BF16)
            qz.append(pulled_ref[0:zw, here] * mask)
            qp = pulled_ref[zw : zw + pw, here] * mask
            qn = pulled_ref[zw + pw : zw + 2 * pw, here] * mask
            qpn += [qp, qn]
            qnp += [qn, -qp]
        field[0:zw, :] = nn(weight_zero[...], jnp.concatenate(qz, axis=0))
        field[zw : zw + pw, :] = nn(weight_pair[...], jnp.concatenate(qpn, axis=0))
        field[zw + pw : zw + 2 * pw, :] = nn(weight_pair[...], jnp.concatenate(qnp, axis=0))

        def sub_step(sub, inner):
            at = pl.multiple_of(sub * SUB, SUB)

            def part(c):
                return field[pl.ds(SLOT[c] * channels + at, SUB), :]

            def write(c, value):
                turned[pl.ds(c * channels + at, SUB), here] = value.astype(BF16)

            write(0, zero_ref[0:1, here] * part(0))
            values = [part(c) for c in (1, 2, 3)]
            for b in range(3):
                total = one_ref[0, b : b + 1, here] * values[0]
                for a in range(1, 3):
                    total += one_ref[a, b : b + 1, here] * values[a]
                write(1 + b, total)
            values = [part(c) for c in (5, 6, 7)]
            for b in range(5):
                total = two_ref[1, b : b + 1, here] * values[0]
                for a in range(2, 4):
                    total += two_ref[a, b : b + 1, here] * values[a - 1]
                write(4 + b, total)
            return inner

        lax.fori_loop(0, channels // SUB, sub_step, 0)
        return carry

    lax.fori_loop(0, edges // CHUNK, chunk_step, 0)
    for c in range(9):
        summed = nt(pick_all[...], turned[c * channels : (c + 1) * channels, :])
        own_ref[c] = summed[:atoms]
        blocks = [summed[atoms + block * face : atoms + (block + 1) * face] for block in range(4)]
        for side in range(2):
            even = lax.rem(lax.axis_index(("gx", "yz")[side]), 2) == 0
            low, high = blocks[2 * side], blocks[2 * side + 1]
            ghost_refs[3 - side][c] = jnp.where(even, high, low).astype(BF16)
            ghost_refs[1 - side][c] = jnp.where(even, low, high).astype(BF16)


def back(edge, zero, one, two, pulled, pieces, places, rows, atoms, slots, face):
    members = pieces[0].shape[1]
    edges = pulled.shape[1]
    channels = pulled.shape[0] // 7
    shape = jax.ShapeDtypeStruct
    return pl.pallas_call(
        functools.partial(
            back_kernel, pieces=len(pieces), members=members, atoms=atoms, face=face, places=places
        ),
        in_specs=[VMEM] * (5 + len(pieces)),
        out_specs=[VMEM] * 5,
        out_shape=[shape((9, atoms, channels), F32), *[shape((9, face, channels), BF16)] * 4],
        scratch_shapes=[
            pltpu.VMEM((members, rows, 128), F32),
            pltpu.VMEM((3 * channels, members * 3 * channels), BF16),
            pltpu.VMEM((2 * channels, members * 4 * channels), BF16),
            pltpu.VMEM((7 * channels, CHUNK), F32),
            pltpu.VMEM((9 * channels, edges), BF16),
            pltpu.VMEM((slots, edges), BF16),
        ],
        compiler_params=limits(24),
        cost_estimate=cost(9 * 10**9, 7 * 10**6),
        name="back",
    )(edge, zero, one, two, pulled, *pieces)


def core_kernel(own_ref, came_ref, keep_ref, far_ref, send_ref):
    height = keep_ref.shape[0]
    row = lax.axis_index("yz")
    for k in range(4):
        at = pl.ds(pl.multiple_of((row ^ k) * height, 16), height)
        total = own_ref[at, :].astype(F32) + came_ref[at, :].astype(F32)
        if k == 0:
            keep_ref[...] = total
        elif k == 2:
            far_ref[...] = total
        else:
            send_ref[k // 2] = total.astype(BF16)


def core_sum(own, came):
    height = own.shape[0] // 4
    shape = jax.ShapeDtypeStruct
    return pl.pallas_call(
        core_kernel,
        in_specs=[VMEM, VMEM],
        out_specs=[VMEM] * 3,
        out_shape=[shape((height, 128), F32), shape((height, 128), F32), shape((2, height, 128), BF16)],
        compiler_params=limits(6),
        cost_estimate=cost(10**6, 2 * 10**6),
        name="core_sum",
    )(own, came)


def near_kernel(keep_ref, far_ref, came_ref, mine_ref, send_ref):
    mine_ref[...] = keep_ref[...] + came_ref[0].astype(F32)
    send_ref[...] = (far_ref[...] + came_ref[1].astype(F32)).astype(BF16)


def near_sum(keep, far, came):
    shape = jax.ShapeDtypeStruct
    return pl.pallas_call(
        near_kernel,
        in_specs=[VMEM] * 3,
        out_specs=[VMEM] * 2,
        out_shape=[shape(keep.shape, F32), shape(keep.shape, BF16)],
        compiler_params=limits(6),
        cost_estimate=cost(10**6, 10**6),
        name="near_sum",
    )(keep, far, came)


def total_kernel(*refs):
    total = refs[0][...].astype(F32)
    for ref in refs[1:-1]:
        total += ref[...].astype(F32)
    refs[-1][...] = total.astype(BF16)


def total_sum(parts):
    return pl.pallas_call(
        total_kernel,
        in_specs=[VMEM] * len(parts),
        out_specs=VMEM,
        out_shape=jax.ShapeDtypeStruct(parts[0].shape, BF16),
        compiler_params=limits(6),
        cost_estimate=cost(10**6, 10**6),
        name="total_sum",
    )(*parts)


def pack_kernel(*refs):
    for index, ref in enumerate(refs[:-1]):
        refs[-1][index] = ref[...]


def pack(pieces):
    return pl.pallas_call(
        pack_kernel,
        in_specs=[VMEM] * len(pieces),
        out_specs=VMEM,
        out_shape=jax.ShapeDtypeStruct((len(pieces), *pieces[0].shape), pieces[0].dtype),
        compiler_params=limits(6),
        cost_estimate=cost(10**5, 10**6),
        name="pack",
    )(*pieces)


def expert_kernel(coef_ref, *refs, scale):
    sums, out_ref, summed = refs[:-2], refs[-2], refs[-1]
    owned = out_ref.shape[0]
    place = lax.axis_index("gx")
    row = lax.broadcasted_iota(jnp.int32, (owned, coef_ref.shape[1]), 0)
    col = lax.broadcasted_iota(jnp.int32, (owned, coef_ref.shape[1]), 1)
    chosen = col == row + place * owned
    picked = [
        jnp.sum(jnp.where(chosen, coef_ref[k : k + 1, :], 0.0), axis=1, keepdims=True) * scale for k in range(2)
    ]
    even = lax.rem(place, 2) == 0
    first = jnp.broadcast_to(jnp.where(even, picked[0], picked[1]), (owned, 128))
    second = jnp.broadcast_to(jnp.where(even, picked[1], picked[0]), (owned, 128))
    half = len(sums) // 2
    for side in range(2):
        total = sums[side * half][...].astype(F32)
        for ref in sums[side * half + 1 : (side + 1) * half]:
            total += ref[...].astype(F32)
        summed[side] = total
    for row in range(summed.shape[1]):
        out_ref[:, row * 128 : (row + 1) * 128] = (
            first * summed[0, row : row + 1, :] + second * summed[1, row : row + 1, :]
        )


def expert_product(coef, sums, owned, scale):
    rows = sums[0].shape[0]
    return pl.pallas_call(
        functools.partial(expert_kernel, scale=scale),
        in_specs=[VMEM] * (1 + len(sums)),
        out_specs=VMEM,
        out_shape=jax.ShapeDtypeStruct((owned, rows * 128), F32),
        scratch_shapes=[pltpu.VMEM((2, rows, 128), F32)],
        compiler_params=limits(8),
        cost_estimate=cost(10**6, 4 * 10**6),
        name="expert_product",
    )(coef, *sums)


def finish_kernel(send_ref, own_ref, a_ref, b_ref, c_ref, d_ref, out_ref):
    atoms = own_ref.shape[1]
    face = send_ref.shape[1]
    row = lax.broadcasted_iota(jnp.int32, (atoms, face), 0)
    picks = []
    for side in range(2):
        even = lax.rem(lax.axis_index(("gx", "yz")[side]), 2) == 0
        below, above = send_ref[2 * side : 2 * side + 1, :], send_ref[2 * side + 1 : 2 * side + 2, :]
        for faces in (jnp.where(even, above, below), jnp.where(even, below, above)):
            picks.append((row == faces).astype(F32).astype(BF16))
    picks = [picks[3], picks[1], picks[2], picks[0]]
    for c in range(9):
        total = own_ref[c]
        for pick, ref in zip(picks, (a_ref, b_ref, c_ref, d_ref)):
            total += nn(pick, ref[c])
        out_ref[c] = total.astype(BF16)


def finish(send, own, returned):
    return pl.pallas_call(
        finish_kernel,
        in_specs=[VMEM] * 6,
        out_specs=VMEM,
        out_shape=jax.ShapeDtypeStruct(own.shape, BF16),
        compiler_params=limits(6),
        cost_estimate=cost(10**8, 2 * 10**6),
        name="finish",
    )(send, own, *returned)


def swap(value, axis, bit):
    return lax.ppermute(value, axis, [(i, i ^ bit) for i in range(lax.axis_size(axis))])


def neighbour_pairs(value, axis, first):
    count = lax.axis_size(axis)
    moves = []
    for low in range(first, count, 2):
        high = (low + 1) % count
        moves += [(low, high), (high, low)]
    return lax.ppermute(value, axis, moves)


def local(
    saved_input, cotangent, neighbours, rot_zero, rot_one, rot_two, send_index, atom_class, live_blocks,
    merge_coef, experts,
):
    atoms, fanout = neighbours.shape
    slots = saved_input.shape[0]
    channels = cotangent.shape[2]
    face = send_index.shape[1]
    count_yz, count_gx = lax.axis_size("yz"), lax.axis_size("gx")
    row, column = lax.axis_index("yz"), lax.axis_index("gx")
    core = column % 2
    height = experts.shape[1] // 128
    rows = height * count_yz
    direct = height % 32 == 0 and count_yz == 4 and count_gx == 4

    zero = rot_zero.reshape(1, -1)
    source = jnp.transpose(saved_input, (1, 0, 2))
    target = jnp.transpose(cotangent, (1, 0, 2))

    if direct:
        half = height // 2
        mine = merge(merge_coef, experts, 2)
        far = swap(mine, "yz", 2)
        near = swap(mine, "yz", 1)
        source, target, mine = lax.optimization_barrier((source, target, mine))

        def places():
            here, side = lax.axis_index("yz"), lax.rem(lax.axis_index("gx"), 2)
            starts = [(here ^ k) * height for k in range(4)]
            return [at + side * half for at in starts] + [at + (1 - side) * half for at in starts]
    else:
        part = jnp.dot(merge_coef, experts.astype(F32), precision=lax.Precision.HIGHEST).astype(BF16)
        merged = lax.all_gather(part, "yz", axis=1, tiled=True)
        pieces = [merged.reshape(1, merged.shape[0], rows, 128)]

        def places():
            return [0]

    rotated, pulled, edge = features(
        live_blocks, neighbours.T, atom_class.reshape(1, -1), zero, rot_one, rot_two, source, target, fanout
    )
    if direct:
        rotated, far, near = lax.optimization_barrier((rotated, far, near))
        passed = swap(far, "yz", 1)
    other, own = class_grads(rotated, pulled, edge, rows)
    if direct:
        other, passed = lax.optimization_barrier((other, passed))
        came = swap(other, "gx", 1)
        held = pack([mine, near, far, passed])
        pieces = [held, swap(held, "gx", 1)]
        keep, beyond, away = core_sum(own, came)
        arrived = swap(away, "yz", 1)
    grad_own, *ghosts = back(edge, zero, rot_one, rot_two, pulled, pieces, places, rows, atoms, slots, face)
    returned = [
        neighbour_pairs(ghost, axis, first)
        for ghost, axis, first in zip(ghosts, ("yz", "gx", "yz", "gx"), (1, 1, 0, 0))
    ]
    if direct:
        grad_own, keep, beyond, arrived = lax.optimization_barrier((grad_own, keep, beyond, arrived))
        partial, away = near_sum(keep, beyond, arrived)
        gathered = [partial, swap(away, "yz", 2)]
        summed, *returned = lax.optimization_barrier((total_sum(gathered), *returned))
        across = swap(summed, "gx", 2)
        input_grad = finish(send_index, grad_own, returned)
        across, input_grad = lax.optimization_barrier((across, input_grad))
        sums = [summed, across, swap(summed, "gx", 1), swap(across, "gx", 1)]
    else:
        mixed = jnp.stack([own, other]).astype(F32)
        mixed = jnp.where(core == 0, mixed, mixed[::-1])
        whole = lax.psum(mixed, ("yz", "gx"))
        piece = lax.dynamic_slice_in_dim(whole, row * height, height, 1)
        piece = jnp.where(core == 0, piece, piece[::-1])
        sums = [piece[0], piece[1]]
        input_grad = finish(send_index, grad_own, returned)
    grad_scale = math.sqrt(fanout / (atoms * count_yz * count_gx))
    expert_grad = expert_product(merge_coef, sums, merge_coef.shape[1] // count_gx, grad_scale)
    return (jnp.transpose(input_grad, (1, 0, 2)), expert_grad)


def solution(mesh):
    tiles = ("rep", "yz", "gx")
    in_specs = (
        P(tiles, None, None),
        P(tiles, None, None),
        P(tiles, None),
        P(tiles),
        P(None, None, tiles),
        P(None, None, tiles),
        P(tiles, None),
        P(tiles),
        P(tiles),
        P(),
        P(None, "yz"),
    )
    out_specs = (P(tiles, None, None), P(("rep", "gx"), "yz"))
    return jax.shard_map(local, mesh=mesh, in_specs=in_specs, out_specs=out_specs, check_vma=False)
```

```python
import functools
import math

import jax
import jax.numpy as jnp
from jax import lax
from jax.experimental import pallas as pl
from jax.experimental.pallas import tpu as pltpu
from jax.sharding import PartitionSpec as P

LIVE_BLOCK = 64
CHUNK = 256
SUB = 16
F32 = jnp.float32
BF16 = jnp.bfloat16

STACK = (0, 2, 6, 3, 7, 1, 5)
SLOT = {component: place for place, component in enumerate(STACK)}

VMEM = pl.BlockSpec(memory_space=pltpu.VMEM)
HBM = pl.BlockSpec(memory_space=pltpu.HBM)


def limits(mebibytes):
    return pltpu.CompilerParams(vmem_limit_bytes=mebibytes * 1024 * 1024)


def cost(flops, moved):
    return pl.CostEstimate(flops=flops, bytes_accessed=moved, transcendentals=0)


def nn(left, right):
    return lax.dot_general(left, right, (((1,), (0,)), ((), ())), preferred_element_type=F32)


def nt(left, right):
    return lax.dot_general(left, right, (((1,), (1,)), ((), ())), preferred_element_type=F32)


def split3(value):
    high = value.astype(BF16)
    rest = value - high.astype(F32)
    middle = rest.astype(BF16)
    low = (rest - middle.astype(F32)).astype(BF16)
    return high, middle, low


def merge_kernel(coef_in_ref, experts_ref, out_ref, held, coef_ref, arrived, coef_arrived):
    members, experts = coef_in_ref.shape
    rows = out_ref.shape[1]
    start = pl.multiple_of(lax.rem(lax.axis_index("gx"), 2) * rows * 128, 128)
    stripes = arrived.shape[0]
    blocks = rows // 16
    edges = [blocks * stripe // stripes for stripe in range(stripes + 1)]
    copies = []
    for stripe in range(stripes):
        at, wide = edges[stripe] * 2048, (edges[stripe + 1] - edges[stripe]) * 2048
        copies.append(
            pltpu.make_async_copy(
                experts_ref.at[:, pl.ds(start + at, wide)], held.at[:, pl.ds(at, wide)], arrived.at[stripe]
            )
        )
        copies[-1].start()
    coef_copy = pltpu.make_async_copy(coef_in_ref, coef_ref, coef_arrived)
    coef_copy.start()
    coef_copy.wait()
    wide = 8 * experts
    row = lax.broadcasted_iota(jnp.int32, (8, wide), 0)
    col = lax.broadcasted_iota(jnp.int32, (8, wide), 1)
    diagonal = row == col // experts
    source = lax.broadcasted_iota(jnp.int32, (experts, wide), 0)
    target = lax.broadcasted_iota(jnp.int32, (experts, wide), 1)
    tile = (source == target % experts).astype(F32).astype(BF16)
    lefts = []
    for term in split3(coef_ref[...]):
        tiled = nn(term, tile)
        for member in range(members):
            lefts.append(jnp.where(diagonal, tiled[member : member + 1, :], 0.0).astype(BF16))
    lefts = jnp.concatenate(lefts, axis=0)
    height = 8 * members
    for block in range(blocks):
        if block in edges:
            copies[edges.index(block)].wait()
        halves = []
        for half in range(2):
            first = block * 16 + half * 8
            groups = [held[:, (first + g) * 128 : (first + g + 1) * 128] for g in range(8)]
            halves.append(jnp.concatenate(groups, axis=0))
        product = nn(lefts, jnp.concatenate(halves, axis=1))
        total = product[:height] + product[height : 2 * height] + product[2 * height :]
        for member in range(members):
            part = total[member * 8 : member * 8 + 8]
            out_ref[member, block * 16 : block * 16 + 16, :] = jnp.concatenate(
                [part[:, :128], part[:, 128:]], axis=0
            ).astype(BF16)


def merge(coef, experts, parts):
    members, count = coef.shape
    columns = experts.shape[1] // parts
    rows = columns // 128
    return pl.pallas_call(
        merge_kernel,
        in_specs=[HBM, HBM],
        out_specs=VMEM,
        out_shape=jax.ShapeDtypeStruct((members, rows, 128), BF16),
        scratch_shapes=[
            pltpu.VMEM((count, columns), BF16),
            pltpu.VMEM((members, count), F32),
            pltpu.SemaphoreType.DMA((2,)),
            pltpu.SemaphoreType.DMA,
        ],
        compiler_params=limits(52),
        cost_estimate=cost(96 * 16 * columns, 2 * count * columns),
        name="merge",
    )(coef, experts)


def features_kernel(
    live_in_ref, near_ref, class_ref, zero_ref, one_ref, two_ref, source_ref, target_ref,
    other_ref, own_ref, pulled_ref, edge_ref,
    source_t, target_t, moved, spread, rotated, grads, live_ref, live_arrived,
    *, fanout,
):
    slots, channels = source_ref.shape[1:]
    atoms = target_ref.shape[1]
    edges = atoms * fanout
    live_copy = pltpu.make_async_copy(live_in_ref, live_ref, live_arrived)
    live_copy.start()
    for c in range(9):
        source_t[c * channels : (c + 1) * channels, :] = source_ref[c].T
        target_t[c * channels : (c + 1) * channels, :] = target_ref[c].T
    near = near_ref[...].astype(F32).astype(BF16)
    classes = class_ref[...].astype(F32).astype(BF16)
    live_copy.wait()
    live_edges = live_ref[0] * LIVE_BLOCK * fanout
    scale = 1.0 / math.sqrt(fanout)

    def chunk_step(chunk, carry):
        start = pl.multiple_of(chunk * CHUNK, CHUNK)
        here = pl.ds(start, CHUNK)
        edge = lax.broadcasted_iota(jnp.int32, (atoms, CHUNK), 1) + start
        atom = lax.broadcasted_iota(jnp.int32, (atoms, CHUNK), 0)
        repeat = (edge // fanout == atom).astype(F32).astype(BF16)
        edge8 = lax.broadcasted_iota(jnp.int32, (fanout, CHUNK), 1) + start
        lane8 = lax.broadcasted_iota(jnp.int32, (fanout, CHUNK), 0)
        picked = jnp.where(edge8 % fanout == lane8, nn(near, repeat), 0.0)
        near_row = jnp.sum(picked, axis=0, keepdims=True)
        class_row = nn(classes, repeat)
        edge_ref[0:1, here] = near_row
        edge_ref[1:2, here] = jnp.where(edge8[0:1] < live_edges, class_row, -1.0)
        slot = lax.broadcasted_iota(jnp.int32, (slots, CHUNK), 0).astype(F32)
        pick = (slot == near_row).astype(F32).astype(BF16)
        moved[...] = nn(source_t[...], pick)
        spread[...] = nn(target_t[...], repeat)

        def sub_step(sub, inner):
            at = pl.multiple_of(sub * SUB, SUB)

            def turn(field, write):
                def part(c):
                    return field[pl.ds(c * channels + at, SUB), :]

                write(0, zero_ref[0:1, here] * part(0))
                values = [part(c) for c in (1, 2, 3)]
                for a in range(3):
                    total = one_ref[a, 0:1, here] * values[0]
                    for b in range(1, 3):
                        total += one_ref[a, b : b + 1, here] * values[b]
                    write(1 + a, total)
                values = [part(c) for c in (4, 5, 6, 7, 8)]
                for a in range(1, 4):
                    total = two_ref[a, 0:1, here] * values[0]
                    for b in range(1, 5):
                        total += two_ref[a, b : b + 1, here] * values[b]
                    write(4 + a, total)

            def write_rotated(c, value):
                rotated[pl.ds(SLOT[c] * channels + at, SUB), here] = value.astype(BF16)

            def write_pulled(c, value):
                pulled_ref[pl.ds(SLOT[c] * channels + at, SUB), here] = (value * scale).astype(BF16)

            turn(moved, write_rotated)
            turn(spread, write_pulled)
            return inner

        lax.fori_loop(0, channels // SUB, sub_step, 0)
        return carry

    lax.fori_loop(0, edges // CHUNK, chunk_step, 0)
    zw, pw = 3 * channels, 2 * channels
    first = zw * zw // 128
    second = first + pw * pw // 128
    own = lax.rem(lax.axis_index("gx"), 2).astype(F32)
    for out_ref, wanted in ((other_ref, 1.0 - own), (own_ref, own)):
        mask = (edge_ref[1:2, :] == wanted).astype(F32).astype(BF16)
        qz = pulled_ref[0:zw, :] * mask
        qp = pulled_ref[zw : zw + pw, :] * mask
        qn = pulled_ref[zw + pw : zw + 2 * pw, :] * mask
        z, p, n = rotated[0:zw, :], rotated[zw : zw + pw, :], rotated[zw + pw : zw + 2 * pw, :]
        whole = nt(z, qz)
        for j in range(zw // 128):
            grads[pl.ds(j, zw, stride=zw // 128), :] = whole[:, j * 128 : (j + 1) * 128]
        coupled = nt(p, qp) + nt(n, qn)
        crossed = nt(p, qn) - nt(n, qp)
        for j in range(pw // 128):
            grads[pl.ds(first + j, pw, stride=pw // 128), :] = coupled[:, j * 128 : (j + 1) * 128]
            grads[pl.ds(second + j, pw, stride=pw // 128), :] = crossed[:, j * 128 : (j + 1) * 128]
        out_ref[...] = grads[...].astype(BF16)


def features(live, near, classes, zero, one, two, source, target, rows, fanout):
    slots, channels = source.shape[1:]
    atoms = target.shape[1]
    edges = atoms * fanout
    shape = jax.ShapeDtypeStruct
    return pl.pallas_call(
        functools.partial(features_kernel, fanout=fanout),
        in_specs=[HBM] + [VMEM] * 7,
        out_specs=[VMEM] * 4,
        out_shape=[
            shape((rows, 128), BF16),
            shape((rows, 128), BF16),
            shape((7 * channels, edges), BF16),
            shape((8, edges), F32),
        ],
        scratch_shapes=[
            pltpu.VMEM((9 * channels, slots), BF16),
            pltpu.VMEM((9 * channels, atoms), BF16),
            pltpu.VMEM((9 * channels, CHUNK), F32),
            pltpu.VMEM((9 * channels, CHUNK), F32),
            pltpu.VMEM((7 * channels, edges), BF16),
            pltpu.VMEM((rows, 128), F32),
            pltpu.SMEM((1,), jnp.int32),
            pltpu.SemaphoreType.DMA,
        ],
        compiler_params=limits(24),
        cost_estimate=cost(9 * 10**9, 7 * 10**6),
        name="features",
    )(live, near, classes, zero, one, two, source, target)


def back_kernel(
    edge_ref, zero_ref, one_ref, two_ref, pulled_ref, *rest, pieces, members, atoms, face, places,
):
    piece_refs = rest[:pieces]
    own_ref, *ghost_refs = rest[pieces : pieces + 5]
    flat, weight_zero, weight_pair, field, turned, pick_all = rest[pieces + 5 :]
    rows = flat.shape[1]
    channels = own_ref.shape[2]
    slots = pick_all.shape[0]
    edges = pulled_ref.shape[1]
    zw, pw = 3 * channels, 2 * channels
    first = zw * zw // 128
    second = first + pw * pw // 128
    placed = [(piece, index) for piece in piece_refs for index in range(piece.shape[0])]
    for (piece, index), place in zip(placed, places()):
        height = piece.shape[2]
        at = pl.ds(pl.multiple_of(place, 16), height)
        for k in range(members):
            flat[k, at, :] = piece[index, k].astype(F32)
    for k in range(members):
        for j in range(zw // 128):
            weight_zero[:, k * zw + j * 128 : k * zw + (j + 1) * 128] = flat[
                k, pl.ds(j, zw, stride=zw // 128), :
            ].astype(BF16)
        for j in range(pw // 128):
            at = k * 2 * pw + j * 128
            weight_pair[:, at : at + 128] = flat[k, pl.ds(first + j, pw, stride=pw // 128), :].astype(BF16)
            weight_pair[:, at + pw : at + pw + 128] = flat[
                k, pl.ds(second + j, pw, stride=pw // 128), :
            ].astype(BF16)

    def chunk_step(chunk, carry):
        start = pl.multiple_of(chunk * CHUNK, CHUNK)
        here = pl.ds(start, CHUNK)
        slot = lax.broadcasted_iota(jnp.int32, (slots, CHUNK), 0).astype(F32)
        pick_all[:, here] = (slot == edge_ref[0:1, here]).astype(F32).astype(BF16)
        qz, qpn, qnp = [], [], []
        for k in range(members):
            mask = (edge_ref[1:2, here] == float(k)).astype(F32).astype(BF16)
            qz.append(pulled_ref[0:zw, here] * mask)
            qp = pulled_ref[zw : zw + pw, here] * mask
            qn = pulled_ref[zw + pw : zw + 2 * pw, here] * mask
            qpn += [qp, qn]
            qnp += [qn, -qp]
        field[0:zw, :] = nn(weight_zero[...], jnp.concatenate(qz, axis=0))
        field[zw : zw + pw, :] = nn(weight_pair[...], jnp.concatenate(qpn, axis=0))
        field[zw + pw : zw + 2 * pw, :] = nn(weight_pair[...], jnp.concatenate(qnp, axis=0))

        def sub_step(sub, inner):
            at = pl.multiple_of(sub * SUB, SUB)

            def part(c):
                return field[pl.ds(SLOT[c] * channels + at, SUB), :]

            def write(c, value):
                turned[pl.ds(c * channels + at, SUB), here] = value.astype(BF16)

            write(0, zero_ref[0:1, here] * part(0))
            values = [part(c) for c in (1, 2, 3)]
            for b in range(3):
                total = one_ref[0, b : b + 1, here] * values[0]
                for a in range(1, 3):
                    total += one_ref[a, b : b + 1, here] * values[a]
                write(1 + b, total)
            values = [part(c) for c in (5, 6, 7)]
            for b in range(5):
                total = two_ref[1, b : b + 1, here] * values[0]
                for a in range(2, 4):
                    total += two_ref[a, b : b + 1, here] * values[a - 1]
                write(4 + b, total)
            return inner

        lax.fori_loop(0, channels // SUB, sub_step, 0)
        return carry

    lax.fori_loop(0, edges // CHUNK, chunk_step, 0)
    for c in range(9):
        summed = nt(pick_all[...], turned[c * channels : (c + 1) * channels, :])
        own_ref[c] = summed[:atoms]
        blocks = [summed[atoms + block * face : atoms + (block + 1) * face] for block in range(4)]
        for side in range(2):
            even = lax.rem(lax.axis_index(("gx", "yz")[side]), 2) == 0
            low, high = blocks[2 * side], blocks[2 * side + 1]
            ghost_refs[3 - side][c] = jnp.where(even, high, low).astype(BF16)
            ghost_refs[1 - side][c] = jnp.where(even, low, high).astype(BF16)


def back(edge, zero, one, two, pulled, pieces, places, rows, atoms, slots, face):
    members = pieces[0].shape[1]
    edges = pulled.shape[1]
    channels = pulled.shape[0] // 7
    shape = jax.ShapeDtypeStruct
    return pl.pallas_call(
        functools.partial(
            back_kernel, pieces=len(pieces), members=members, atoms=atoms, face=face, places=places
        ),
        in_specs=[VMEM] * (5 + len(pieces)),
        out_specs=[VMEM] * 5,
        out_shape=[shape((9, atoms, channels), F32), *[shape((9, face, channels), BF16)] * 4],
        scratch_shapes=[
            pltpu.VMEM((members, rows, 128), F32),
            pltpu.VMEM((3 * channels, members * 3 * channels), BF16),
            pltpu.VMEM((2 * channels, members * 4 * channels), BF16),
            pltpu.VMEM((7 * channels, CHUNK), F32),
            pltpu.VMEM((9 * channels, edges), BF16),
            pltpu.VMEM((slots, edges), BF16),
        ],
        compiler_params=limits(24),
        cost_estimate=cost(9 * 10**9, 7 * 10**6),
        name="back",
    )(edge, zero, one, two, pulled, *pieces)


def pair_kernel(own_ref, came_ref, *out_refs):
    height = out_refs[0].shape[0]
    row = lax.axis_index("yz")
    for index, out_ref in enumerate(out_refs):
        at = pl.ds(pl.multiple_of((row ^ index) * height, 16), height)
        out_ref[...] = (own_ref[at, :].astype(F32) + came_ref[at, :].astype(F32)).astype(BF16)


def pair_sum(own, came, count):
    height = own.shape[0] // count
    return pl.pallas_call(
        pair_kernel,
        in_specs=[VMEM, VMEM],
        out_specs=[VMEM] * count,
        out_shape=[jax.ShapeDtypeStruct((height, 128), BF16)] * count,
        compiler_params=limits(6),
        cost_estimate=cost(10**6, 2 * 10**6),
        name="pair_sum",
    )(own, came)


def total_kernel(*refs):
    total = refs[0][...].astype(F32)
    for ref in refs[1:-1]:
        total += ref[...].astype(F32)
    refs[-1][...] = total.astype(BF16)


def total_sum(parts):
    return pl.pallas_call(
        total_kernel,
        in_specs=[VMEM] * len(parts),
        out_specs=VMEM,
        out_shape=jax.ShapeDtypeStruct(parts[0].shape, BF16),
        compiler_params=limits(6),
        cost_estimate=cost(10**6, 10**6),
        name="total_sum",
    )(*parts)


def pack_kernel(*refs):
    for index, ref in enumerate(refs[:-1]):
        refs[-1][index] = ref[...]


def pack(pieces):
    return pl.pallas_call(
        pack_kernel,
        in_specs=[VMEM] * len(pieces),
        out_specs=VMEM,
        out_shape=jax.ShapeDtypeStruct((len(pieces), *pieces[0].shape), pieces[0].dtype),
        compiler_params=limits(6),
        cost_estimate=cost(10**5, 10**6),
        name="pack",
    )(*pieces)


def expert_kernel(coef_ref, *refs, scale):
    sums, out_ref, summed, staged, written = refs[:-4], *refs[-4:]
    owned = out_ref.shape[0]
    place = lax.axis_index("gx")
    row = lax.broadcasted_iota(jnp.int32, (owned, coef_ref.shape[1]), 0)
    col = lax.broadcasted_iota(jnp.int32, (owned, coef_ref.shape[1]), 1)
    chosen = col == row + place * owned
    picked = [
        jnp.sum(jnp.where(chosen, coef_ref[k : k + 1, :], 0.0), axis=1, keepdims=True) * scale for k in range(2)
    ]
    even = lax.rem(place, 2) == 0
    first = jnp.broadcast_to(jnp.where(even, picked[0], picked[1]), (owned, 128))
    second = jnp.broadcast_to(jnp.where(even, picked[1], picked[0]), (owned, 128))
    half = len(sums) // 2
    for side in range(2):
        total = sums[side * half][...].astype(F32)
        for ref in sums[side * half + 1 : (side + 1) * half]:
            total += ref[...].astype(F32)
        summed[side] = total
    rows = summed.shape[1]
    stripes = written.shape[0]
    copies = []
    for stripe in range(stripes):
        low, high = rows * stripe // stripes, rows * (stripe + 1) // stripes
        for row in range(low, high):
            staged[:, row * 128 : (row + 1) * 128] = (
                first * summed[0, row : row + 1, :] + second * summed[1, row : row + 1, :]
            )
        span = pl.ds(low * 128, (high - low) * 128)
        copies.append(pltpu.make_async_copy(staged.at[:, span], out_ref.at[:, span], written.at[stripe]))
        copies[-1].start()
    for copy in copies:
        copy.wait()


def expert_product(coef, sums, owned, scale):
    rows = sums[0].shape[0]
    return pl.pallas_call(
        functools.partial(expert_kernel, scale=scale),
        in_specs=[VMEM] * (1 + len(sums)),
        out_specs=HBM,
        out_shape=jax.ShapeDtypeStruct((owned, rows * 128), F32),
        scratch_shapes=[
            pltpu.VMEM((2, rows, 128), F32),
            pltpu.VMEM((owned, rows * 128), F32),
            pltpu.SemaphoreType.DMA((4,)),
        ],
        compiler_params=limits(8),
        cost_estimate=cost(10**6, 4 * 10**6),
        name="expert_product",
    )(coef, *sums)


def finish_kernel(send_ref, own_ref, a_ref, b_ref, c_ref, d_ref, out_ref):
    atoms = own_ref.shape[1]
    face = send_ref.shape[1]
    row = lax.broadcasted_iota(jnp.int32, (atoms, face), 0)
    picks = []
    for side in range(2):
        even = lax.rem(lax.axis_index(("gx", "yz")[side]), 2) == 0
        below, above = send_ref[2 * side : 2 * side + 1, :], send_ref[2 * side + 1 : 2 * side + 2, :]
        for faces in (jnp.where(even, above, below), jnp.where(even, below, above)):
            picks.append((row == faces).astype(F32).astype(BF16))
    picks = [picks[3], picks[1], picks[2], picks[0]]
    for c in range(9):
        total = own_ref[c]
        for pick, ref in zip(picks, (a_ref, b_ref, c_ref, d_ref)):
            total += nn(pick, ref[c])
        out_ref[c] = total.astype(BF16)


def finish(send, own, returned):
    return pl.pallas_call(
        finish_kernel,
        in_specs=[VMEM] * 6,
        out_specs=VMEM,
        out_shape=jax.ShapeDtypeStruct(own.shape, BF16),
        compiler_params=limits(6),
        cost_estimate=cost(10**8, 2 * 10**6),
        name="finish",
    )(send, own, *returned)


def swap(value, axis, bit):
    return lax.ppermute(value, axis, [(i, i ^ bit) for i in range(lax.axis_size(axis))])


def neighbour_pairs(value, axis, first):
    count = lax.axis_size(axis)
    moves = []
    for low in range(first, count, 2):
        high = (low + 1) % count
        moves += [(low, high), (high, low)]
    return lax.ppermute(value, axis, moves)


def local(
    saved_input, cotangent, neighbours, rot_zero, rot_one, rot_two, send_index, atom_class, live_blocks,
    merge_coef, experts,
):
    atoms, fanout = neighbours.shape
    slots = saved_input.shape[0]
    channels = cotangent.shape[2]
    face = send_index.shape[1]
    count_yz, count_gx = lax.axis_size("yz"), lax.axis_size("gx")
    row, column = lax.axis_index("yz"), lax.axis_index("gx")
    core = column % 2
    height = experts.shape[1] // 128
    rows = height * count_yz
    direct = height % 32 == 0 and count_yz & (count_yz - 1) == 0 and count_gx == 4

    zero = rot_zero.reshape(1, -1)
    source = jnp.transpose(saved_input, (1, 0, 2))
    target = jnp.transpose(cotangent, (1, 0, 2))

    if direct:
        half = height // 2
        mine = merge(merge_coef, experts, 2)
        order = sorted(range(1, count_yz), key=lambda k: (k == 1, k))
        held = [mine] + [swap(mine, "yz", k) for k in reversed(order)]
        source, target, mine = lax.optimization_barrier((source, target, mine))

        def places():
            here, side = lax.axis_index("yz"), lax.rem(lax.axis_index("gx"), 2)
            starts = [(here ^ k) * height for k in [0, *reversed(order)]]
            return [at + side * half for at in starts] + [at + (1 - side) * half for at in starts]
    else:
        part = jnp.dot(merge_coef, experts.astype(F32), precision=lax.Precision.HIGHEST).astype(BF16)
        merged = lax.all_gather(part, "yz", axis=1, tiled=True)
        pieces = [merged.reshape(1, merged.shape[0], rows, 128)]

        def places():
            return [0]

    other, own, pulled, edge = features(
        live_blocks, neighbours.T, atom_class.reshape(1, -1), zero, rot_one, rot_two, source, target, rows, fanout
    )
    if direct:
        other, *held = lax.optimization_barrier((other, *held))
        came = swap(other, "gx", 1)
        parts = pair_sum(own, came, count_yz)
        gathered = [parts[0]] + [swap(parts[k], "yz", k) for k in order]
        held = pack(held)
        pieces = [held, swap(held, "gx", 1)]
    grad_own, *ghosts = back(edge, zero, rot_one, rot_two, pulled, pieces, places, rows, atoms, slots, face)
    returned = [
        neighbour_pairs(ghost, axis, first)
        for ghost, axis, first in zip(ghosts, ("yz", "gx", "yz", "gx"), (1, 1, 0, 0))
    ]
    if direct:
        grad_own, *gathered = lax.optimization_barrier((grad_own, *gathered))
        summed, *returned[:2] = lax.optimization_barrier((total_sum(gathered), *returned[:2]))
        across = swap(summed, "gx", 2)
        input_grad = finish(send_index, grad_own, returned)
        across, input_grad = lax.optimization_barrier((across, input_grad))
        sums = [summed, across, swap(summed, "gx", 1), swap(across, "gx", 1)]
    else:
        mixed = jnp.stack([own, other]).astype(F32)
        mixed = jnp.where(core == 0, mixed, mixed[::-1])
        whole = lax.psum(mixed, ("yz", "gx"))
        piece = lax.dynamic_slice_in_dim(whole, row * height, height, 1)
        piece = jnp.where(core == 0, piece, piece[::-1])
        sums = [piece[0], piece[1]]
        input_grad = finish(send_index, grad_own, returned)
    grad_scale = math.sqrt(fanout / (atoms * count_yz * count_gx))
    expert_grad = expert_product(merge_coef, sums, merge_coef.shape[1] // count_gx, grad_scale)
    return (jnp.transpose(input_grad, (1, 0, 2)), expert_grad)


def solution(mesh):
    tiles = ("rep", "yz", "gx")
    in_specs = (
        P(tiles, None, None),
        P(tiles, None, None),
        P(tiles, None),
        P(tiles),
        P(None, None, tiles),
        P(None, None, tiles),
        P(tiles, None),
        P(tiles),
        P(tiles),
        P(),
        P(None, "yz"),
    )
    out_specs = (P(tiles, None, None), P(("rep", "gx"), "yz"))
    return jax.shard_map(local, mesh=mesh, in_specs=in_specs, out_specs=out_specs, check_vma=False)
```

```python
import functools
import math

import jax
import jax.numpy as jnp
from jax import lax
from jax.experimental import pallas as pl
from jax.experimental.pallas import tpu as pltpu
from jax.sharding import PartitionSpec as P

LIVE_BLOCK = 64
CHUNK = 256
SUB = 16
F32 = jnp.float32
BF16 = jnp.bfloat16

STACK = (0, 2, 6, 3, 7, 1, 5)
SLOT = {component: place for place, component in enumerate(STACK)}

VMEM = pl.BlockSpec(memory_space=pltpu.VMEM)
HBM = pl.BlockSpec(memory_space=pltpu.HBM)


def limits(mebibytes):
    return pltpu.CompilerParams(vmem_limit_bytes=mebibytes * 1024 * 1024)


def cost(flops, moved):
    return pl.CostEstimate(flops=flops, bytes_accessed=moved, transcendentals=0)


def nn(left, right):
    return lax.dot_general(left, right, (((1,), (0,)), ((), ())), preferred_element_type=F32)


def nt(left, right):
    return lax.dot_general(left, right, (((1,), (1,)), ((), ())), preferred_element_type=F32)


def split3(value):
    high = value.astype(BF16)
    rest = value - high.astype(F32)
    middle = rest.astype(BF16)
    low = (rest - middle.astype(F32)).astype(BF16)
    return high, middle, low


def merge_kernel(coef_in_ref, experts_ref, out_ref, held, coef_ref, arrived, coef_arrived):
    members, experts = coef_in_ref.shape
    rows = out_ref.shape[1]
    start = pl.multiple_of(lax.rem(lax.axis_index("gx"), 2) * rows * 128, 128)
    stripes = arrived.shape[0]
    blocks = rows // 16
    edges = [blocks * stripe // stripes for stripe in range(stripes + 1)]
    copies = []
    for stripe in range(stripes):
        at, wide = edges[stripe] * 2048, (edges[stripe + 1] - edges[stripe]) * 2048
        copies.append(
            pltpu.make_async_copy(
                experts_ref.at[:, pl.ds(start + at, wide)], held.at[:, pl.ds(at, wide)], arrived.at[stripe]
            )
        )
        copies[-1].start()
    coef_copy = pltpu.make_async_copy(coef_in_ref, coef_ref, coef_arrived)
    coef_copy.start()
    coef_copy.wait()
    wide = 8 * experts
    row = lax.broadcasted_iota(jnp.int32, (8, wide), 0)
    col = lax.broadcasted_iota(jnp.int32, (8, wide), 1)
    diagonal = row == col // experts
    source = lax.broadcasted_iota(jnp.int32, (experts, wide), 0)
    target = lax.broadcasted_iota(jnp.int32, (experts, wide), 1)
    tile = (source == target % experts).astype(F32).astype(BF16)
    lefts = []
    for term in split3(coef_ref[...]):
        tiled = nn(term, tile)
        for member in range(members):
            lefts.append(jnp.where(diagonal, tiled[member : member + 1, :], 0.0).astype(BF16))
    lefts = jnp.concatenate(lefts, axis=0)
    height = 8 * members
    for block in range(blocks):
        if block in edges:
            copies[edges.index(block)].wait()
        halves = []
        for half in range(2):
            first = block * 16 + half * 8
            groups = [held[:, (first + g) * 128 : (first + g + 1) * 128] for g in range(8)]
            halves.append(jnp.concatenate(groups, axis=0))
        product = nn(lefts, jnp.concatenate(halves, axis=1))
        total = product[:height] + product[height : 2 * height] + product[2 * height :]
        for member in range(members):
            part = total[member * 8 : member * 8 + 8]
            out_ref[member, block * 16 : block * 16 + 16, :] = jnp.concatenate(
                [part[:, :128], part[:, 128:]], axis=0
            ).astype(BF16)


def merge(coef, experts, parts):
    members, count = coef.shape
    columns = experts.shape[1] // parts
    rows = columns // 128
    return pl.pallas_call(
        merge_kernel,
        in_specs=[HBM, HBM],
        out_specs=VMEM,
        out_shape=jax.ShapeDtypeStruct((members, rows, 128), BF16),
        scratch_shapes=[
            pltpu.VMEM((count, columns), BF16),
            pltpu.VMEM((members, count), F32),
            pltpu.SemaphoreType.DMA((2,)),
            pltpu.SemaphoreType.DMA,
        ],
        compiler_params=limits(52),
        cost_estimate=cost(96 * 16 * columns, 2 * count * columns),
        name="merge",
    )(coef, experts)


def features_kernel(
    live_in_ref, near_ref, class_ref, zero_ref, one_ref, two_ref, source_ref, target_ref,
    other_ref, own_ref, pulled_ref, edge_ref,
    source_t, target_t, moved, spread, rotated, grads, live_ref, live_arrived,
    *, fanout,
):
    slots, channels = source_ref.shape[1:]
    atoms = target_ref.shape[1]
    edges = atoms * fanout
    live_copy = pltpu.make_async_copy(live_in_ref, live_ref, live_arrived)
    live_copy.start()
    for c in range(9):
        source_t[c * channels : (c + 1) * channels, :] = source_ref[c].T
        target_t[c * channels : (c + 1) * channels, :] = target_ref[c].T
    near = near_ref[...].astype(F32).astype(BF16)
    classes = class_ref[...].astype(F32).astype(BF16)
    scale = 1.0 / math.sqrt(fanout)

    def chunk_step(chunk, carry):
        start = pl.multiple_of(chunk * CHUNK, CHUNK)
        here = pl.ds(start, CHUNK)
        edge = lax.broadcasted_iota(jnp.int32, (atoms, CHUNK), 1) + start
        atom = lax.broadcasted_iota(jnp.int32, (atoms, CHUNK), 0)
        repeat = (edge // fanout == atom).astype(F32).astype(BF16)
        edge8 = lax.broadcasted_iota(jnp.int32, (fanout, CHUNK), 1) + start
        lane8 = lax.broadcasted_iota(jnp.int32, (fanout, CHUNK), 0)
        picked = jnp.where(edge8 % fanout == lane8, nn(near, repeat), 0.0)
        near_row = jnp.sum(picked, axis=0, keepdims=True)
        class_row = nn(classes, repeat)
        edge_ref[0:1, here] = near_row
        edge_ref[1:2, here] = class_row
        slot = lax.broadcasted_iota(jnp.int32, (slots, CHUNK), 0).astype(F32)
        pick = (slot == near_row).astype(F32).astype(BF16)
        moved[...] = nn(source_t[...], pick)
        spread[...] = nn(target_t[...], repeat)

        def sub_step(sub, inner):
            at = pl.multiple_of(sub * SUB, SUB)

            def turn(field, write):
                def part(c):
                    return field[pl.ds(c * channels + at, SUB), :]

                write(0, zero_ref[0:1, here] * part(0))
                values = [part(c) for c in (1, 2, 3)]
                for a in range(3):
                    total = one_ref[a, 0:1, here] * values[0]
                    for b in range(1, 3):
                        total += one_ref[a, b : b + 1, here] * values[b]
                    write(1 + a, total)
                values = [part(c) for c in (4, 5, 6, 7, 8)]
                for a in range(1, 4):
                    total = two_ref[a, 0:1, here] * values[0]
                    for b in range(1, 5):
                        total += two_ref[a, b : b + 1, here] * values[b]
                    write(4 + a, total)

            def write_rotated(c, value):
                rotated[pl.ds(SLOT[c] * channels + at, SUB), here] = value.astype(BF16)

            def write_pulled(c, value):
                pulled_ref[pl.ds(SLOT[c] * channels + at, SUB), here] = (value * scale).astype(BF16)

            turn(moved, write_rotated)
            turn(spread, write_pulled)
            return inner

        lax.fori_loop(0, channels // SUB, sub_step, 0)
        return carry

    lax.fori_loop(0, edges // CHUNK, chunk_step, 0)
    live_copy.wait()
    edge_row = lax.broadcasted_iota(jnp.int32, (1, edges), 1)
    edge_ref[1:2, :] = jnp.where(edge_row < live_ref[0] * LIVE_BLOCK * fanout, edge_ref[1:2, :], -1.0)
    zw, pw = 3 * channels, 2 * channels
    first = zw * zw // 128
    second = first + pw * pw // 128
    own = lax.rem(lax.axis_index("gx"), 2).astype(F32)
    for out_ref, wanted in ((other_ref, 1.0 - own), (own_ref, own)):
        mask = (edge_ref[1:2, :] == wanted).astype(F32).astype(BF16)
        qz = pulled_ref[0:zw, :] * mask
        qp = pulled_ref[zw : zw + pw, :] * mask
        qn = pulled_ref[zw + pw : zw + 2 * pw, :] * mask
        z, p, n = rotated[0:zw, :], rotated[zw : zw + pw, :], rotated[zw + pw : zw + 2 * pw, :]
        whole = nt(z, qz)
        for j in range(zw // 128):
            grads[pl.ds(j, zw, stride=zw // 128), :] = whole[:, j * 128 : (j + 1) * 128]
        coupled = nt(p, qp) + nt(n, qn)
        crossed = nt(p, qn) - nt(n, qp)
        for j in range(pw // 128):
            grads[pl.ds(first + j, pw, stride=pw // 128), :] = coupled[:, j * 128 : (j + 1) * 128]
            grads[pl.ds(second + j, pw, stride=pw // 128), :] = crossed[:, j * 128 : (j + 1) * 128]
        out_ref[...] = grads[...].astype(BF16)


def features(live, near, classes, zero, one, two, source, target, rows, fanout):
    slots, channels = source.shape[1:]
    atoms = target.shape[1]
    edges = atoms * fanout
    shape = jax.ShapeDtypeStruct
    return pl.pallas_call(
        functools.partial(features_kernel, fanout=fanout),
        in_specs=[HBM] + [VMEM] * 7,
        out_specs=[VMEM] * 4,
        out_shape=[
            shape((rows, 128), BF16),
            shape((rows, 128), BF16),
            shape((7 * channels, edges), BF16),
            shape((8, edges), F32),
        ],
        scratch_shapes=[
            pltpu.VMEM((9 * channels, slots), BF16),
            pltpu.VMEM((9 * channels, atoms), BF16),
            pltpu.VMEM((9 * channels, CHUNK), F32),
            pltpu.VMEM((9 * channels, CHUNK), F32),
            pltpu.VMEM((7 * channels, edges), BF16),
            pltpu.VMEM((rows, 128), F32),
            pltpu.SMEM((1,), jnp.int32),
            pltpu.SemaphoreType.DMA,
        ],
        compiler_params=limits(24),
        cost_estimate=cost(9 * 10**9, 7 * 10**6),
        name="features",
    )(live, near, classes, zero, one, two, source, target)


def back_kernel(
    edge_ref, zero_ref, one_ref, two_ref, pulled_ref, *rest, pieces, members, atoms, face, places,
):
    piece_refs = rest[:pieces]
    own_ref, *ghost_refs = rest[pieces : pieces + 5]
    flat, weight_zero, weight_pair, field, turned, pick_all = rest[pieces + 5 :]
    rows = flat.shape[1]
    channels = own_ref.shape[2]
    slots = pick_all.shape[0]
    edges = pulled_ref.shape[1]
    zw, pw = 3 * channels, 2 * channels
    first = zw * zw // 128
    second = first + pw * pw // 128
    placed = [(piece, index) for piece in piece_refs for index in range(piece.shape[0])]
    for (piece, index), place in zip(placed, places()):
        height = piece.shape[2]
        at = pl.ds(pl.multiple_of(place, 16), height)
        for k in range(members):
            flat[k, at, :] = piece[index, k].astype(F32)
    for k in range(members):
        for j in range(zw // 128):
            weight_zero[:, k * zw + j * 128 : k * zw + (j + 1) * 128] = flat[
                k, pl.ds(j, zw, stride=zw // 128), :
            ].astype(BF16)
        for j in range(pw // 128):
            at = k * 2 * pw + j * 128
            weight_pair[:, at : at + 128] = flat[k, pl.ds(first + j, pw, stride=pw // 128), :].astype(BF16)
            weight_pair[:, at + pw : at + pw + 128] = flat[
                k, pl.ds(second + j, pw, stride=pw // 128), :
            ].astype(BF16)

    def chunk_step(chunk, carry):
        start = pl.multiple_of(chunk * CHUNK, CHUNK)
        here = pl.ds(start, CHUNK)
        slot = lax.broadcasted_iota(jnp.int32, (slots, CHUNK), 0).astype(F32)
        pick_all[:, here] = (slot == edge_ref[0:1, here]).astype(F32).astype(BF16)
        qz, qpn, qnp = [], [], []
        for k in range(members):
            mask = (edge_ref[1:2, here] == float(k)).astype(F32).astype(BF16)
            qz.append(pulled_ref[0:zw, here] * mask)
            qp = pulled_ref[zw : zw + pw, here] * mask
            qn = pulled_ref[zw + pw : zw + 2 * pw, here] * mask
            qpn += [qp, qn]
            qnp += [qn, -qp]
        field[0:zw, :] = nn(weight_zero[...], jnp.concatenate(qz, axis=0))
        field[zw : zw + pw, :] = nn(weight_pair[...], jnp.concatenate(qpn, axis=0))
        field[zw + pw : zw + 2 * pw, :] = nn(weight_pair[...], jnp.concatenate(qnp, axis=0))

        def sub_step(sub, inner):
            at = pl.multiple_of(sub * SUB, SUB)

            def part(c):
                return field[pl.ds(SLOT[c] * channels + at, SUB), :]

            def write(c, value):
                turned[pl.ds(c * channels + at, SUB), here] = value.astype(BF16)

            write(0, zero_ref[0:1, here] * part(0))
            values = [part(c) for c in (1, 2, 3)]
            for b in range(3):
                total = one_ref[0, b : b + 1, here] * values[0]
                for a in range(1, 3):
                    total += one_ref[a, b : b + 1, here] * values[a]
                write(1 + b, total)
            values = [part(c) for c in (5, 6, 7)]
            for b in range(5):
                total = two_ref[1, b : b + 1, here] * values[0]
                for a in range(2, 4):
                    total += two_ref[a, b : b + 1, here] * values[a - 1]
                write(4 + b, total)
            return inner

        lax.fori_loop(0, channels // SUB, sub_step, 0)
        return carry

    lax.fori_loop(0, edges // CHUNK, chunk_step, 0)
    for c in range(9):
        summed = nt(pick_all[...], turned[c * channels : (c + 1) * channels, :])
        own_ref[c] = summed[:atoms]
        blocks = [summed[atoms + block * face : atoms + (block + 1) * face] for block in range(4)]
        for side in range(2):
            even = lax.rem(lax.axis_index(("gx", "yz")[side]), 2) == 0
            low, high = blocks[2 * side], blocks[2 * side + 1]
            ghost_refs[3 - side][c] = jnp.where(even, high, low).astype(BF16)
            ghost_refs[1 - side][c] = jnp.where(even, low, high).astype(BF16)


def back(edge, zero, one, two, pulled, pieces, places, rows, atoms, slots, face):
    members = pieces[0].shape[1]
    edges = pulled.shape[1]
    channels = pulled.shape[0] // 7
    shape = jax.ShapeDtypeStruct
    return pl.pallas_call(
        functools.partial(
            back_kernel, pieces=len(pieces), members=members, atoms=atoms, face=face, places=places
        ),
        in_specs=[VMEM] * (5 + len(pieces)),
        out_specs=[VMEM] * 5,
        out_shape=[shape((9, atoms, channels), F32), *[shape((9, face, channels), BF16)] * 4],
        scratch_shapes=[
            pltpu.VMEM((members, rows, 128), F32),
            pltpu.VMEM((3 * channels, members * 3 * channels), BF16),
            pltpu.VMEM((2 * channels, members * 4 * channels), BF16),
            pltpu.VMEM((7 * channels, CHUNK), F32),
            pltpu.VMEM((9 * channels, edges), BF16),
            pltpu.VMEM((slots, edges), BF16),
        ],
        compiler_params=limits(24),
        cost_estimate=cost(9 * 10**9, 7 * 10**6),
        name="back",
    )(edge, zero, one, two, pulled, *pieces)


def pair_kernel(own_ref, came_ref, *out_refs):
    height = out_refs[0].shape[0]
    row = lax.axis_index("yz")
    for index, out_ref in enumerate(out_refs):
        at = pl.ds(pl.multiple_of((row ^ index) * height, 16), height)
        out_ref[...] = (own_ref[at, :].astype(F32) + came_ref[at, :].astype(F32)).astype(BF16)


def pair_sum(own, came, count):
    height = own.shape[0] // count
    return pl.pallas_call(
        pair_kernel,
        in_specs=[VMEM, VMEM],
        out_specs=[VMEM] * count,
        out_shape=[jax.ShapeDtypeStruct((height, 128), BF16)] * count,
        compiler_params=limits(6),
        cost_estimate=cost(10**6, 2 * 10**6),
        name="pair_sum",
    )(own, came)


def total_kernel(*refs):
    total = refs[0][...].astype(F32)
    for ref in refs[1:-1]:
        total += ref[...].astype(F32)
    refs[-1][...] = total.astype(BF16)


def total_sum(parts):
    return pl.pallas_call(
        total_kernel,
        in_specs=[VMEM] * len(parts),
        out_specs=VMEM,
        out_shape=jax.ShapeDtypeStruct(parts[0].shape, BF16),
        compiler_params=limits(6),
        cost_estimate=cost(10**6, 10**6),
        name="total_sum",
    )(*parts)


def pack_kernel(*refs):
    for index, ref in enumerate(refs[:-1]):
        refs[-1][index] = ref[...]


def pack(pieces):
    return pl.pallas_call(
        pack_kernel,
        in_specs=[VMEM] * len(pieces),
        out_specs=VMEM,
        out_shape=jax.ShapeDtypeStruct((len(pieces), *pieces[0].shape), pieces[0].dtype),
        compiler_params=limits(6),
        cost_estimate=cost(10**5, 10**6),
        name="pack",
    )(*pieces)


def expert_kernel(coef_ref, *refs, scale):
    sums, out_ref, summed, staged, written = refs[:-4], *refs[-4:]
    owned = out_ref.shape[0]
    place = lax.axis_index("gx")
    row = lax.broadcasted_iota(jnp.int32, (owned, coef_ref.shape[1]), 0)
    col = lax.broadcasted_iota(jnp.int32, (owned, coef_ref.shape[1]), 1)
    chosen = col == row + place * owned
    picked = [
        jnp.sum(jnp.where(chosen, coef_ref[k : k + 1, :], 0.0), axis=1, keepdims=True) * scale for k in range(2)
    ]
    even = lax.rem(place, 2) == 0
    first = jnp.broadcast_to(jnp.where(even, picked[0], picked[1]), (owned, 128))
    second = jnp.broadcast_to(jnp.where(even, picked[1], picked[0]), (owned, 128))
    half = len(sums) // 2
    for side in range(2):
        total = sums[side * half][...].astype(F32)
        for ref in sums[side * half + 1 : (side + 1) * half]:
            total += ref[...].astype(F32)
        summed[side] = total
    rows = summed.shape[1]
    stripes = written.shape[0]
    copies = []
    for stripe in range(stripes):
        low, high = rows * stripe // stripes, rows * (stripe + 1) // stripes
        for row in range(low, high):
            staged[:, row * 128 : (row + 1) * 128] = (
                first * summed[0, row : row + 1, :] + second * summed[1, row : row + 1, :]
            )
        span = pl.ds(low * 128, (high - low) * 128)
        copies.append(pltpu.make_async_copy(staged.at[:, span], out_ref.at[:, span], written.at[stripe]))
        copies[-1].start()
    for copy in copies:
        copy.wait()


def expert_product(coef, sums, owned, scale):
    rows = sums[0].shape[0]
    return pl.pallas_call(
        functools.partial(expert_kernel, scale=scale),
        in_specs=[VMEM] * (1 + len(sums)),
        out_specs=HBM,
        out_shape=jax.ShapeDtypeStruct((owned, rows * 128), F32),
        scratch_shapes=[
            pltpu.VMEM((2, rows, 128), F32),
            pltpu.VMEM((owned, rows * 128), F32),
            pltpu.SemaphoreType.DMA((4,)),
        ],
        compiler_params=limits(8),
        cost_estimate=cost(10**6, 4 * 10**6),
        name="expert_product",
    )(coef, *sums)


def finish_kernel(send_ref, own_ref, a_ref, b_ref, c_ref, d_ref, out_ref):
    atoms = own_ref.shape[1]
    face = send_ref.shape[1]
    row = lax.broadcasted_iota(jnp.int32, (atoms, face), 0)
    picks = []
    for side in range(2):
        even = lax.rem(lax.axis_index(("gx", "yz")[side]), 2) == 0
        below, above = send_ref[2 * side : 2 * side + 1, :], send_ref[2 * side + 1 : 2 * side + 2, :]
        for faces in (jnp.where(even, above, below), jnp.where(even, below, above)):
            picks.append((row == faces).astype(F32).astype(BF16))
    picks = [picks[3], picks[1], picks[2], picks[0]]
    for c in range(9):
        total = own_ref[c]
        for pick, ref in zip(picks, (a_ref, b_ref, c_ref, d_ref)):
            total += nn(pick, ref[c])
        out_ref[c] = total.astype(BF16)


def finish(send, own, returned):
    return pl.pallas_call(
        finish_kernel,
        in_specs=[VMEM] * 6,
        out_specs=VMEM,
        out_shape=jax.ShapeDtypeStruct(own.shape, BF16),
        compiler_params=limits(6),
        cost_estimate=cost(10**8, 2 * 10**6),
        name="finish",
    )(send, own, *returned)


def swap(value, axis, bit):
    return lax.ppermute(value, axis, [(i, i ^ bit) for i in range(lax.axis_size(axis))])


def neighbour_pairs(value, axis, first):
    count = lax.axis_size(axis)
    moves = []
    for low in range(first, count, 2):
        high = (low + 1) % count
        moves += [(low, high), (high, low)]
    return lax.ppermute(value, axis, moves)


def local(
    saved_input, cotangent, neighbours, rot_zero, rot_one, rot_two, send_index, atom_class, live_blocks,
    merge_coef, experts,
):
    atoms, fanout = neighbours.shape
    slots = saved_input.shape[0]
    channels = cotangent.shape[2]
    face = send_index.shape[1]
    count_yz, count_gx = lax.axis_size("yz"), lax.axis_size("gx")
    row, column = lax.axis_index("yz"), lax.axis_index("gx")
    core = column % 2
    height = experts.shape[1] // 128
    rows = height * count_yz
    direct = height % 32 == 0 and count_yz & (count_yz - 1) == 0 and count_gx == 4

    zero = rot_zero.reshape(1, -1)
    source = jnp.transpose(saved_input, (1, 0, 2))
    target = jnp.transpose(cotangent, (1, 0, 2))

    if direct:
        half = height // 2
        mine = merge(merge_coef, experts, 2)
        held = [mine] + [swap(mine, "yz", k) for k in range(1, count_yz)]
        source, target, mine = lax.optimization_barrier((source, target, mine))

        def places():
            here, side = lax.axis_index("yz"), lax.rem(lax.axis_index("gx"), 2)
            starts = [(here ^ k) * height for k in range(count_yz)]
            return [at + side * half for at in starts] + [at + (1 - side) * half for at in starts]
    else:
        part = jnp.dot(merge_coef, experts.astype(F32), precision=lax.Precision.HIGHEST).astype(BF16)
        merged = lax.all_gather(part, "yz", axis=1, tiled=True)
        pieces = [merged.reshape(1, merged.shape[0], rows, 128)]

        def places():
            return [0]

    other, own, pulled, edge = features(
        live_blocks, neighbours.T, atom_class.reshape(1, -1), zero, rot_one, rot_two, source, target, rows, fanout
    )
    if direct:
        other, *held = lax.optimization_barrier((other, *held))
        came = swap(other, "gx", 1)
        parts = pair_sum(own, came, count_yz)
        gathered = [parts[0]] + [swap(parts[k], "yz", k) for k in reversed(range(1, count_yz))]
        held = pack(held)
        pieces = [held, swap(held, "gx", 1)]
    grad_own, *ghosts = back(edge, zero, rot_one, rot_two, pulled, pieces, places, rows, atoms, slots, face)
    returned = [
        neighbour_pairs(ghost, axis, first)
        for ghost, axis, first in zip(ghosts, ("yz", "gx", "yz", "gx"), (1, 1, 0, 0))
    ]
    if direct:
        grad_own, *gathered = lax.optimization_barrier((grad_own, *gathered))
        summed, *returned = lax.optimization_barrier((total_sum(gathered), *returned))
        across = swap(summed, "gx", 2)
        input_grad = finish(send_index, grad_own, returned)
        across, input_grad = lax.optimization_barrier((across, input_grad))
        sums = [summed, across, swap(summed, "gx", 1), swap(across, "gx", 1)]
    else:
        mixed = jnp.stack([own, other]).astype(F32)
        mixed = jnp.where(core == 0, mixed, mixed[::-1])
        whole = lax.psum(mixed, ("yz", "gx"))
        piece = lax.dynamic_slice_in_dim(whole, row * height, height, 1)
        piece = jnp.where(core == 0, piece, piece[::-1])
        sums = [piece[0], piece[1]]
        input_grad = finish(send_index, grad_own, returned)
    grad_scale = math.sqrt(fanout / (atoms * count_yz * count_gx))
    expert_grad = expert_product(merge_coef, sums, merge_coef.shape[1] // count_gx, grad_scale)
    return (jnp.transpose(input_grad, (1, 0, 2)), expert_grad)


def solution(mesh):
    tiles = ("rep", "yz", "gx")
    in_specs = (
        P(tiles, None, None),
        P(tiles, None, None),
        P(tiles, None),
        P(tiles),
        P(None, None, tiles),
        P(None, None, tiles),
        P(tiles, None),
        P(tiles),
        P(tiles),
        P(),
        P(None, "yz"),
    )
    out_specs = (P(tiles, None, None), P(("rep", "gx"), "yz"))
    return jax.shard_map(local, mesh=mesh, in_specs=in_specs, out_specs=out_specs, check_vma=False)
```

```python
import functools
import math

import jax
import jax.numpy as jnp
from jax import lax
from jax.experimental import pallas as pl
from jax.experimental.pallas import tpu as pltpu
from jax.sharding import PartitionSpec as P

LIVE_BLOCK = 64
CHUNK = 256
SUB = 16
F32 = jnp.float32
BF16 = jnp.bfloat16

STACK = (0, 2, 6, 3, 7, 1, 5)
SLOT = {component: place for place, component in enumerate(STACK)}

VMEM = pl.BlockSpec(memory_space=pltpu.VMEM)
HBM = pl.BlockSpec(memory_space=pltpu.HBM)


def limits(mebibytes):
    return pltpu.CompilerParams(vmem_limit_bytes=mebibytes * 1024 * 1024)


def cost(flops, moved):
    return pl.CostEstimate(flops=flops, bytes_accessed=moved, transcendentals=0)


def nn(left, right):
    return lax.dot_general(left, right, (((1,), (0,)), ((), ())), preferred_element_type=F32)


def nt(left, right):
    return lax.dot_general(left, right, (((1,), (1,)), ((), ())), preferred_element_type=F32)


def split3(value):
    high = value.astype(BF16)
    rest = value - high.astype(F32)
    middle = rest.astype(BF16)
    low = (rest - middle.astype(F32)).astype(BF16)
    return high, middle, low


def merge_kernel(coef_in_ref, experts_ref, out_ref, held, coef_ref, arrived, coef_arrived):
    members, experts = coef_in_ref.shape
    rows = out_ref.shape[1]
    start = pl.multiple_of(lax.rem(lax.axis_index("gx"), 2) * rows * 128, 128)
    stripes = arrived.shape[0]
    blocks = rows // 16
    edges = [blocks * stripe // stripes for stripe in range(stripes + 1)]
    copies = []
    for stripe in range(stripes):
        at, wide = edges[stripe] * 2048, (edges[stripe + 1] - edges[stripe]) * 2048
        copies.append(
            pltpu.make_async_copy(
                experts_ref.at[:, pl.ds(start + at, wide)], held.at[:, pl.ds(at, wide)], arrived.at[stripe]
            )
        )
        copies[-1].start()
    coef_copy = pltpu.make_async_copy(coef_in_ref, coef_ref, coef_arrived)
    coef_copy.start()
    coef_copy.wait()
    wide = 8 * experts
    row = lax.broadcasted_iota(jnp.int32, (8, wide), 0)
    col = lax.broadcasted_iota(jnp.int32, (8, wide), 1)
    diagonal = row == col // experts
    source = lax.broadcasted_iota(jnp.int32, (experts, wide), 0)
    target = lax.broadcasted_iota(jnp.int32, (experts, wide), 1)
    tile = (source == target % experts).astype(F32).astype(BF16)
    lefts = []
    for term in split3(coef_ref[...]):
        tiled = nn(term, tile)
        for member in range(members):
            lefts.append(jnp.where(diagonal, tiled[member : member + 1, :], 0.0).astype(BF16))
    lefts = jnp.concatenate(lefts, axis=0)
    height = 8 * members
    for block in range(blocks):
        if block in edges:
            copies[edges.index(block)].wait()
        halves = []
        for half in range(2):
            first = block * 16 + half * 8
            groups = [held[:, (first + g) * 128 : (first + g + 1) * 128] for g in range(8)]
            halves.append(jnp.concatenate(groups, axis=0))
        product = nn(lefts, jnp.concatenate(halves, axis=1))
        total = product[:height] + product[height : 2 * height] + product[2 * height :]
        for member in range(members):
            part = total[member * 8 : member * 8 + 8]
            out_ref[member, block * 16 : block * 16 + 16, :] = jnp.concatenate(
                [part[:, :128], part[:, 128:]], axis=0
            ).astype(BF16)


def merge(coef, experts, parts):
    members, count = coef.shape
    columns = experts.shape[1] // parts
    rows = columns // 128
    return pl.pallas_call(
        merge_kernel,
        in_specs=[HBM, HBM],
        out_specs=VMEM,
        out_shape=jax.ShapeDtypeStruct((members, rows, 128), BF16),
        scratch_shapes=[
            pltpu.VMEM((count, columns), BF16),
            pltpu.VMEM((members, count), F32),
            pltpu.SemaphoreType.DMA((2,)),
            pltpu.SemaphoreType.DMA,
        ],
        compiler_params=limits(52),
        cost_estimate=cost(96 * 16 * columns, 2 * count * columns),
        name="merge",
    )(coef, experts)


def features_kernel(
    near_ref, class_ref, zero_ref, one_ref, two_ref, source_ref, target_ref,
    other_ref, own_ref, pulled_ref, edge_ref,
    source_t, target_t, moved, spread, rotated, grads,
    *, fanout,
):
    slots, channels = source_ref.shape[1:]
    atoms = target_ref.shape[1]
    edges = atoms * fanout
    for c in range(9):
        source_t[c * channels : (c + 1) * channels, :] = source_ref[c].T
        target_t[c * channels : (c + 1) * channels, :] = target_ref[c].T
    near = near_ref[...].astype(F32).astype(BF16)
    classes = class_ref[...].astype(F32).astype(BF16)
    scale = 1.0 / math.sqrt(fanout)

    def chunk_step(chunk, carry):
        start = pl.multiple_of(chunk * CHUNK, CHUNK)
        here = pl.ds(start, CHUNK)
        edge = lax.broadcasted_iota(jnp.int32, (atoms, CHUNK), 1) + start
        atom = lax.broadcasted_iota(jnp.int32, (atoms, CHUNK), 0)
        repeat = (edge // fanout == atom).astype(F32).astype(BF16)
        edge8 = lax.broadcasted_iota(jnp.int32, (fanout, CHUNK), 1) + start
        lane8 = lax.broadcasted_iota(jnp.int32, (fanout, CHUNK), 0)
        picked = jnp.where(edge8 % fanout == lane8, nn(near, repeat), 0.0)
        near_row = jnp.sum(picked, axis=0, keepdims=True)
        class_row = nn(classes, repeat)
        edge_ref[0:1, here] = near_row
        edge_ref[1:2, here] = class_row
        slot = lax.broadcasted_iota(jnp.int32, (slots, CHUNK), 0).astype(F32)
        pick = (slot == near_row).astype(F32).astype(BF16)
        moved[...] = nn(source_t[...], pick)
        spread[...] = nn(target_t[...], repeat)

        def sub_step(sub, inner):
            at = pl.multiple_of(sub * SUB, SUB)

            def turn(field, write):
                def part(c):
                    return field[pl.ds(c * channels + at, SUB), :]

                write(0, zero_ref[0:1, here] * part(0))
                values = [part(c) for c in (1, 2, 3)]
                for a in range(3):
                    total = one_ref[a, 0:1, here] * values[0]
                    for b in range(1, 3):
                        total += one_ref[a, b : b + 1, here] * values[b]
                    write(1 + a, total)
                values = [part(c) for c in (4, 5, 6, 7, 8)]
                for a in range(1, 4):
                    total = two_ref[a, 0:1, here] * values[0]
                    for b in range(1, 5):
                        total += two_ref[a, b : b + 1, here] * values[b]
                    write(4 + a, total)

            def write_rotated(c, value):
                rotated[pl.ds(SLOT[c] * channels + at, SUB), here] = value.astype(BF16)

            def write_pulled(c, value):
                pulled_ref[pl.ds(SLOT[c] * channels + at, SUB), here] = (value * scale).astype(BF16)

            turn(moved, write_rotated)
            turn(spread, write_pulled)
            return inner

        lax.fori_loop(0, channels // SUB, sub_step, 0)
        return carry

    lax.fori_loop(0, edges // CHUNK, chunk_step, 0)
    zw, pw = 3 * channels, 2 * channels
    first = zw * zw // 128
    second = first + pw * pw // 128
    own = lax.rem(lax.axis_index("gx"), 2).astype(F32)
    for out_ref, wanted in ((other_ref, 1.0 - own), (own_ref, own)):
        mask = (edge_ref[1:2, :] == wanted).astype(F32).astype(BF16)
        qz = pulled_ref[0:zw, :] * mask
        qp = pulled_ref[zw : zw + pw, :] * mask
        qn = pulled_ref[zw + pw : zw + 2 * pw, :] * mask
        z, p, n = rotated[0:zw, :], rotated[zw : zw + pw, :], rotated[zw + pw : zw + 2 * pw, :]
        whole = nt(z, qz)
        for j in range(zw // 128):
            grads[pl.ds(j, zw, stride=zw // 128), :] = whole[:, j * 128 : (j + 1) * 128]
        coupled = nt(p, qp) + nt(n, qn)
        crossed = nt(p, qn) - nt(n, qp)
        for j in range(pw // 128):
            grads[pl.ds(first + j, pw, stride=pw // 128), :] = coupled[:, j * 128 : (j + 1) * 128]
            grads[pl.ds(second + j, pw, stride=pw // 128), :] = crossed[:, j * 128 : (j + 1) * 128]
        out_ref[...] = grads[...].astype(BF16)


def features(near, classes, zero, one, two, source, target, rows, fanout):
    slots, channels = source.shape[1:]
    atoms = target.shape[1]
    edges = atoms * fanout
    shape = jax.ShapeDtypeStruct
    return pl.pallas_call(
        functools.partial(features_kernel, fanout=fanout),
        in_specs=[VMEM] * 7,
        out_specs=[VMEM] * 4,
        out_shape=[
            shape((rows, 128), BF16),
            shape((rows, 128), BF16),
            shape((7 * channels, edges), BF16),
            shape((8, edges), F32),
        ],
        scratch_shapes=[
            pltpu.VMEM((9 * channels, slots), BF16),
            pltpu.VMEM((9 * channels, atoms), BF16),
            pltpu.VMEM((9 * channels, CHUNK), F32),
            pltpu.VMEM((9 * channels, CHUNK), F32),
            pltpu.VMEM((7 * channels, edges), BF16),
            pltpu.VMEM((rows, 128), F32),
        ],
        compiler_params=limits(24),
        cost_estimate=cost(9 * 10**9, 7 * 10**6),
        name="features",
    )(near, classes, zero, one, two, source, target)


def back_kernel(
    edge_ref, zero_ref, one_ref, two_ref, pulled_ref, *rest, pieces, members, atoms, face, places,
):
    piece_refs = rest[:pieces]
    own_ref, *ghost_refs = rest[pieces : pieces + 5]
    flat, weight_zero, weight_pair, field, turned, pick_all = rest[pieces + 5 :]
    rows = flat.shape[1]
    channels = own_ref.shape[2]
    slots = pick_all.shape[0]
    edges = pulled_ref.shape[1]
    zw, pw = 3 * channels, 2 * channels
    first = zw * zw // 128
    second = first + pw * pw // 128
    placed = [(piece, index) for piece in piece_refs for index in range(piece.shape[0])]
    for (piece, index), place in zip(placed, places()):
        height = piece.shape[2]
        at = pl.ds(pl.multiple_of(place, 16), height)
        for k in range(members):
            flat[k, at, :] = piece[index, k].astype(F32)
    for k in range(members):
        for j in range(zw // 128):
            weight_zero[:, k * zw + j * 128 : k * zw + (j + 1) * 128] = flat[
                k, pl.ds(j, zw, stride=zw // 128), :
            ].astype(BF16)
        for j in range(pw // 128):
            at = k * 2 * pw + j * 128
            weight_pair[:, at : at + 128] = flat[k, pl.ds(first + j, pw, stride=pw // 128), :].astype(BF16)
            weight_pair[:, at + pw : at + pw + 128] = flat[
                k, pl.ds(second + j, pw, stride=pw // 128), :
            ].astype(BF16)

    def chunk_step(chunk, carry):
        start = pl.multiple_of(chunk * CHUNK, CHUNK)
        here = pl.ds(start, CHUNK)
        slot = lax.broadcasted_iota(jnp.int32, (slots, CHUNK), 0).astype(F32)
        pick_all[:, here] = (slot == edge_ref[0:1, here]).astype(F32).astype(BF16)
        qz, qpn, qnp = [], [], []
        for k in range(members):
            mask = (edge_ref[1:2, here] == float(k)).astype(F32).astype(BF16)
            qz.append(pulled_ref[0:zw, here] * mask)
            qp = pulled_ref[zw : zw + pw, here] * mask
            qn = pulled_ref[zw + pw : zw + 2 * pw, here] * mask
            qpn += [qp, qn]
            qnp += [qn, -qp]
        field[0:zw, :] = nn(weight_zero[...], jnp.concatenate(qz, axis=0))
        field[zw : zw + pw, :] = nn(weight_pair[...], jnp.concatenate(qpn, axis=0))
        field[zw + pw : zw + 2 * pw, :] = nn(weight_pair[...], jnp.concatenate(qnp, axis=0))

        def sub_step(sub, inner):
            at = pl.multiple_of(sub * SUB, SUB)

            def part(c):
                return field[pl.ds(SLOT[c] * channels + at, SUB), :]

            def write(c, value):
                turned[pl.ds(c * channels + at, SUB), here] = value.astype(BF16)

            write(0, zero_ref[0:1, here] * part(0))
            values = [part(c) for c in (1, 2, 3)]
            for b in range(3):
                total = one_ref[0, b : b + 1, here] * values[0]
                for a in range(1, 3):
                    total += one_ref[a, b : b + 1, here] * values[a]
                write(1 + b, total)
            values = [part(c) for c in (5, 6, 7)]
            for b in range(5):
                total = two_ref[1, b : b + 1, here] * values[0]
                for a in range(2, 4):
                    total += two_ref[a, b : b + 1, here] * values[a - 1]
                write(4 + b, total)
            return inner

        lax.fori_loop(0, channels // SUB, sub_step, 0)
        return carry

    lax.fori_loop(0, edges // CHUNK, chunk_step, 0)
    for c in range(9):
        summed = nt(pick_all[...], turned[c * channels : (c + 1) * channels, :])
        own_ref[c] = summed[:atoms]
        blocks = [summed[atoms + block * face : atoms + (block + 1) * face] for block in range(4)]
        for side in range(2):
            even = lax.rem(lax.axis_index(("gx", "yz")[side]), 2) == 0
            low, high = blocks[2 * side], blocks[2 * side + 1]
            at = pl.ds(c * face, face)
            ghost_refs[2 * side][at, :] = jnp.where(even, high, low).astype(BF16)
            ghost_refs[2 * side + 1][at, :] = jnp.where(even, low, high).astype(BF16)


def back(edge, zero, one, two, pulled, pieces, places, rows, atoms, slots, face):
    members = pieces[0].shape[1]
    edges = pulled.shape[1]
    channels = pulled.shape[0] // 7
    shape = jax.ShapeDtypeStruct
    return pl.pallas_call(
        functools.partial(
            back_kernel, pieces=len(pieces), members=members, atoms=atoms, face=face, places=places
        ),
        in_specs=[VMEM] * (5 + len(pieces)),
        out_specs=[VMEM] * 5,
        out_shape=[shape((9, atoms, channels), F32), *[shape((9 * face, channels), BF16)] * 4],
        scratch_shapes=[
            pltpu.VMEM((members, rows, 128), F32),
            pltpu.VMEM((3 * channels, members * 3 * channels), BF16),
            pltpu.VMEM((2 * channels, members * 4 * channels), BF16),
            pltpu.VMEM((7 * channels, CHUNK), F32),
            pltpu.VMEM((9 * channels, edges), BF16),
            pltpu.VMEM((slots, edges), BF16),
        ],
        compiler_params=limits(24),
        cost_estimate=cost(9 * 10**9, 7 * 10**6),
        name="back",
    )(edge, zero, one, two, pulled, *pieces)


def core_kernel(own_ref, came_ref, away_ref, keep_ref):
    count = lax.axis_size("yz")
    half = keep_ref.shape[0] // count
    row, side = lax.axis_index("yz"), lax.axis_index("gx") // 2
    for k in range(count):
        start = (row ^ k) * 2 * half
        here = pl.ds(k * half, half)
        near = pl.ds(pl.multiple_of(start + side * half, 16), half)
        far = pl.ds(pl.multiple_of(start + (1 - side) * half, 16), half)
        keep_ref[here, :] = own_ref[near, :].astype(F32) + came_ref[near, :].astype(F32)
        away_ref[here, :] = (own_ref[far, :].astype(F32) + came_ref[far, :].astype(F32)).astype(BF16)


def core_sum(own, came):
    shape = (own.shape[0] // 2, 128)
    return pl.pallas_call(
        core_kernel,
        in_specs=[VMEM] * 2,
        out_specs=[VMEM] * 2,
        out_shape=[jax.ShapeDtypeStruct(shape, BF16), jax.ShapeDtypeStruct(shape, F32)],
        compiler_params=limits(6),
        cost_estimate=cost(10**6, 2 * 10**6),
        name="core_sum",
    )(own, came)


def side_kernel(keep_ref, came_ref, low_ref, high_ref, own_ref, *out_refs):
    half = own_ref.shape[0]
    own_ref[...] = keep_ref[:half] + came_ref[:half].astype(F32)
    for k, out_ref in enumerate(out_refs, 1):
        at = pl.ds(k * half, half)
        out_ref[:half] = (keep_ref[at, :] + came_ref[at, :].astype(F32)).astype(BF16)
    for out_ref in out_refs[1:-1]:
        out_ref[half:] = jnp.zeros_like(out_ref[half:])
    out_refs[0][half:] = low_ref[...]
    out_refs[-1][half:] = high_ref[...]


def side_sum(keep, came, low, high, count):
    half = keep.shape[0] // count
    faces = low.shape[0]
    shape = jax.ShapeDtypeStruct
    spare = max(faces + 16 - half, 0)
    sent = [shape((half + (faces if k in (1, count - 1) else spare), 128), BF16) for k in range(1, count)]
    return pl.pallas_call(
        side_kernel,
        in_specs=[VMEM] * 4,
        out_specs=[VMEM] * count,
        out_shape=[shape((half, 128), F32), *sent],
        compiler_params=limits(6),
        cost_estimate=cost(10**6, 2 * 10**6),
        name="side_sum",
    )(keep, came, low, high)


def total_kernel(*refs):
    half = refs[-1].shape[0]
    total = refs[0][...]
    for ref in refs[1:-1]:
        total += ref[:half].astype(F32)
    refs[-1][...] = total.astype(BF16)


def total_sum(parts):
    return pl.pallas_call(
        total_kernel,
        in_specs=[VMEM] * len(parts),
        out_specs=VMEM,
        out_shape=jax.ShapeDtypeStruct(parts[0].shape, BF16),
        compiler_params=limits(6),
        cost_estimate=cost(10**6, 10**6),
        name="total_sum",
    )(*parts)


def pack_kernel(*refs):
    for index, ref in enumerate(refs[:-1]):
        refs[-1][index] = ref[...]


def pack(pieces):
    return pl.pallas_call(
        pack_kernel,
        in_specs=[VMEM] * len(pieces),
        out_specs=VMEM,
        out_shape=jax.ShapeDtypeStruct((len(pieces), *pieces[0].shape), pieces[0].dtype),
        compiler_params=limits(6),
        cost_estimate=cost(10**5, 10**6),
        name="pack",
    )(*pieces)


def expert_kernel(coef_ref, *refs, scale):
    sums, out_ref, summed, staged, written = refs[:-4], *refs[-4:]
    owned = out_ref.shape[0]
    place = lax.axis_index("gx")
    row = lax.broadcasted_iota(jnp.int32, (owned, coef_ref.shape[1]), 0)
    col = lax.broadcasted_iota(jnp.int32, (owned, coef_ref.shape[1]), 1)
    chosen = col == row + place * owned
    picked = [
        jnp.sum(jnp.where(chosen, coef_ref[k : k + 1, :], 0.0), axis=1, keepdims=True) * scale for k in range(2)
    ]
    even = lax.rem(place, 2) == 0
    first = jnp.broadcast_to(jnp.where(even, picked[0], picked[1]), (owned, 128))
    second = jnp.broadcast_to(jnp.where(even, picked[1], picked[0]), (owned, 128))
    if len(sums) == 4:
        half = sums[0].shape[0]
        side = place // 2
        for index, ref in enumerate(sums):
            at = (side if index % 2 == 0 else 1 - side) * half
            summed[index // 2, pl.ds(pl.multiple_of(at, 16), half), :] = ref[...].astype(F32)
    else:
        for index, ref in enumerate(sums):
            summed[index] = ref[...].astype(F32)
    rows = summed.shape[1]
    stripes = written.shape[0]
    copies = []
    for stripe in range(stripes):
        low, high = rows * stripe // stripes, rows * (stripe + 1) // stripes
        for row in range(low, high):
            staged[:, row * 128 : (row + 1) * 128] = (
                first * summed[0, row : row + 1, :] + second * summed[1, row : row + 1, :]
            )
        span = pl.ds(low * 128, (high - low) * 128)
        copies.append(pltpu.make_async_copy(staged.at[:, span], out_ref.at[:, span], written.at[stripe]))
        copies[-1].start()
    for copy in copies:
        copy.wait()


def expert_product(coef, sums, owned, scale):
    rows = sums[0].shape[0] * len(sums) // 2
    return pl.pallas_call(
        functools.partial(expert_kernel, scale=scale),
        in_specs=[VMEM] * (1 + len(sums)),
        out_specs=HBM,
        out_shape=jax.ShapeDtypeStruct((owned, rows * 128), F32),
        scratch_shapes=[
            pltpu.VMEM((2, rows, 128), F32),
            pltpu.VMEM((owned, rows * 128), F32),
            pltpu.SemaphoreType.DMA((4,)),
        ],
        compiler_params=limits(8),
        cost_estimate=cost(10**6, 4 * 10**6),
        name="expert_product",
    )(coef, *sums)


def finish_kernel(send_ref, own_ref, a_ref, b_ref, c_ref, d_ref, out_ref):
    atoms = own_ref.shape[1]
    face = send_ref.shape[1]
    row = lax.broadcasted_iota(jnp.int32, (atoms, face), 0)
    picks = []
    for side in range(2):
        even = lax.rem(lax.axis_index(("gx", "yz")[side]), 2) == 0
        below, above = send_ref[2 * side : 2 * side + 1, :], send_ref[2 * side + 1 : 2 * side + 2, :]
        for faces in (jnp.where(even, above, below), jnp.where(even, below, above)):
            picks.append((row == faces).astype(F32).astype(BF16))
    for c in range(9):
        total = own_ref[c]
        for pick, ref in zip(picks, (a_ref, b_ref, c_ref, d_ref)):
            at = ref.shape[0] - 9 * face + c * face
            total += nn(pick, ref[at : at + face])
        out_ref[c] = total.astype(BF16)


def finish(send, own, returned):
    return pl.pallas_call(
        finish_kernel,
        in_specs=[VMEM] * 6,
        out_specs=VMEM,
        out_shape=jax.ShapeDtypeStruct(own.shape, BF16),
        compiler_params=limits(6),
        cost_estimate=cost(10**8, 2 * 10**6),
        name="finish",
    )(send, own, *returned)


def swap(value, axis, bit):
    return lax.ppermute(value, axis, [(i, i ^ bit) for i in range(lax.axis_size(axis))])


def neighbour_pairs(value, axis, first):
    count = lax.axis_size(axis)
    moves = []
    for low in range(first, count, 2):
        high = (low + 1) % count
        moves += [(low, high), (high, low)]
    return lax.ppermute(value, axis, moves)


def local(
    saved_input, cotangent, neighbours, rot_zero, rot_one, rot_two, send_index, atom_class, live_blocks,
    merge_coef, experts,
):
    atoms, fanout = neighbours.shape
    slots = saved_input.shape[0]
    channels = cotangent.shape[2]
    face = send_index.shape[1]
    count_yz, count_gx = lax.axis_size("yz"), lax.axis_size("gx")
    row, column = lax.axis_index("yz"), lax.axis_index("gx")
    core = column % 2
    height = experts.shape[1] // 128
    rows = height * count_yz
    direct = height % 32 == 0 and count_yz == 4 and count_gx == 4

    zero = rot_zero.reshape(1, -1)
    source = jnp.transpose(saved_input, (1, 0, 2))
    target = jnp.transpose(cotangent, (1, 0, 2))

    alive = jnp.arange(atoms, dtype=jnp.int32) < live_blocks[0] * LIVE_BLOCK
    classes = jnp.where(alive, atom_class, -1).reshape(1, -1)
    merge_coef, classes = lax.optimization_barrier((merge_coef, classes))

    if direct:
        half = height // 2
        mine = merge(merge_coef, experts, 2)
        held = [mine] + [swap(mine, "yz", k) for k in (3, 2, 1)]
        source, target, mine = lax.optimization_barrier((source, target, mine))

        def places():
            here, side = lax.axis_index("yz"), lax.rem(lax.axis_index("gx"), 2)
            starts = [(here ^ k) * height for k in (0, 3, 2, 1)]
            return [at + side * half for at in starts] + [at + (1 - side) * half for at in starts]
    else:
        part = jnp.dot(merge_coef, experts.astype(F32), precision=lax.Precision.HIGHEST).astype(BF16)
        merged = lax.all_gather(part, "yz", axis=1, tiled=True)
        pieces = [merged.reshape(1, merged.shape[0], rows, 128)]

        def places():
            return [0]

    other, own, pulled, edge = features(
        neighbours.T, classes, zero, rot_one, rot_two, source, target, rows, fanout
    )
    if direct:
        other, *held = lax.optimization_barrier((other, *held))
        came = swap(other, "gx", 1)
        away, keep = core_sum(own, came)
        opposite = swap(away, "gx", 2)
        held = pack(held)
        pieces = [held, swap(held, "gx", 1)]
    grad_own, *ghosts = back(edge, zero, rot_one, rot_two, pulled, pieces, places, rows, atoms, slots, face)
    across_gx = [neighbour_pairs(ghosts[first], "gx", first) for first in range(2)]
    if direct:
        order = (3, 2, 1)
        parts = side_sum(keep, opposite, ghosts[2], ghosts[3], count_yz)
        gathered = [parts[0]] + [swap(parts[k], "yz", k) for k in order]
        summed, *across_gx = lax.optimization_barrier((total_sum(gathered), *across_gx))
        across = swap(summed, "gx", 2)
        input_grad = finish(send_index, grad_own, [*across_gx, gathered[3], gathered[1]])
        across, input_grad = lax.optimization_barrier((across, input_grad))
        sums = [summed, across, swap(summed, "gx", 1), swap(across, "gx", 1)]
    else:
        mixed = jnp.stack([own, other]).astype(F32)
        mixed = jnp.where(core == 0, mixed, mixed[::-1])
        whole = lax.psum(mixed, ("yz", "gx"))
        piece = lax.dynamic_slice_in_dim(whole, row * height, height, 1)
        piece = jnp.where(core == 0, piece, piece[::-1])
        sums = [piece[0], piece[1]]
        across_yz = [neighbour_pairs(ghosts[2 + first], "yz", first) for first in range(2)]
        input_grad = finish(send_index, grad_own, [*across_gx, *across_yz])
    grad_scale = math.sqrt(fanout / (atoms * count_yz * count_gx))
    expert_grad = expert_product(merge_coef, sums, merge_coef.shape[1] // count_gx, grad_scale)
    return (jnp.transpose(input_grad, (1, 0, 2)), expert_grad)


def solution(mesh):
    tiles = ("rep", "yz", "gx")
    in_specs = (
        P(tiles, None, None),
        P(tiles, None, None),
        P(tiles, None),
        P(tiles),
        P(None, None, tiles),
        P(None, None, tiles),
        P(tiles, None),
        P(tiles),
        P(tiles),
        P(),
        P(None, "yz"),
    )
    out_specs = (P(tiles, None, None), P(("rep", "gx"), "yz"))
    return jax.shard_map(local, mesh=mesh, in_specs=in_specs, out_specs=out_specs, check_vma=False)
```

```python
import functools
import math

import jax
import jax.numpy as jnp
from jax import lax
from jax.experimental import pallas as pl
from jax.experimental.pallas import tpu as pltpu
from jax.sharding import PartitionSpec as P

LIVE_BLOCK = 64
CHUNK = 256
SUB = 16
F32 = jnp.float32
BF16 = jnp.bfloat16

STACK = (0, 2, 6, 3, 7, 1, 5)
SLOT = {component: place for place, component in enumerate(STACK)}

VMEM = pl.BlockSpec(memory_space=pltpu.VMEM)
HBM = pl.BlockSpec(memory_space=pltpu.HBM)


def limits(mebibytes):
    return pltpu.CompilerParams(vmem_limit_bytes=mebibytes * 1024 * 1024)


def cost(flops, moved):
    return pl.CostEstimate(flops=flops, bytes_accessed=moved, transcendentals=0)


def nn(left, right):
    return lax.dot_general(left, right, (((1,), (0,)), ((), ())), preferred_element_type=F32)


def nt(left, right):
    return lax.dot_general(left, right, (((1,), (1,)), ((), ())), preferred_element_type=F32)


def split3(value):
    high = value.astype(BF16)
    rest = value - high.astype(F32)
    middle = rest.astype(BF16)
    low = (rest - middle.astype(F32)).astype(BF16)
    return high, middle, low


def merge_kernel(coef_in_ref, experts_ref, out_ref, held, coef_ref, arrived, coef_arrived):
    members, experts = coef_in_ref.shape
    rows = out_ref.shape[1]
    start = pl.multiple_of(lax.rem(lax.axis_index("gx"), 2) * rows * 128, 128)
    stripes = arrived.shape[0]
    blocks = rows // 16
    edges = [blocks * stripe // stripes for stripe in range(stripes + 1)]
    copies = []
    for stripe in range(stripes):
        at, wide = edges[stripe] * 2048, (edges[stripe + 1] - edges[stripe]) * 2048
        copies.append(
            pltpu.make_async_copy(
                experts_ref.at[:, pl.ds(start + at, wide)], held.at[:, pl.ds(at, wide)], arrived.at[stripe]
            )
        )
        copies[-1].start()
    coef_copy = pltpu.make_async_copy(coef_in_ref, coef_ref, coef_arrived)
    coef_copy.start()
    coef_copy.wait()
    wide = 8 * experts
    row = lax.broadcasted_iota(jnp.int32, (8, wide), 0)
    col = lax.broadcasted_iota(jnp.int32, (8, wide), 1)
    diagonal = row == col // experts
    source = lax.broadcasted_iota(jnp.int32, (experts, wide), 0)
    target = lax.broadcasted_iota(jnp.int32, (experts, wide), 1)
    tile = (source == target % experts).astype(F32).astype(BF16)
    lefts = []
    for term in split3(coef_ref[...]):
        tiled = nn(term, tile)
        for member in range(members):
            lefts.append(jnp.where(diagonal, tiled[member : member + 1, :], 0.0).astype(BF16))
    lefts = jnp.concatenate(lefts, axis=0)
    height = 8 * members
    for block in range(blocks):
        if block in edges:
            copies[edges.index(block)].wait()
        halves = []
        for half in range(2):
            first = block * 16 + half * 8
            groups = [held[:, (first + g) * 128 : (first + g + 1) * 128] for g in range(8)]
            halves.append(jnp.concatenate(groups, axis=0))
        product = nn(lefts, jnp.concatenate(halves, axis=1))
        total = product[:height] + product[height : 2 * height] + product[2 * height :]
        for member in range(members):
            part = total[member * 8 : member * 8 + 8]
            out_ref[member, block * 16 : block * 16 + 16, :] = jnp.concatenate(
                [part[:, :128], part[:, 128:]], axis=0
            ).astype(BF16)


def merge(coef, experts, parts):
    members, count = coef.shape
    columns = experts.shape[1] // parts
    rows = columns // 128
    return pl.pallas_call(
        merge_kernel,
        in_specs=[HBM, HBM],
        out_specs=VMEM,
        out_shape=jax.ShapeDtypeStruct((members, rows, 128), BF16),
        scratch_shapes=[
            pltpu.VMEM((count, columns), BF16),
            pltpu.VMEM((members, count), F32),
            pltpu.SemaphoreType.DMA((2,)),
            pltpu.SemaphoreType.DMA,
        ],
        compiler_params=limits(52),
        cost_estimate=cost(96 * 16 * columns, 2 * count * columns),
        name="merge",
    )(coef, experts)


def features_kernel(
    near_ref, class_ref, zero_ref, one_ref, two_ref, source_ref, target_ref,
    *refs, fanout, cuts,
):
    other_refs, own_ref, pulled_ref, edge_ref = refs[:cuts], *refs[cuts : cuts + 3]
    source_t, target_t, moved, spread, rotated, grads = refs[cuts + 3 :]
    slots, channels = source_ref.shape[1:]
    atoms = target_ref.shape[1]
    edges = atoms * fanout
    for c in range(9):
        source_t[c * channels : (c + 1) * channels, :] = source_ref[c].T
        target_t[c * channels : (c + 1) * channels, :] = target_ref[c].T
    near = near_ref[...].astype(F32).astype(BF16)
    classes = class_ref[...].astype(F32).astype(BF16)
    scale = 1.0 / math.sqrt(fanout)

    def chunk_step(chunk, carry):
        start = pl.multiple_of(chunk * CHUNK, CHUNK)
        here = pl.ds(start, CHUNK)
        edge = lax.broadcasted_iota(jnp.int32, (atoms, CHUNK), 1) + start
        atom = lax.broadcasted_iota(jnp.int32, (atoms, CHUNK), 0)
        repeat = (edge // fanout == atom).astype(F32).astype(BF16)
        edge8 = lax.broadcasted_iota(jnp.int32, (fanout, CHUNK), 1) + start
        lane8 = lax.broadcasted_iota(jnp.int32, (fanout, CHUNK), 0)
        picked = jnp.where(edge8 % fanout == lane8, nn(near, repeat), 0.0)
        near_row = jnp.sum(picked, axis=0, keepdims=True)
        class_row = nn(classes, repeat)
        edge_ref[0:1, here] = near_row
        edge_ref[1:2, here] = class_row
        slot = lax.broadcasted_iota(jnp.int32, (slots, CHUNK), 0).astype(F32)
        pick = (slot == near_row).astype(F32).astype(BF16)
        moved[...] = nn(source_t[...], pick)
        spread[...] = nn(target_t[...], repeat)

        def sub_step(sub, inner):
            at = pl.multiple_of(sub * SUB, SUB)

            def turn(field, write):
                def part(c):
                    return field[pl.ds(c * channels + at, SUB), :]

                write(0, zero_ref[0:1, here] * part(0))
                values = [part(c) for c in (1, 2, 3)]
                for a in range(3):
                    total = one_ref[a, 0:1, here] * values[0]
                    for b in range(1, 3):
                        total += one_ref[a, b : b + 1, here] * values[b]
                    write(1 + a, total)
                values = [part(c) for c in (4, 5, 6, 7, 8)]
                for a in range(1, 4):
                    total = two_ref[a, 0:1, here] * values[0]
                    for b in range(1, 5):
                        total += two_ref[a, b : b + 1, here] * values[b]
                    write(4 + a, total)

            def write_rotated(c, value):
                rotated[pl.ds(SLOT[c] * channels + at, SUB), here] = value.astype(BF16)

            def write_pulled(c, value):
                pulled_ref[pl.ds(SLOT[c] * channels + at, SUB), here] = (value * scale).astype(BF16)

            turn(moved, write_rotated)
            turn(spread, write_pulled)
            return inner

        lax.fori_loop(0, channels // SUB, sub_step, 0)
        return carry

    lax.fori_loop(0, edges // CHUNK, chunk_step, 0)
    zw, pw = 3 * channels, 2 * channels
    first = zw * zw // 128
    second = first + pw * pw // 128
    own = lax.rem(lax.axis_index("gx"), 2).astype(F32)
    for out_refs, wanted in ((other_refs, 1.0 - own), ((own_ref,), own)):
        mask = (edge_ref[1:2, :] == wanted).astype(F32).astype(BF16)
        qz = pulled_ref[0:zw, :] * mask
        qp = pulled_ref[zw : zw + pw, :] * mask
        qn = pulled_ref[zw + pw : zw + 2 * pw, :] * mask
        z, p, n = rotated[0:zw, :], rotated[zw : zw + pw, :], rotated[zw + pw : zw + 2 * pw, :]
        whole = nt(z, qz)
        for j in range(zw // 128):
            grads[pl.ds(j, zw, stride=zw // 128), :] = whole[:, j * 128 : (j + 1) * 128]
        coupled = nt(p, qp) + nt(n, qn)
        crossed = nt(p, qn) - nt(n, qp)
        for j in range(pw // 128):
            grads[pl.ds(first + j, pw, stride=pw // 128), :] = coupled[:, j * 128 : (j + 1) * 128]
            grads[pl.ds(second + j, pw, stride=pw // 128), :] = crossed[:, j * 128 : (j + 1) * 128]
        height = out_refs[0].shape[0]
        for index, out_ref in enumerate(out_refs):
            per = max(len(out_refs) // 4, 1)
            at = (lax.axis_index("yz") ^ (index // per)) * per * height + index % per * height
            at = pl.multiple_of(at, 16) if len(out_refs) > 1 else 0
            out_ref[...] = grads[pl.ds(at, height), :].astype(BF16)


def features(near, classes, zero, one, two, source, target, rows, fanout, cuts):
    slots, channels = source.shape[1:]
    atoms = target.shape[1]
    edges = atoms * fanout
    shape = jax.ShapeDtypeStruct
    return pl.pallas_call(
        functools.partial(features_kernel, fanout=fanout, cuts=cuts),
        in_specs=[VMEM] * 7,
        out_specs=[VMEM] * (cuts + 3),
        out_shape=[
            *[shape((rows // cuts, 128), BF16)] * cuts,
            shape((rows, 128), BF16),
            shape((7 * channels, edges), BF16),
            shape((8, edges), F32),
        ],
        scratch_shapes=[
            pltpu.VMEM((9 * channels, slots), BF16),
            pltpu.VMEM((9 * channels, atoms), BF16),
            pltpu.VMEM((9 * channels, CHUNK), F32),
            pltpu.VMEM((9 * channels, CHUNK), F32),
            pltpu.VMEM((7 * channels, edges), BF16),
            pltpu.VMEM((rows, 128), F32),
        ],
        compiler_params=limits(24),
        cost_estimate=cost(9 * 10**9, 7 * 10**6),
        name="features",
    )(near, classes, zero, one, two, source, target)


def back_kernel(
    edge_ref, zero_ref, one_ref, two_ref, pulled_ref, *rest, pieces, members, atoms, face, places,
):
    piece_refs = rest[:pieces]
    own_ref, *ghost_refs = rest[pieces : pieces + 5]
    flat, weight_zero, weight_pair, field, turned, pick_all = rest[pieces + 5 :]
    rows = flat.shape[1]
    channels = own_ref.shape[2]
    slots = pick_all.shape[0]
    edges = pulled_ref.shape[1]
    zw, pw = 3 * channels, 2 * channels
    first = zw * zw // 128
    second = first + pw * pw // 128
    placed = [(piece, index) for piece in piece_refs for index in range(piece.shape[0])]
    for (piece, index), place in zip(placed, places()):
        height = piece.shape[2]
        at = pl.ds(pl.multiple_of(place, 16), height)
        for k in range(members):
            flat[k, at, :] = piece[index, k].astype(F32)
    for k in range(members):
        for j in range(zw // 128):
            weight_zero[:, k * zw + j * 128 : k * zw + (j + 1) * 128] = flat[
                k, pl.ds(j, zw, stride=zw // 128), :
            ].astype(BF16)
        for j in range(pw // 128):
            at = k * 2 * pw + j * 128
            weight_pair[:, at : at + 128] = flat[k, pl.ds(first + j, pw, stride=pw // 128), :].astype(BF16)
            weight_pair[:, at + pw : at + pw + 128] = flat[
                k, pl.ds(second + j, pw, stride=pw // 128), :
            ].astype(BF16)

    def chunk_step(chunk, carry):
        start = pl.multiple_of(chunk * CHUNK, CHUNK)
        here = pl.ds(start, CHUNK)
        slot = lax.broadcasted_iota(jnp.int32, (slots, CHUNK), 0).astype(F32)
        pick_all[:, here] = (slot == edge_ref[0:1, here]).astype(F32).astype(BF16)
        qz, qpn, qnp = [], [], []
        for k in range(members):
            mask = (edge_ref[1:2, here] == float(k)).astype(F32).astype(BF16)
            qz.append(pulled_ref[0:zw, here] * mask)
            qp = pulled_ref[zw : zw + pw, here] * mask
            qn = pulled_ref[zw + pw : zw + 2 * pw, here] * mask
            qpn += [qp, qn]
            qnp += [qn, -qp]
        field[0:zw, :] = nn(weight_zero[...], jnp.concatenate(qz, axis=0))
        field[zw : zw + pw, :] = nn(weight_pair[...], jnp.concatenate(qpn, axis=0))
        field[zw + pw : zw + 2 * pw, :] = nn(weight_pair[...], jnp.concatenate(qnp, axis=0))

        def sub_step(sub, inner):
            at = pl.multiple_of(sub * SUB, SUB)

            def part(c):
                return field[pl.ds(SLOT[c] * channels + at, SUB), :]

            def write(c, value):
                turned[pl.ds(c * channels + at, SUB), here] = value.astype(BF16)

            write(0, zero_ref[0:1, here] * part(0))
            values = [part(c) for c in (1, 2, 3)]
            for b in range(3):
                total = one_ref[0, b : b + 1, here] * values[0]
                for a in range(1, 3):
                    total += one_ref[a, b : b + 1, here] * values[a]
                write(1 + b, total)
            values = [part(c) for c in (5, 6, 7)]
            for b in range(5):
                total = two_ref[1, b : b + 1, here] * values[0]
                for a in range(2, 4):
                    total += two_ref[a, b : b + 1, here] * values[a - 1]
                write(4 + b, total)
            return inner

        lax.fori_loop(0, channels // SUB, sub_step, 0)
        return carry

    lax.fori_loop(0, edges // CHUNK, chunk_step, 0)
    for c in range(9):
        summed = nt(pick_all[...], turned[c * channels : (c + 1) * channels, :])
        own_ref[c] = summed[:atoms]
        blocks = [summed[atoms + block * face : atoms + (block + 1) * face] for block in range(4)]
        for side in range(2):
            even = lax.rem(lax.axis_index(("gx", "yz")[side]), 2) == 0
            low, high = blocks[2 * side], blocks[2 * side + 1]
            ghost_refs[3 - side][c] = jnp.where(even, high, low).astype(BF16)
            ghost_refs[1 - side][c] = jnp.where(even, low, high).astype(BF16)


def back(edge, zero, one, two, pulled, pieces, places, rows, atoms, slots, face):
    members = pieces[0].shape[1]
    edges = pulled.shape[1]
    channels = pulled.shape[0] // 7
    shape = jax.ShapeDtypeStruct
    return pl.pallas_call(
        functools.partial(
            back_kernel, pieces=len(pieces), members=members, atoms=atoms, face=face, places=places
        ),
        in_specs=[VMEM] * (5 + len(pieces)),
        out_specs=[VMEM] * 5,
        out_shape=[shape((9, atoms, channels), F32), *[shape((9, face, channels), BF16)] * 4],
        scratch_shapes=[
            pltpu.VMEM((members, rows, 128), F32),
            pltpu.VMEM((3 * channels, members * 3 * channels), BF16),
            pltpu.VMEM((2 * channels, members * 4 * channels), BF16),
            pltpu.VMEM((7 * channels, CHUNK), F32),
            pltpu.VMEM((9 * channels, edges), BF16),
            pltpu.VMEM((slots, edges), BF16),
        ],
        compiler_params=limits(24),
        cost_estimate=cost(9 * 10**9, 7 * 10**6),
        name="back",
    )(edge, zero, one, two, pulled, *pieces)


def pair_kernel(own_ref, *refs, cuts):
    came_refs, out_refs = refs[:cuts], refs[cuts:]
    row = lax.axis_index("yz")
    per = cuts // len(out_refs)
    height = came_refs[0].shape[0]
    for index, came_ref in enumerate(came_refs):
        at = pl.multiple_of((row ^ (index // per)) * per * height + index % per * height, 16)
        total = own_ref[pl.ds(at, height), :].astype(F32) + came_ref[...].astype(F32)
        out_refs[index // per][pl.ds(index % per * height, height), :] = total.astype(BF16)


def pair_sum(own, came, count):
    height = own.shape[0] // count
    return pl.pallas_call(
        functools.partial(pair_kernel, cuts=len(came)),
        in_specs=[VMEM] * (1 + len(came)),
        out_specs=[VMEM] * count,
        out_shape=[jax.ShapeDtypeStruct((height, 128), BF16)] * count,
        compiler_params=limits(6),
        cost_estimate=cost(10**6, 2 * 10**6),
        name="pair_sum",
    )(own, *came)


def total_kernel(*refs):
    total = refs[0][...].astype(F32)
    for ref in refs[1:-1]:
        total += ref[...].astype(F32)
    refs[-1][...] = total.astype(BF16)


def total_sum(parts):
    return pl.pallas_call(
        total_kernel,
        in_specs=[VMEM] * len(parts),
        out_specs=VMEM,
        out_shape=jax.ShapeDtypeStruct(parts[0].shape, BF16),
        compiler_params=limits(6),
        cost_estimate=cost(10**6, 10**6),
        name="total_sum",
    )(*parts)


def pack_kernel(*refs):
    for index, ref in enumerate(refs[:-1]):
        refs[-1][index] = ref[...]


def pack(pieces):
    return pl.pallas_call(
        pack_kernel,
        in_specs=[VMEM] * len(pieces),
        out_specs=VMEM,
        out_shape=jax.ShapeDtypeStruct((len(pieces), *pieces[0].shape), pieces[0].dtype),
        compiler_params=limits(6),
        cost_estimate=cost(10**5, 10**6),
        name="pack",
    )(*pieces)


def expert_kernel(coef_ref, *refs, scale):
    sums, out_ref, summed, staged, written = refs[:-4], *refs[-4:]
    owned = out_ref.shape[0]
    place = lax.axis_index("gx")
    row = lax.broadcasted_iota(jnp.int32, (owned, coef_ref.shape[1]), 0)
    col = lax.broadcasted_iota(jnp.int32, (owned, coef_ref.shape[1]), 1)
    chosen = col == row + place * owned
    picked = [
        jnp.sum(jnp.where(chosen, coef_ref[k : k + 1, :], 0.0), axis=1, keepdims=True) * scale for k in range(2)
    ]
    even = lax.rem(place, 2) == 0
    first = jnp.broadcast_to(jnp.where(even, picked[0], picked[1]), (owned, 128))
    second = jnp.broadcast_to(jnp.where(even, picked[1], picked[0]), (owned, 128))
    half = len(sums) // 2
    for side in range(2):
        total = sums[side * half][...].astype(F32)
        for ref in sums[side * half + 1 : (side + 1) * half]:
            total += ref[...].astype(F32)
        summed[side] = total
    rows = summed.shape[1]
    stripes = written.shape[0]
    copies = []
    for stripe in range(stripes):
        low, high = rows * stripe // stripes, rows * (stripe + 1) // stripes
        for row in range(low, high):
            staged[:, row * 128 : (row + 1) * 128] = (
                first * summed[0, row : row + 1, :] + second * summed[1, row : row + 1, :]
            )
        span = pl.ds(low * 128, (high - low) * 128)
        copies.append(pltpu.make_async_copy(staged.at[:, span], out_ref.at[:, span], written.at[stripe]))
        copies[-1].start()
    for copy in copies:
        copy.wait()


def expert_product(coef, sums, owned, scale):
    rows = sums[0].shape[0]
    return pl.pallas_call(
        functools.partial(expert_kernel, scale=scale),
        in_specs=[VMEM] * (1 + len(sums)),
        out_specs=HBM,
        out_shape=jax.ShapeDtypeStruct((owned, rows * 128), F32),
        scratch_shapes=[
            pltpu.VMEM((2, rows, 128), F32),
            pltpu.VMEM((owned, rows * 128), F32),
            pltpu.SemaphoreType.DMA((4,)),
        ],
        compiler_params=limits(8),
        cost_estimate=cost(10**6, 4 * 10**6),
        name="expert_product",
    )(coef, *sums)


def finish_kernel(send_ref, own_ref, a_ref, b_ref, c_ref, d_ref, out_ref):
    atoms = own_ref.shape[1]
    face = send_ref.shape[1]
    row = lax.broadcasted_iota(jnp.int32, (atoms, face), 0)
    picks = []
    for side in range(2):
        even = lax.rem(lax.axis_index(("gx", "yz")[side]), 2) == 0
        below, above = send_ref[2 * side : 2 * side + 1, :], send_ref[2 * side + 1 : 2 * side + 2, :]
        for faces in (jnp.where(even, above, below), jnp.where(even, below, above)):
            picks.append((row == faces).astype(F32).astype(BF16))
    picks = [picks[3], picks[1], picks[2], picks[0]]
    for c in range(9):
        total = own_ref[c]
        for pick, ref in zip(picks, (a_ref, b_ref, c_ref, d_ref)):
            total += nn(pick, ref[c])
        out_ref[c] = total.astype(BF16)


def finish(send, own, returned):
    return pl.pallas_call(
        finish_kernel,
        in_specs=[VMEM] * 6,
        out_specs=VMEM,
        out_shape=jax.ShapeDtypeStruct(own.shape, BF16),
        compiler_params=limits(6),
        cost_estimate=cost(10**8, 2 * 10**6),
        name="finish",
    )(send, own, *returned)


def swap(value, axis, bit):
    return lax.ppermute(value, axis, [(i, i ^ bit) for i in range(lax.axis_size(axis))])


def neighbour_pairs(value, axis, first):
    count = lax.axis_size(axis)
    moves = []
    for low in range(first, count, 2):
        high = (low + 1) % count
        moves += [(low, high), (high, low)]
    return lax.ppermute(value, axis, moves)


def local(
    saved_input, cotangent, neighbours, rot_zero, rot_one, rot_two, send_index, atom_class, live_blocks,
    merge_coef, experts,
):
    atoms, fanout = neighbours.shape
    slots = saved_input.shape[0]
    channels = cotangent.shape[2]
    face = send_index.shape[1]
    count_yz, count_gx = lax.axis_size("yz"), lax.axis_size("gx")
    row, column = lax.axis_index("yz"), lax.axis_index("gx")
    core = column % 2
    height = experts.shape[1] // 128
    rows = height * count_yz
    direct = height % 32 == 0 and count_yz == 4 and count_gx == 4
    cuts = 4 if direct else 1

    zero = rot_zero.reshape(1, -1)
    source = jnp.transpose(saved_input, (1, 0, 2))
    target = jnp.transpose(cotangent, (1, 0, 2))

    alive = jnp.arange(atoms, dtype=jnp.int32) < live_blocks[0] * LIVE_BLOCK
    classes = jnp.where(alive, atom_class, -1).reshape(1, -1)
    experts, classes = lax.optimization_barrier((experts, classes))

    if direct:
        half = height // 2
        mine = merge(merge_coef, experts, 2)
        held = [mine] + [swap(mine, "yz", k) for k in range(1, count_yz)]
        source, target, mine = lax.optimization_barrier((source, target, mine))

        def places():
            here, side = lax.axis_index("yz"), lax.rem(lax.axis_index("gx"), 2)
            starts = [(here ^ k) * height for k in range(count_yz)]
            return [at + side * half for at in starts] + [at + (1 - side) * half for at in starts]
    else:
        part = jnp.dot(merge_coef, experts.astype(F32), precision=lax.Precision.HIGHEST).astype(BF16)
        merged = lax.all_gather(part, "yz", axis=1, tiled=True)
        pieces = [merged.reshape(1, merged.shape[0], rows, 128)]

        def places():
            return [0]

    *other, own, pulled, edge = features(
        neighbours.T, classes, zero, rot_one, rot_two, source, target, rows, fanout, cuts
    )
    if direct:
        came = [swap(piece, "gx", 1) for piece in other]
        received = lax.optimization_barrier((*came, *held))
        came, held = received[:cuts], received[cuts:]
        parts = pair_sum(own, came, count_yz)
        gathered = [parts[0]] + [swap(parts[k], "yz", k) for k in reversed(range(1, count_yz))]
        held = pack(held)
        pieces = [held, swap(held, "gx", 1)]
    grad_own, *ghosts = back(edge, zero, rot_one, rot_two, pulled, pieces, places, rows, atoms, slots, face)
    returned = [
        neighbour_pairs(ghost, axis, first)
        for ghost, axis, first in zip(ghosts, ("yz", "gx", "yz", "gx"), (1, 1, 0, 0))
    ]
    if direct:
        grad_own, *gathered = lax.optimization_barrier((grad_own, *gathered))
        summed, *returned = lax.optimization_barrier((total_sum(gathered), *returned))
        across = swap(summed, "gx", 2)
        input_grad = finish(send_index, grad_own, returned)
        across, input_grad = lax.optimization_barrier((across, input_grad))
        sums = [summed, across, swap(summed, "gx", 1), swap(across, "gx", 1)]
    else:
        mixed = jnp.stack([own, other[0]]).astype(F32)
        mixed = jnp.where(core == 0, mixed, mixed[::-1])
        whole = lax.psum(mixed, ("yz", "gx"))
        piece = lax.dynamic_slice_in_dim(whole, row * height, height, 1)
        piece = jnp.where(core == 0, piece, piece[::-1])
        sums = [piece[0], piece[1]]
        input_grad = finish(send_index, grad_own, returned)
    grad_scale = math.sqrt(fanout / (atoms * count_yz * count_gx))
    expert_grad = expert_product(merge_coef, sums, merge_coef.shape[1] // count_gx, grad_scale)
    return (jnp.transpose(input_grad, (1, 0, 2)), expert_grad)


def solution(mesh):
    tiles = ("rep", "yz", "gx")
    in_specs = (
        P(tiles, None, None),
        P(tiles, None, None),
        P(tiles, None),
        P(tiles),
        P(None, None, tiles),
        P(None, None, tiles),
        P(tiles, None),
        P(tiles),
        P(tiles),
        P(),
        P(None, "yz"),
    )
    out_specs = (P(tiles, None, None), P(("rep", "gx"), "yz"))
    return jax.shard_map(local, mesh=mesh, in_specs=in_specs, out_specs=out_specs, check_vma=False)
```

```python
import functools
import math

import jax
import jax.numpy as jnp
from jax import lax
from jax.experimental import pallas as pl
from jax.experimental.pallas import tpu as pltpu
from jax.sharding import PartitionSpec as P

LIVE_BLOCK = 64
CHUNK = 512
SUB = 32
F32 = jnp.float32
BF16 = jnp.bfloat16

STACK = (0, 2, 6, 3, 7, 1, 5)
SLOT = {component: place for place, component in enumerate(STACK)}

VMEM = pl.BlockSpec(memory_space=pltpu.VMEM)
HBM = pl.BlockSpec(memory_space=pltpu.HBM)


def limits(mebibytes):
    return pltpu.CompilerParams(vmem_limit_bytes=mebibytes * 1024 * 1024)


def cost(flops, moved):
    return pl.CostEstimate(flops=flops, bytes_accessed=moved, transcendentals=0)


def nn(left, right):
    return lax.dot_general(left, right, (((1,), (0,)), ((), ())), preferred_element_type=F32)


def nt(left, right):
    return lax.dot_general(left, right, (((1,), (1,)), ((), ())), preferred_element_type=F32)


def split3(value):
    high = value.astype(BF16)
    rest = value - high.astype(F32)
    middle = rest.astype(BF16)
    low = (rest - middle.astype(F32)).astype(BF16)
    return high, middle, low


def merge_kernel(coef_in_ref, experts_ref, out_ref, held, coef_ref, arrived, coef_arrived):
    members, experts = coef_in_ref.shape
    rows = out_ref.shape[1]
    start = pl.multiple_of(lax.rem(lax.axis_index("gx"), 2) * rows * 128, 128)
    stripes = arrived.shape[0]
    blocks = rows // 16
    edges = [blocks * stripe // stripes for stripe in range(stripes + 1)]
    copies = []
    for stripe in range(stripes):
        at, wide = edges[stripe] * 2048, (edges[stripe + 1] - edges[stripe]) * 2048
        copies.append(
            pltpu.make_async_copy(
                experts_ref.at[:, pl.ds(start + at, wide)], held.at[:, pl.ds(at, wide)], arrived.at[stripe]
            )
        )
        copies[-1].start()
    coef_copy = pltpu.make_async_copy(coef_in_ref, coef_ref, coef_arrived)
    coef_copy.start()
    coef_copy.wait()
    wide = 8 * experts
    row = lax.broadcasted_iota(jnp.int32, (8, wide), 0)
    col = lax.broadcasted_iota(jnp.int32, (8, wide), 1)
    diagonal = row == col // experts
    source = lax.broadcasted_iota(jnp.int32, (experts, wide), 0)
    target = lax.broadcasted_iota(jnp.int32, (experts, wide), 1)
    tile = (source == target % experts).astype(F32).astype(BF16)
    lefts = []
    for term in split3(coef_ref[...]):
        tiled = nn(term, tile)
        for member in range(members):
            lefts.append(jnp.where(diagonal, tiled[member : member + 1, :], 0.0).astype(BF16))
    lefts = jnp.concatenate(lefts, axis=0)
    height = 8 * members
    for block in range(blocks):
        if block in edges:
            copies[edges.index(block)].wait()
        halves = []
        for half in range(2):
            first = block * 16 + half * 8
            groups = [held[:, (first + g) * 128 : (first + g + 1) * 128] for g in range(8)]
            halves.append(jnp.concatenate(groups, axis=0))
        product = nn(lefts, jnp.concatenate(halves, axis=1))
        total = product[:height] + product[height : 2 * height] + product[2 * height :]
        for member in range(members):
            part = total[member * 8 : member * 8 + 8]
            out_ref[member, block * 16 : block * 16 + 16, :] = jnp.concatenate(
                [part[:, :128], part[:, 128:]], axis=0
            ).astype(BF16)


def merge(coef, experts, parts):
    members, count = coef.shape
    columns = experts.shape[1] // parts
    rows = columns // 128
    return pl.pallas_call(
        merge_kernel,
        in_specs=[HBM, HBM],
        out_specs=VMEM,
        out_shape=jax.ShapeDtypeStruct((members, rows, 128), BF16),
        scratch_shapes=[
            pltpu.VMEM((count, columns), BF16),
            pltpu.VMEM((members, count), F32),
            pltpu.SemaphoreType.DMA((2,)),
            pltpu.SemaphoreType.DMA,
        ],
        compiler_params=limits(52),
        cost_estimate=cost(96 * 16 * columns, 2 * count * columns),
        name="merge",
    )(coef, experts)


def features_kernel(
    live_in_ref, near_ref, class_ref, zero_ref, one_ref, two_ref, source_ref, target_ref,
    other_ref, own_ref, pulled_ref, edge_ref,
    source_t, target_t, moved, spread, rotated, grads, live_ref, live_arrived,
    *, fanout,
):
    slots, channels = source_ref.shape[1:]
    atoms = target_ref.shape[1]
    edges = atoms * fanout
    live_copy = pltpu.make_async_copy(live_in_ref, live_ref, live_arrived)
    live_copy.start()
    for c in range(9):
        source_t[c * channels : (c + 1) * channels, :] = source_ref[c].T
        target_t[c * channels : (c + 1) * channels, :] = target_ref[c].T
    near = near_ref[...].astype(F32).astype(BF16)
    classes = class_ref[...].astype(F32).astype(BF16)
    scale = 1.0 / math.sqrt(fanout)

    def chunk_step(chunk, carry):
        start = pl.multiple_of(chunk * CHUNK, CHUNK)
        here = pl.ds(start, CHUNK)
        edge = lax.broadcasted_iota(jnp.int32, (atoms, CHUNK), 1) + start
        atom = lax.broadcasted_iota(jnp.int32, (atoms, CHUNK), 0)
        repeat = (edge // fanout == atom).astype(F32).astype(BF16)
        edge8 = lax.broadcasted_iota(jnp.int32, (fanout, CHUNK), 1) + start
        lane8 = lax.broadcasted_iota(jnp.int32, (fanout, CHUNK), 0)
        picked = jnp.where(edge8 % fanout == lane8, nn(near, repeat), 0.0)
        near_row = jnp.sum(picked, axis=0, keepdims=True)
        class_row = nn(classes, repeat)
        edge_ref[0:1, here] = near_row
        edge_ref[1:2, here] = class_row
        slot = lax.broadcasted_iota(jnp.int32, (slots, CHUNK), 0).astype(F32)
        pick = (slot == near_row).astype(F32).astype(BF16)
        moved[...] = nn(source_t[...], pick)
        spread[...] = nn(target_t[...], repeat)

        def sub_step(sub, inner):
            at = pl.multiple_of(sub * SUB, SUB)

            def turn(field, write):
                def part(c):
                    return field[pl.ds(c * channels + at, SUB), :]

                write(0, zero_ref[0:1, here] * part(0))
                values = [part(c) for c in (1, 2, 3)]
                for a in range(3):
                    total = one_ref[a, 0:1, here] * values[0]
                    for b in range(1, 3):
                        total += one_ref[a, b : b + 1, here] * values[b]
                    write(1 + a, total)
                values = [part(c) for c in (4, 5, 6, 7, 8)]
                for a in range(1, 4):
                    total = two_ref[a, 0:1, here] * values[0]
                    for b in range(1, 5):
                        total += two_ref[a, b : b + 1, here] * values[b]
                    write(4 + a, total)

            def write_rotated(c, value):
                rotated[pl.ds(SLOT[c] * channels + at, SUB), here] = value.astype(BF16)

            def write_pulled(c, value):
                pulled_ref[pl.ds(SLOT[c] * channels + at, SUB), here] = (value * scale).astype(BF16)

            turn(moved, write_rotated)
            turn(spread, write_pulled)
            return inner

        lax.fori_loop(0, channels // SUB, sub_step, 0)
        return carry

    lax.fori_loop(0, edges // CHUNK, chunk_step, 0)
    live_copy.wait()
    edge_row = lax.broadcasted_iota(jnp.int32, (1, edges), 1)
    edge_ref[1:2, :] = jnp.where(edge_row < live_ref[0] * LIVE_BLOCK * fanout, edge_ref[1:2, :], -1.0)
    zw, pw = 3 * channels, 2 * channels
    first = zw * zw // 128
    second = first + pw * pw // 128
    own = lax.rem(lax.axis_index("gx"), 2).astype(F32)
    for out_ref, wanted in ((other_ref, 1.0 - own), (own_ref, own)):
        mask = (edge_ref[1:2, :] == wanted).astype(F32).astype(BF16)
        qz = pulled_ref[0:zw, :] * mask
        qp = pulled_ref[zw : zw + pw, :] * mask
        qn = pulled_ref[zw + pw : zw + 2 * pw, :] * mask
        z, p, n = rotated[0:zw, :], rotated[zw : zw + pw, :], rotated[zw + pw : zw + 2 * pw, :]
        whole = nt(z, qz)
        for j in range(zw // 128):
            grads[pl.ds(j, zw, stride=zw // 128), :] = whole[:, j * 128 : (j + 1) * 128]
        coupled = nt(p, qp) + nt(n, qn)
        crossed = nt(p, qn) - nt(n, qp)
        for j in range(pw // 128):
            grads[pl.ds(first + j, pw, stride=pw // 128), :] = coupled[:, j * 128 : (j + 1) * 128]
            grads[pl.ds(second + j, pw, stride=pw // 128), :] = crossed[:, j * 128 : (j + 1) * 128]
        out_ref[...] = grads[...].astype(BF16)


def features(live, near, classes, zero, one, two, source, target, rows, fanout):
    slots, channels = source.shape[1:]
    atoms = target.shape[1]
    edges = atoms * fanout
    shape = jax.ShapeDtypeStruct
    return pl.pallas_call(
        functools.partial(features_kernel, fanout=fanout),
        in_specs=[HBM] + [VMEM] * 7,
        out_specs=[VMEM] * 4,
        out_shape=[
            shape((rows, 128), BF16),
            shape((rows, 128), BF16),
            shape((7 * channels, edges), BF16),
            shape((8, edges), F32),
        ],
        scratch_shapes=[
            pltpu.VMEM((9 * channels, slots), BF16),
            pltpu.VMEM((9 * channels, atoms), BF16),
            pltpu.VMEM((9 * channels, CHUNK), F32),
            pltpu.VMEM((9 * channels, CHUNK), F32),
            pltpu.VMEM((7 * channels, edges), BF16),
            pltpu.VMEM((rows, 128), F32),
            pltpu.SMEM((1,), jnp.int32),
            pltpu.SemaphoreType.DMA,
        ],
        compiler_params=limits(24),
        cost_estimate=cost(9 * 10**9, 7 * 10**6),
        name="features",
    )(live, near, classes, zero, one, two, source, target)


def back_kernel(
    edge_ref, zero_ref, one_ref, two_ref, pulled_ref, *rest, pieces, members, atoms, face, places,
):
    piece_refs = rest[:pieces]
    own_ref, *ghost_refs = rest[pieces : pieces + 5]
    flat, weight_zero, weight_pair, field, turned, pick_all = rest[pieces + 5 :]
    rows = flat.shape[1]
    channels = own_ref.shape[2]
    slots = pick_all.shape[0]
    edges = pulled_ref.shape[1]
    zw, pw = 3 * channels, 2 * channels
    first = zw * zw // 128
    second = first + pw * pw // 128
    placed = [(piece, index) for piece in piece_refs for index in range(piece.shape[0])]
    for (piece, index), place in zip(placed, places()):
        height = piece.shape[2]
        at = pl.ds(pl.multiple_of(place, 16), height)
        for k in range(members):
            flat[k, at, :] = piece[index, k].astype(F32)
    for k in range(members):
        for j in range(zw // 128):
            weight_zero[:, k * zw + j * 128 : k * zw + (j + 1) * 128] = flat[
                k, pl.ds(j, zw, stride=zw // 128), :
            ].astype(BF16)
        for j in range(pw // 128):
            at = k * 2 * pw + j * 128
            weight_pair[:, at : at + 128] = flat[k, pl.ds(first + j, pw, stride=pw // 128), :].astype(BF16)
            weight_pair[:, at + pw : at + pw + 128] = flat[
                k, pl.ds(second + j, pw, stride=pw // 128), :
            ].astype(BF16)

    def chunk_step(chunk, carry):
        start = pl.multiple_of(chunk * CHUNK, CHUNK)
        here = pl.ds(start, CHUNK)
        slot = lax.broadcasted_iota(jnp.int32, (slots, CHUNK), 0).astype(F32)
        pick_all[:, here] = (slot == edge_ref[0:1, here]).astype(F32).astype(BF16)
        qz, qpn, qnp = [], [], []
        for k in range(members):
            mask = (edge_ref[1:2, here] == float(k)).astype(F32).astype(BF16)
            qz.append(pulled_ref[0:zw, here] * mask)
            qp = pulled_ref[zw : zw + pw, here] * mask
            qn = pulled_ref[zw + pw : zw + 2 * pw, here] * mask
            qpn += [qp, qn]
            qnp += [qn, -qp]
        field[0:zw, :] = nn(weight_zero[...], jnp.concatenate(qz, axis=0))
        field[zw : zw + pw, :] = nn(weight_pair[...], jnp.concatenate(qpn, axis=0))
        field[zw + pw : zw + 2 * pw, :] = nn(weight_pair[...], jnp.concatenate(qnp, axis=0))

        def sub_step(sub, inner):
            at = pl.multiple_of(sub * SUB, SUB)

            def part(c):
                return field[pl.ds(SLOT[c] * channels + at, SUB), :]

            def write(c, value):
                turned[pl.ds(c * channels + at, SUB), here] = value.astype(BF16)

            write(0, zero_ref[0:1, here] * part(0))
            values = [part(c) for c in (1, 2, 3)]
            for b in range(3):
                total = one_ref[0, b : b + 1, here] * values[0]
                for a in range(1, 3):
                    total += one_ref[a, b : b + 1, here] * values[a]
                write(1 + b, total)
            values = [part(c) for c in (5, 6, 7)]
            for b in range(5):
                total = two_ref[1, b : b + 1, here] * values[0]
                for a in range(2, 4):
                    total += two_ref[a, b : b + 1, here] * values[a - 1]
                write(4 + b, total)
            return inner

        lax.fori_loop(0, channels // SUB, sub_step, 0)
        return carry

    lax.fori_loop(0, edges // CHUNK, chunk_step, 0)
    for c in range(9):
        summed = nt(pick_all[...], turned[c * channels : (c + 1) * channels, :])
        own_ref[c] = summed[:atoms]
        blocks = [summed[atoms + block * face : atoms + (block + 1) * face] for block in range(4)]
        for side in range(2):
            even = lax.rem(lax.axis_index(("gx", "yz")[side]), 2) == 0
            low, high = blocks[2 * side], blocks[2 * side + 1]
            ghost_refs[3 - side][c] = jnp.where(even, high, low).astype(BF16)
            ghost_refs[1 - side][c] = jnp.where(even, low, high).astype(BF16)


def back(edge, zero, one, two, pulled, pieces, places, rows, atoms, slots, face):
    members = pieces[0].shape[1]
    edges = pulled.shape[1]
    channels = pulled.shape[0] // 7
    shape = jax.ShapeDtypeStruct
    return pl.pallas_call(
        functools.partial(
            back_kernel, pieces=len(pieces), members=members, atoms=atoms, face=face, places=places
        ),
        in_specs=[VMEM] * (5 + len(pieces)),
        out_specs=[VMEM] * 5,
        out_shape=[shape((9, atoms, channels), F32), *[shape((9, face, channels), BF16)] * 4],
        scratch_shapes=[
            pltpu.VMEM((members, rows, 128), F32),
            pltpu.VMEM((3 * channels, members * 3 * channels), BF16),
            pltpu.VMEM((2 * channels, members * 4 * channels), BF16),
            pltpu.VMEM((7 * channels, CHUNK), F32),
            pltpu.VMEM((9 * channels, edges), BF16),
            pltpu.VMEM((slots, edges), BF16),
        ],
        compiler_params=limits(24),
        cost_estimate=cost(9 * 10**9, 7 * 10**6),
        name="back",
    )(edge, zero, one, two, pulled, *pieces)


def pair_kernel(own_ref, came_ref, *out_refs):
    height = out_refs[0].shape[0]
    row = lax.axis_index("yz")
    for index, out_ref in enumerate(out_refs):
        at = pl.ds(pl.multiple_of((row ^ index) * height, 16), height)
        out_ref[...] = (own_ref[at, :].astype(F32) + came_ref[at, :].astype(F32)).astype(BF16)


def pair_sum(own, came, count):
    height = own.shape[0] // count
    return pl.pallas_call(
        pair_kernel,
        in_specs=[VMEM, VMEM],
        out_specs=[VMEM] * count,
        out_shape=[jax.ShapeDtypeStruct((height, 128), BF16)] * count,
        compiler_params=limits(6),
        cost_estimate=cost(10**6, 2 * 10**6),
        name="pair_sum",
    )(own, came)


def total_kernel(*refs):
    total = refs[0][...].astype(F32)
    for ref in refs[1:-1]:
        total += ref[...].astype(F32)
    refs[-1][...] = total.astype(BF16)


def total_sum(parts):
    return pl.pallas_call(
        total_kernel,
        in_specs=[VMEM] * len(parts),
        out_specs=VMEM,
        out_shape=jax.ShapeDtypeStruct(parts[0].shape, BF16),
        compiler_params=limits(6),
        cost_estimate=cost(10**6, 10**6),
        name="total_sum",
    )(*parts)


def pack_kernel(*refs):
    for index, ref in enumerate(refs[:-1]):
        refs[-1][index] = ref[...]


def pack(pieces):
    return pl.pallas_call(
        pack_kernel,
        in_specs=[VMEM] * len(pieces),
        out_specs=VMEM,
        out_shape=jax.ShapeDtypeStruct((len(pieces), *pieces[0].shape), pieces[0].dtype),
        compiler_params=limits(6),
        cost_estimate=cost(10**5, 10**6),
        name="pack",
    )(*pieces)


def expert_kernel(coef_ref, *refs, scale):
    sums, out_ref, summed, staged, written = refs[:-4], *refs[-4:]
    owned = out_ref.shape[0]
    place = lax.axis_index("gx")
    row = lax.broadcasted_iota(jnp.int32, (owned, coef_ref.shape[1]), 0)
    col = lax.broadcasted_iota(jnp.int32, (owned, coef_ref.shape[1]), 1)
    chosen = col == row + place * owned
    picked = [
        jnp.sum(jnp.where(chosen, coef_ref[k : k + 1, :], 0.0), axis=1, keepdims=True) * scale for k in range(2)
    ]
    even = lax.rem(place, 2) == 0
    first = jnp.broadcast_to(jnp.where(even, picked[0], picked[1]), (owned, 128))
    second = jnp.broadcast_to(jnp.where(even, picked[1], picked[0]), (owned, 128))
    half = len(sums) // 2
    for side in range(2):
        total = sums[side * half][...].astype(F32)
        for ref in sums[side * half + 1 : (side + 1) * half]:
            total += ref[...].astype(F32)
        summed[side] = total
    rows = summed.shape[1]
    stripes = written.shape[0]
    copies = []
    for stripe in range(stripes):
        low, high = rows * stripe // stripes, rows * (stripe + 1) // stripes
        for row in range(low, high):
            staged[:, row * 128 : (row + 1) * 128] = (
                first * summed[0, row : row + 1, :] + second * summed[1, row : row + 1, :]
            )
        span = pl.ds(low * 128, (high - low) * 128)
        copies.append(pltpu.make_async_copy(staged.at[:, span], out_ref.at[:, span], written.at[stripe]))
        copies[-1].start()
    for copy in copies:
        copy.wait()


def expert_product(coef, sums, owned, scale):
    rows = sums[0].shape[0]
    return pl.pallas_call(
        functools.partial(expert_kernel, scale=scale),
        in_specs=[VMEM] * (1 + len(sums)),
        out_specs=HBM,
        out_shape=jax.ShapeDtypeStruct((owned, rows * 128), F32),
        scratch_shapes=[
            pltpu.VMEM((2, rows, 128), F32),
            pltpu.VMEM((owned, rows * 128), F32),
            pltpu.SemaphoreType.DMA((4,)),
        ],
        compiler_params=limits(8),
        cost_estimate=cost(10**6, 4 * 10**6),
        name="expert_product",
    )(coef, *sums)


def finish_kernel(send_ref, own_ref, a_ref, b_ref, c_ref, d_ref, out_ref):
    atoms = own_ref.shape[1]
    face = send_ref.shape[1]
    row = lax.broadcasted_iota(jnp.int32, (atoms, face), 0)
    picks = []
    for side in range(2):
        even = lax.rem(lax.axis_index(("gx", "yz")[side]), 2) == 0
        below, above = send_ref[2 * side : 2 * side + 1, :], send_ref[2 * side + 1 : 2 * side + 2, :]
        for faces in (jnp.where(even, above, below), jnp.where(even, below, above)):
            picks.append((row == faces).astype(F32).astype(BF16))
    picks = [picks[3], picks[1], picks[2], picks[0]]
    for c in range(9):
        total = own_ref[c]
        for pick, ref in zip(picks, (a_ref, b_ref, c_ref, d_ref)):
            total += nn(pick, ref[c])
        out_ref[c] = total.astype(BF16)


def finish(send, own, returned):
    return pl.pallas_call(
        finish_kernel,
        in_specs=[VMEM] * 6,
        out_specs=VMEM,
        out_shape=jax.ShapeDtypeStruct(own.shape, BF16),
        compiler_params=limits(6),
        cost_estimate=cost(10**8, 2 * 10**6),
        name="finish",
    )(send, own, *returned)


def swap(value, axis, bit):
    return lax.ppermute(value, axis, [(i, i ^ bit) for i in range(lax.axis_size(axis))])


def neighbour_pairs(value, axis, first):
    count = lax.axis_size(axis)
    moves = []
    for low in range(first, count, 2):
        high = (low + 1) % count
        moves += [(low, high), (high, low)]
    return lax.ppermute(value, axis, moves)


def local(
    saved_input, cotangent, neighbours, rot_zero, rot_one, rot_two, send_index, atom_class, live_blocks,
    merge_coef, experts,
):
    atoms, fanout = neighbours.shape
    slots = saved_input.shape[0]
    channels = cotangent.shape[2]
    face = send_index.shape[1]
    count_yz, count_gx = lax.axis_size("yz"), lax.axis_size("gx")
    row, column = lax.axis_index("yz"), lax.axis_index("gx")
    core = column % 2
    height = experts.shape[1] // 128
    rows = height * count_yz
    direct = height % 32 == 0 and count_yz & (count_yz - 1) == 0 and count_gx == 4

    zero = rot_zero.reshape(1, -1)
    source = jnp.transpose(saved_input, (1, 0, 2))
    target = jnp.transpose(cotangent, (1, 0, 2))

    if direct:
        half = height // 2
        mine = merge(merge_coef, experts, 2)
        held = [mine] + [swap(mine, "yz", k) for k in range(1, count_yz)]
        source, target, mine = lax.optimization_barrier((source, target, mine))

        def places():
            here, side = lax.axis_index("yz"), lax.rem(lax.axis_index("gx"), 2)
            starts = [(here ^ k) * height for k in range(count_yz)]
            return [at + side * half for at in starts] + [at + (1 - side) * half for at in starts]
    else:
        part = jnp.dot(merge_coef, experts.astype(F32), precision=lax.Precision.HIGHEST).astype(BF16)
        merged = lax.all_gather(part, "yz", axis=1, tiled=True)
        pieces = [merged.reshape(1, merged.shape[0], rows, 128)]

        def places():
            return [0]

    other, own, pulled, edge = features(
        live_blocks, neighbours.T, atom_class.reshape(1, -1), zero, rot_one, rot_two, source, target, rows, fanout
    )
    if direct:
        other, *held = lax.optimization_barrier((other, *held))
        came = swap(other, "gx", 1)
        parts = pair_sum(own, came, count_yz)
        gathered = [parts[0]] + [swap(parts[k], "yz", k) for k in reversed(range(1, count_yz))]
        held = pack(held)
        pieces = [held, swap(held, "gx", 1)]
    grad_own, *ghosts = back(edge, zero, rot_one, rot_two, pulled, pieces, places, rows, atoms, slots, face)
    returned = [
        neighbour_pairs(ghost, axis, first)
        for ghost, axis, first in zip(ghosts, ("yz", "gx", "yz", "gx"), (1, 1, 0, 0))
    ]
    if direct:
        grad_own, *gathered = lax.optimization_barrier((grad_own, *gathered))
        summed, *returned = lax.optimization_barrier((total_sum(gathered), *returned))
        across = swap(summed, "gx", 2)
        input_grad = finish(send_index, grad_own, returned)
        across, input_grad = lax.optimization_barrier((across, input_grad))
        sums = [summed, across, swap(summed, "gx", 1), swap(across, "gx", 1)]
    else:
        mixed = jnp.stack([own, other]).astype(F32)
        mixed = jnp.where(core == 0, mixed, mixed[::-1])
        whole = lax.psum(mixed, ("yz", "gx"))
        piece = lax.dynamic_slice_in_dim(whole, row * height, height, 1)
        piece = jnp.where(core == 0, piece, piece[::-1])
        sums = [piece[0], piece[1]]
        input_grad = finish(send_index, grad_own, returned)
    grad_scale = math.sqrt(fanout / (atoms * count_yz * count_gx))
    expert_grad = expert_product(merge_coef, sums, merge_coef.shape[1] // count_gx, grad_scale)
    return (jnp.transpose(input_grad, (1, 0, 2)), expert_grad)


def solution(mesh):
    tiles = ("rep", "yz", "gx")
    in_specs = (
        P(tiles, None, None),
        P(tiles, None, None),
        P(tiles, None),
        P(tiles),
        P(None, None, tiles),
        P(None, None, tiles),
        P(tiles, None),
        P(tiles),
        P(tiles),
        P(),
        P(None, "yz"),
    )
    out_specs = (P(tiles, None, None), P(("rep", "gx"), "yz"))
    return jax.shard_map(local, mesh=mesh, in_specs=in_specs, out_specs=out_specs, check_vma=False)
```

```python
import functools
import math

import jax
import jax.numpy as jnp
from jax import lax
from jax.experimental import pallas as pl
from jax.experimental.pallas import tpu as pltpu
from jax.sharding import PartitionSpec as P

LIVE_BLOCK = 64
CHUNK = 512
SUB = 32
F32 = jnp.float32
BF16 = jnp.bfloat16

STACK = (0, 2, 6, 3, 7, 1, 5)
SLOT = {component: place for place, component in enumerate(STACK)}

VMEM = pl.BlockSpec(memory_space=pltpu.VMEM)
HBM = pl.BlockSpec(memory_space=pltpu.HBM)


def limits(mebibytes):
    return pltpu.CompilerParams(vmem_limit_bytes=mebibytes * 1024 * 1024)


def cost(flops, moved):
    return pl.CostEstimate(flops=flops, bytes_accessed=moved, transcendentals=0)


def nn(left, right):
    return lax.dot_general(left, right, (((1,), (0,)), ((), ())), preferred_element_type=F32)


def nt(left, right):
    return lax.dot_general(left, right, (((1,), (1,)), ((), ())), preferred_element_type=F32)


def split3(value):
    high = value.astype(BF16)
    rest = value - high.astype(F32)
    middle = rest.astype(BF16)
    low = (rest - middle.astype(F32)).astype(BF16)
    return high, middle, low


def merge_kernel(coef_in_ref, experts_ref, out_ref, held, coef_ref, arrived, coef_arrived):
    members, experts = coef_in_ref.shape
    rows = out_ref.shape[1]
    start = pl.multiple_of(lax.rem(lax.axis_index("gx"), 2) * rows * 128, 128)
    stripes = arrived.shape[0]
    blocks = rows // 16
    edges = [blocks * stripe // stripes for stripe in range(stripes + 1)]
    copies = []
    for stripe in range(stripes):
        at, wide = edges[stripe] * 2048, (edges[stripe + 1] - edges[stripe]) * 2048
        copies.append(
            pltpu.make_async_copy(
                experts_ref.at[:, pl.ds(start + at, wide)], held.at[:, pl.ds(at, wide)], arrived.at[stripe]
            )
        )
        copies[-1].start()
    coef_copy = pltpu.make_async_copy(coef_in_ref, coef_ref, coef_arrived)
    coef_copy.start()
    coef_copy.wait()
    wide = 8 * experts
    row = lax.broadcasted_iota(jnp.int32, (8, wide), 0)
    col = lax.broadcasted_iota(jnp.int32, (8, wide), 1)
    diagonal = row == col // experts
    source = lax.broadcasted_iota(jnp.int32, (experts, wide), 0)
    target = lax.broadcasted_iota(jnp.int32, (experts, wide), 1)
    tile = (source == target % experts).astype(F32).astype(BF16)
    lefts = []
    for term in split3(coef_ref[...]):
        tiled = nn(term, tile)
        for member in range(members):
            lefts.append(jnp.where(diagonal, tiled[member : member + 1, :], 0.0).astype(BF16))
    lefts = jnp.concatenate(lefts, axis=0)
    height = 8 * members
    for block in range(blocks):
        if block in edges:
            copies[edges.index(block)].wait()
        halves = []
        for half in range(2):
            first = block * 16 + half * 8
            groups = [held[:, (first + g) * 128 : (first + g + 1) * 128] for g in range(8)]
            halves.append(jnp.concatenate(groups, axis=0))
        product = nn(lefts, jnp.concatenate(halves, axis=1))
        total = product[:height] + product[height : 2 * height] + product[2 * height :]
        for member in range(members):
            part = total[member * 8 : member * 8 + 8]
            out_ref[member, block * 16 : block * 16 + 16, :] = jnp.concatenate(
                [part[:, :128], part[:, 128:]], axis=0
            ).astype(BF16)


def merge(coef, experts, parts):
    members, count = coef.shape
    columns = experts.shape[1] // parts
    rows = columns // 128
    return pl.pallas_call(
        merge_kernel,
        in_specs=[HBM, HBM],
        out_specs=VMEM,
        out_shape=jax.ShapeDtypeStruct((members, rows, 128), BF16),
        scratch_shapes=[
            pltpu.VMEM((count, columns), BF16),
            pltpu.VMEM((members, count), F32),
            pltpu.SemaphoreType.DMA((2,)),
            pltpu.SemaphoreType.DMA,
        ],
        compiler_params=limits(52),
        cost_estimate=cost(96 * 16 * columns, 2 * count * columns),
        name="merge",
    )(coef, experts)


def features_kernel(
    live_in_ref, near_ref, class_ref, zero_ref, one_ref, two_ref, source_ref, target_ref,
    *refs, fanout, cuts,
):
    other_refs, own_ref, pulled_ref, edge_ref = refs[:cuts], *refs[cuts : cuts + 3]
    source_t, target_t, moved, spread, rotated, grads, live_ref, live_arrived = refs[cuts + 3 :]
    slots, channels = source_ref.shape[1:]
    atoms = target_ref.shape[1]
    edges = atoms * fanout
    live_copy = pltpu.make_async_copy(live_in_ref, live_ref, live_arrived)
    live_copy.start()
    for c in range(9):
        source_t[c * channels : (c + 1) * channels, :] = source_ref[c].T
        target_t[c * channels : (c + 1) * channels, :] = target_ref[c].T
    near = near_ref[...].astype(F32).astype(BF16)
    classes = class_ref[...].astype(F32).astype(BF16)
    scale = 1.0 / math.sqrt(fanout)

    def chunk_step(chunk, carry):
        start = pl.multiple_of(chunk * CHUNK, CHUNK)
        here = pl.ds(start, CHUNK)
        edge = lax.broadcasted_iota(jnp.int32, (atoms, CHUNK), 1) + start
        atom = lax.broadcasted_iota(jnp.int32, (atoms, CHUNK), 0)
        repeat = (edge // fanout == atom).astype(F32).astype(BF16)
        edge8 = lax.broadcasted_iota(jnp.int32, (fanout, CHUNK), 1) + start
        lane8 = lax.broadcasted_iota(jnp.int32, (fanout, CHUNK), 0)
        picked = jnp.where(edge8 % fanout == lane8, nn(near, repeat), 0.0)
        near_row = jnp.sum(picked, axis=0, keepdims=True)
        class_row = nn(classes, repeat)
        edge_ref[0:1, here] = near_row
        edge_ref[1:2, here] = class_row
        slot = lax.broadcasted_iota(jnp.int32, (slots, CHUNK), 0).astype(F32)
        pick = (slot == near_row).astype(F32).astype(BF16)
        moved[...] = nn(source_t[...], pick)
        spread[...] = nn(target_t[...], repeat)

        def sub_step(sub, inner):
            at = pl.multiple_of(sub * SUB, SUB)

            def turn(field, write):
                def part(c):
                    return field[pl.ds(c * channels + at, SUB), :]

                write(0, zero_ref[0:1, here] * part(0))
                values = [part(c) for c in (1, 2, 3)]
                for a in range(3):
                    total = one_ref[a, 0:1, here] * values[0]
                    for b in range(1, 3):
                        total += one_ref[a, b : b + 1, here] * values[b]
                    write(1 + a, total)
                values = [part(c) for c in (4, 5, 6, 7, 8)]
                for a in range(1, 4):
                    total = two_ref[a, 0:1, here] * values[0]
                    for b in range(1, 5):
                        total += two_ref[a, b : b + 1, here] * values[b]
                    write(4 + a, total)

            def write_rotated(c, value):
                rotated[pl.ds(SLOT[c] * channels + at, SUB), here] = value.astype(BF16)

            def write_pulled(c, value):
                pulled_ref[pl.ds(SLOT[c] * channels + at, SUB), here] = (value * scale).astype(BF16)

            turn(moved, write_rotated)
            turn(spread, write_pulled)
            return inner

        lax.fori_loop(0, channels // SUB, sub_step, 0)
        return carry

    lax.fori_loop(0, edges // CHUNK, chunk_step, 0)
    live_copy.wait()
    edge_row = lax.broadcasted_iota(jnp.int32, (1, edges), 1)
    edge_ref[1:2, :] = jnp.where(edge_row < live_ref[0] * LIVE_BLOCK * fanout, edge_ref[1:2, :], -1.0)
    zw, pw = 3 * channels, 2 * channels
    first = zw * zw // 128
    second = first + pw * pw // 128
    own = lax.rem(lax.axis_index("gx"), 2).astype(F32)
    for out_refs, wanted in ((other_refs, 1.0 - own), ((own_ref,), own)):
        mask = (edge_ref[1:2, :] == wanted).astype(F32).astype(BF16)
        qz = pulled_ref[0:zw, :] * mask
        qp = pulled_ref[zw : zw + pw, :] * mask
        qn = pulled_ref[zw + pw : zw + 2 * pw, :] * mask
        z, p, n = rotated[0:zw, :], rotated[zw : zw + pw, :], rotated[zw + pw : zw + 2 * pw, :]
        whole = nt(z, qz)
        for j in range(zw // 128):
            grads[pl.ds(j, zw, stride=zw // 128), :] = whole[:, j * 128 : (j + 1) * 128]
        coupled = nt(p, qp) + nt(n, qn)
        crossed = nt(p, qn) - nt(n, qp)
        for j in range(pw // 128):
            grads[pl.ds(first + j, pw, stride=pw // 128), :] = coupled[:, j * 128 : (j + 1) * 128]
            grads[pl.ds(second + j, pw, stride=pw // 128), :] = crossed[:, j * 128 : (j + 1) * 128]
        height = out_refs[0].shape[0]
        for index, out_ref in enumerate(out_refs):
            per = max(len(out_refs) // 4, 1)
            at = (lax.axis_index("yz") ^ (index // per)) * per * height + index % per * height
            at = pl.multiple_of(at, 16) if len(out_refs) > 1 else 0
            out_ref[...] = grads[pl.ds(at, height), :].astype(BF16)


def features(live, near, classes, zero, one, two, source, target, rows, fanout, cuts):
    slots, channels = source.shape[1:]
    atoms = target.shape[1]
    edges = atoms * fanout
    shape = jax.ShapeDtypeStruct
    return pl.pallas_call(
        functools.partial(features_kernel, fanout=fanout, cuts=cuts),
        in_specs=[HBM] + [VMEM] * 7,
        out_specs=[VMEM] * (cuts + 3),
        out_shape=[
            *[shape((rows // cuts, 128), BF16)] * cuts,
            shape((rows, 128), BF16),
            shape((7 * channels, edges), BF16),
            shape((8, edges), F32),
        ],
        scratch_shapes=[
            pltpu.VMEM((9 * channels, slots), BF16),
            pltpu.VMEM((9 * channels, atoms), BF16),
            pltpu.VMEM((9 * channels, CHUNK), F32),
            pltpu.VMEM((9 * channels, CHUNK), F32),
            pltpu.VMEM((7 * channels, edges), BF16),
            pltpu.VMEM((rows, 128), F32),
            pltpu.SMEM((1,), jnp.int32),
            pltpu.SemaphoreType.DMA,
        ],
        compiler_params=limits(24),
        cost_estimate=cost(9 * 10**9, 7 * 10**6),
        name="features",
    )(live, near, classes, zero, one, two, source, target)


def back_kernel(
    edge_ref, zero_ref, one_ref, two_ref, pulled_ref, *rest, pieces, members, atoms, face, places,
):
    piece_refs = rest[:pieces]
    own_ref, *ghost_refs = rest[pieces : pieces + 5]
    flat, weight_zero, weight_pair, field, turned, pick_all = rest[pieces + 5 :]
    rows = flat.shape[1]
    channels = own_ref.shape[2]
    slots = pick_all.shape[0]
    edges = pulled_ref.shape[1]
    zw, pw = 3 * channels, 2 * channels
    first = zw * zw // 128
    second = first + pw * pw // 128
    placed = [(piece, index) for piece in piece_refs for index in range(piece.shape[0])]
    for (piece, index), place in zip(placed, places()):
        height = piece.shape[2]
        at = pl.ds(pl.multiple_of(place, 16), height)
        for k in range(members):
            flat[k, at, :] = piece[index, k].astype(F32)
    for k in range(members):
        for j in range(zw // 128):
            weight_zero[:, k * zw + j * 128 : k * zw + (j + 1) * 128] = flat[
                k, pl.ds(j, zw, stride=zw // 128), :
            ].astype(BF16)
        for j in range(pw // 128):
            at = k * 2 * pw + j * 128
            weight_pair[:, at : at + 128] = flat[k, pl.ds(first + j, pw, stride=pw // 128), :].astype(BF16)
            weight_pair[:, at + pw : at + pw + 128] = flat[
                k, pl.ds(second + j, pw, stride=pw // 128), :
            ].astype(BF16)

    def chunk_step(chunk, carry):
        start = pl.multiple_of(chunk * CHUNK, CHUNK)
        here = pl.ds(start, CHUNK)
        slot = lax.broadcasted_iota(jnp.int32, (slots, CHUNK), 0).astype(F32)
        pick_all[:, here] = (slot == edge_ref[0:1, here]).astype(F32).astype(BF16)
        qz, qpn, qnp = [], [], []
        for k in range(members):
            mask = (edge_ref[1:2, here] == float(k)).astype(F32).astype(BF16)
            qz.append(pulled_ref[0:zw, here] * mask)
            qp = pulled_ref[zw : zw + pw, here] * mask
            qn = pulled_ref[zw + pw : zw + 2 * pw, here] * mask
            qpn += [qp, qn]
            qnp += [qn, -qp]
        field[0:zw, :] = nn(weight_zero[...], jnp.concatenate(qz, axis=0))
        field[zw : zw + pw, :] = nn(weight_pair[...], jnp.concatenate(qpn, axis=0))
        field[zw + pw : zw + 2 * pw, :] = nn(weight_pair[...], jnp.concatenate(qnp, axis=0))

        def sub_step(sub, inner):
            at = pl.multiple_of(sub * SUB, SUB)

            def part(c):
                return field[pl.ds(SLOT[c] * channels + at, SUB), :]

            def write(c, value):
                turned[pl.ds(c * channels + at, SUB), here] = value.astype(BF16)

            write(0, zero_ref[0:1, here] * part(0))
            values = [part(c) for c in (1, 2, 3)]
            for b in range(3):
                total = one_ref[0, b : b + 1, here] * values[0]
                for a in range(1, 3):
                    total += one_ref[a, b : b + 1, here] * values[a]
                write(1 + b, total)
            values = [part(c) for c in (5, 6, 7)]
            for b in range(5):
                total = two_ref[1, b : b + 1, here] * values[0]
                for a in range(2, 4):
                    total += two_ref[a, b : b + 1, here] * values[a - 1]
                write(4 + b, total)
            return inner

        lax.fori_loop(0, channels // SUB, sub_step, 0)
        return carry

    lax.fori_loop(0, edges // CHUNK, chunk_step, 0)
    for c in range(9):
        summed = nt(pick_all[...], turned[c * channels : (c + 1) * channels, :])
        own_ref[c] = summed[:atoms]
        blocks = [summed[atoms + block * face : atoms + (block + 1) * face] for block in range(4)]
        for side in range(2):
            even = lax.rem(lax.axis_index(("gx", "yz")[side]), 2) == 0
            low, high = blocks[2 * side], blocks[2 * side + 1]
            ghost_refs[3 - side][c] = jnp.where(even, high, low).astype(BF16)
            ghost_refs[1 - side][c] = jnp.where(even, low, high).astype(BF16)


def back(edge, zero, one, two, pulled, pieces, places, rows, atoms, slots, face):
    members = pieces[0].shape[1]
    edges = pulled.shape[1]
    channels = pulled.shape[0] // 7
    shape = jax.ShapeDtypeStruct
    return pl.pallas_call(
        functools.partial(
            back_kernel, pieces=len(pieces), members=members, atoms=atoms, face=face, places=places
        ),
        in_specs=[VMEM] * (5 + len(pieces)),
        out_specs=[VMEM] * 5,
        out_shape=[shape((9, atoms, channels), F32), *[shape((9, face, channels), BF16)] * 4],
        scratch_shapes=[
            pltpu.VMEM((members, rows, 128), F32),
            pltpu.VMEM((3 * channels, members * 3 * channels), BF16),
            pltpu.VMEM((2 * channels, members * 4 * channels), BF16),
            pltpu.VMEM((7 * channels, CHUNK), F32),
            pltpu.VMEM((9 * channels, edges), BF16),
            pltpu.VMEM((slots, edges), BF16),
        ],
        compiler_params=limits(24),
        cost_estimate=cost(9 * 10**9, 7 * 10**6),
        name="back",
    )(edge, zero, one, two, pulled, *pieces)


def pair_kernel(own_ref, *refs, cuts):
    came_refs, out_refs = refs[:cuts], refs[cuts:]
    row = lax.axis_index("yz")
    per = cuts // len(out_refs)
    height = came_refs[0].shape[0]
    for index, came_ref in enumerate(came_refs):
        at = pl.multiple_of((row ^ (index // per)) * per * height + index % per * height, 16)
        total = own_ref[pl.ds(at, height), :].astype(F32) + came_ref[...].astype(F32)
        out_refs[index // per][pl.ds(index % per * height, height), :] = total.astype(BF16)


def pair_sum(own, came, count):
    height = own.shape[0] // count
    return pl.pallas_call(
        functools.partial(pair_kernel, cuts=len(came)),
        in_specs=[VMEM] * (1 + len(came)),
        out_specs=[VMEM] * count,
        out_shape=[jax.ShapeDtypeStruct((height, 128), BF16)] * count,
        compiler_params=limits(6),
        cost_estimate=cost(10**6, 2 * 10**6),
        name="pair_sum",
    )(own, *came)


def total_kernel(*refs):
    total = refs[0][...].astype(F32)
    for ref in refs[1:-1]:
        total += ref[...].astype(F32)
    refs[-1][...] = total.astype(BF16)


def total_sum(parts):
    return pl.pallas_call(
        total_kernel,
        in_specs=[VMEM] * len(parts),
        out_specs=VMEM,
        out_shape=jax.ShapeDtypeStruct(parts[0].shape, BF16),
        compiler_params=limits(6),
        cost_estimate=cost(10**6, 10**6),
        name="total_sum",
    )(*parts)


def pack_kernel(*refs):
    for index, ref in enumerate(refs[:-1]):
        refs[-1][index] = ref[...]


def pack(pieces):
    return pl.pallas_call(
        pack_kernel,
        in_specs=[VMEM] * len(pieces),
        out_specs=VMEM,
        out_shape=jax.ShapeDtypeStruct((len(pieces), *pieces[0].shape), pieces[0].dtype),
        compiler_params=limits(6),
        cost_estimate=cost(10**5, 10**6),
        name="pack",
    )(*pieces)


def expert_kernel(coef_ref, *refs, scale):
    sums, out_ref, summed, staged, written = refs[:-4], *refs[-4:]
    owned = out_ref.shape[0]
    place = lax.axis_index("gx")
    row = lax.broadcasted_iota(jnp.int32, (owned, coef_ref.shape[1]), 0)
    col = lax.broadcasted_iota(jnp.int32, (owned, coef_ref.shape[1]), 1)
    chosen = col == row + place * owned
    picked = [
        jnp.sum(jnp.where(chosen, coef_ref[k : k + 1, :], 0.0), axis=1, keepdims=True) * scale for k in range(2)
    ]
    even = lax.rem(place, 2) == 0
    first = jnp.broadcast_to(jnp.where(even, picked[0], picked[1]), (owned, 128))
    second = jnp.broadcast_to(jnp.where(even, picked[1], picked[0]), (owned, 128))
    half = len(sums) // 2
    for side in range(2):
        total = sums[side * half][...].astype(F32)
        for ref in sums[side * half + 1 : (side + 1) * half]:
            total += ref[...].astype(F32)
        summed[side] = total
    rows = summed.shape[1]
    stripes = written.shape[0]
    copies = []
    for stripe in range(stripes):
        low, high = rows * stripe // stripes, rows * (stripe + 1) // stripes
        for row in range(low, high):
            staged[:, row * 128 : (row + 1) * 128] = (
                first * summed[0, row : row + 1, :] + second * summed[1, row : row + 1, :]
            )
        span = pl.ds(low * 128, (high - low) * 128)
        copies.append(pltpu.make_async_copy(staged.at[:, span], out_ref.at[:, span], written.at[stripe]))
        copies[-1].start()
    for copy in copies:
        copy.wait()


def expert_product(coef, sums, owned, scale):
    rows = sums[0].shape[0]
    return pl.pallas_call(
        functools.partial(expert_kernel, scale=scale),
        in_specs=[VMEM] * (1 + len(sums)),
        out_specs=HBM,
        out_shape=jax.ShapeDtypeStruct((owned, rows * 128), F32),
        scratch_shapes=[
            pltpu.VMEM((2, rows, 128), F32),
            pltpu.VMEM((owned, rows * 128), F32),
            pltpu.SemaphoreType.DMA((4,)),
        ],
        compiler_params=limits(8),
        cost_estimate=cost(10**6, 4 * 10**6),
        name="expert_product",
    )(coef, *sums)


def finish_kernel(send_ref, own_ref, a_ref, b_ref, c_ref, d_ref, out_ref):
    atoms = own_ref.shape[1]
    face = send_ref.shape[1]
    row = lax.broadcasted_iota(jnp.int32, (atoms, face), 0)
    picks = []
    for side in range(2):
        even = lax.rem(lax.axis_index(("gx", "yz")[side]), 2) == 0
        below, above = send_ref[2 * side : 2 * side + 1, :], send_ref[2 * side + 1 : 2 * side + 2, :]
        for faces in (jnp.where(even, above, below), jnp.where(even, below, above)):
            picks.append((row == faces).astype(F32).astype(BF16))
    picks = [picks[3], picks[1], picks[2], picks[0]]
    for c in range(9):
        total = own_ref[c]
        for pick, ref in zip(picks, (a_ref, b_ref, c_ref, d_ref)):
            total += nn(pick, ref[c])
        out_ref[c] = total.astype(BF16)


def finish(send, own, returned):
    return pl.pallas_call(
        finish_kernel,
        in_specs=[VMEM] * 6,
        out_specs=VMEM,
        out_shape=jax.ShapeDtypeStruct(own.shape, BF16),
        compiler_params=limits(6),
        cost_estimate=cost(10**8, 2 * 10**6),
        name="finish",
    )(send, own, *returned)


def swap(value, axis, bit):
    return lax.ppermute(value, axis, [(i, i ^ bit) for i in range(lax.axis_size(axis))])


def neighbour_pairs(value, axis, first):
    count = lax.axis_size(axis)
    moves = []
    for low in range(first, count, 2):
        high = (low + 1) % count
        moves += [(low, high), (high, low)]
    return lax.ppermute(value, axis, moves)


def local(
    saved_input, cotangent, neighbours, rot_zero, rot_one, rot_two, send_index, atom_class, live_blocks,
    merge_coef, experts,
):
    atoms, fanout = neighbours.shape
    slots = saved_input.shape[0]
    channels = cotangent.shape[2]
    face = send_index.shape[1]
    count_yz, count_gx = lax.axis_size("yz"), lax.axis_size("gx")
    row, column = lax.axis_index("yz"), lax.axis_index("gx")
    core = column % 2
    height = experts.shape[1] // 128
    rows = height * count_yz
    direct = height % 32 == 0 and count_yz == 4 and count_gx == 4
    cuts = 4 if direct else 1

    zero = rot_zero.reshape(1, -1)
    source = jnp.transpose(saved_input, (1, 0, 2))
    target = jnp.transpose(cotangent, (1, 0, 2))

    if direct:
        half = height // 2
        mine = merge(merge_coef, experts, 2)
        held = [mine] + [swap(mine, "yz", k) for k in (2, 1, 3)]
        source, target, mine = lax.optimization_barrier((source, target, mine))

        def places():
            here, side = lax.axis_index("yz"), lax.rem(lax.axis_index("gx"), 2)
            starts = [(here ^ k) * height for k in (0, 2, 1, 3)]
            return [at + side * half for at in starts] + [at + (1 - side) * half for at in starts]
    else:
        part = jnp.dot(merge_coef, experts.astype(F32), precision=lax.Precision.HIGHEST).astype(BF16)
        merged = lax.all_gather(part, "yz", axis=1, tiled=True)
        pieces = [merged.reshape(1, merged.shape[0], rows, 128)]

        def places():
            return [0]

    *other, own, pulled, edge = features(
        live_blocks, neighbours.T, atom_class.reshape(1, -1), zero, rot_one, rot_two, source, target, rows, fanout, cuts
    )
    if direct:
        came = [swap(piece, "gx", 1) for piece in other]
        received = lax.optimization_barrier((*came, *held))
        came, held = received[:cuts], received[cuts:]
        parts = pair_sum(own, came, count_yz)
        gathered = [parts[0]] + [swap(parts[k], "yz", k) for k in reversed(range(1, count_yz))]
        held = pack(held)
        pieces = [held, swap(held, "gx", 1)]
    grad_own, *ghosts = back(edge, zero, rot_one, rot_two, pulled, pieces, places, rows, atoms, slots, face)
    returned = [
        neighbour_pairs(ghost, axis, first)
        for ghost, axis, first in zip(ghosts, ("yz", "gx", "yz", "gx"), (1, 1, 0, 0))
    ]
    if direct:
        grad_own, *gathered = lax.optimization_barrier((grad_own, *gathered))
        summed, *returned = lax.optimization_barrier((total_sum(gathered), *returned))
        across = swap(summed, "gx", 2)
        input_grad = finish(send_index, grad_own, returned)
        across, input_grad = lax.optimization_barrier((across, input_grad))
        sums = [summed, across, swap(summed, "gx", 1), swap(across, "gx", 1)]
    else:
        mixed = jnp.stack([own, other[0]]).astype(F32)
        mixed = jnp.where(core == 0, mixed, mixed[::-1])
        whole = lax.psum(mixed, ("yz", "gx"))
        piece = lax.dynamic_slice_in_dim(whole, row * height, height, 1)
        piece = jnp.where(core == 0, piece, piece[::-1])
        sums = [piece[0], piece[1]]
        input_grad = finish(send_index, grad_own, returned)
    grad_scale = math.sqrt(fanout / (atoms * count_yz * count_gx))
    expert_grad = expert_product(merge_coef, sums, merge_coef.shape[1] // count_gx, grad_scale)
    return (jnp.transpose(input_grad, (1, 0, 2)), expert_grad)


def solution(mesh):
    tiles = ("rep", "yz", "gx")
    in_specs = (
        P(tiles, None, None),
        P(tiles, None, None),
        P(tiles, None),
        P(tiles),
        P(None, None, tiles),
        P(None, None, tiles),
        P(tiles, None),
        P(tiles),
        P(tiles),
        P(),
        P(None, "yz"),
    )
    out_specs = (P(tiles, None, None), P(("rep", "gx"), "yz"))
    return jax.shard_map(local, mesh=mesh, in_specs=in_specs, out_specs=out_specs, check_vma=False)
```

```python
import functools
import math

import jax
import jax.numpy as jnp
from jax import lax
from jax.experimental import pallas as pl
from jax.experimental.pallas import tpu as pltpu
from jax.sharding import PartitionSpec as P

LIVE_BLOCK = 64
CHUNK = 512
SUB = 32
F32 = jnp.float32
BF16 = jnp.bfloat16

STACK = (0, 2, 6, 3, 7, 1, 5)
SLOT = {component: place for place, component in enumerate(STACK)}

VMEM = pl.BlockSpec(memory_space=pltpu.VMEM)
HBM = pl.BlockSpec(memory_space=pltpu.HBM)


def limits(mebibytes):
    return pltpu.CompilerParams(vmem_limit_bytes=mebibytes * 1024 * 1024)


def cost(flops, moved):
    return pl.CostEstimate(flops=flops, bytes_accessed=moved, transcendentals=0)


def nn(left, right):
    return lax.dot_general(left, right, (((1,), (0,)), ((), ())), preferred_element_type=F32)


def nt(left, right):
    return lax.dot_general(left, right, (((1,), (1,)), ((), ())), preferred_element_type=F32)


def split3(value):
    high = value.astype(BF16)
    rest = value - high.astype(F32)
    middle = rest.astype(BF16)
    low = (rest - middle.astype(F32)).astype(BF16)
    return high, middle, low


def merge_kernel(coef_in_ref, experts_ref, out_ref, held, coef_ref, arrived, coef_arrived):
    members, experts = coef_in_ref.shape
    rows = out_ref.shape[1]
    start = pl.multiple_of(lax.rem(lax.axis_index("gx"), 2) * rows * 128, 128)
    stripes = arrived.shape[0]
    blocks = rows // 16
    edges = [blocks * stripe // stripes for stripe in range(stripes + 1)]
    copies = []
    for stripe in range(stripes):
        at, wide = edges[stripe] * 2048, (edges[stripe + 1] - edges[stripe]) * 2048
        copies.append(
            pltpu.make_async_copy(
                experts_ref.at[:, pl.ds(start + at, wide)], held.at[:, pl.ds(at, wide)], arrived.at[stripe]
            )
        )
        copies[-1].start()
    coef_copy = pltpu.make_async_copy(coef_in_ref, coef_ref, coef_arrived)
    coef_copy.start()
    coef_copy.wait()
    wide = 8 * experts
    row = lax.broadcasted_iota(jnp.int32, (8, wide), 0)
    col = lax.broadcasted_iota(jnp.int32, (8, wide), 1)
    diagonal = row == col // experts
    source = lax.broadcasted_iota(jnp.int32, (experts, wide), 0)
    target = lax.broadcasted_iota(jnp.int32, (experts, wide), 1)
    tile = (source == target % experts).astype(F32).astype(BF16)
    lefts = []
    for term in split3(coef_ref[...]):
        tiled = nn(term, tile)
        for member in range(members):
            lefts.append(jnp.where(diagonal, tiled[member : member + 1, :], 0.0).astype(BF16))
    lefts = jnp.concatenate(lefts, axis=0)
    height = 8 * members
    for block in range(blocks):
        if block in edges:
            copies[edges.index(block)].wait()
        halves = []
        for half in range(2):
            first = block * 16 + half * 8
            groups = [held[:, (first + g) * 128 : (first + g + 1) * 128] for g in range(8)]
            halves.append(jnp.concatenate(groups, axis=0))
        product = nn(lefts, jnp.concatenate(halves, axis=1))
        total = product[:height] + product[height : 2 * height] + product[2 * height :]
        for member in range(members):
            part = total[member * 8 : member * 8 + 8]
            out_ref[member, block * 16 : block * 16 + 16, :] = jnp.concatenate(
                [part[:, :128], part[:, 128:]], axis=0
            ).astype(BF16)


def merge(coef, experts, parts):
    members, count = coef.shape
    columns = experts.shape[1] // parts
    rows = columns // 128
    return pl.pallas_call(
        merge_kernel,
        in_specs=[HBM, HBM],
        out_specs=VMEM,
        out_shape=jax.ShapeDtypeStruct((members, rows, 128), BF16),
        scratch_shapes=[
            pltpu.VMEM((count, columns), BF16),
            pltpu.VMEM((members, count), F32),
            pltpu.SemaphoreType.DMA((2,)),
            pltpu.SemaphoreType.DMA,
        ],
        compiler_params=limits(52),
        cost_estimate=cost(96 * 16 * columns, 2 * count * columns),
        name="merge",
    )(coef, experts)


def features_kernel(
    live_in_ref, near_ref, class_ref, zero_ref, one_ref, two_ref, source_ref, target_ref,
    *refs, fanout, cuts,
):
    other_refs, own_ref, pulled_ref, edge_ref = refs[:cuts], *refs[cuts : cuts + 3]
    source_t, target_t, moved, spread, rotated, grads, live_ref, live_arrived = refs[cuts + 3 :]
    slots, channels = source_ref.shape[1:]
    atoms = target_ref.shape[1]
    edges = atoms * fanout
    live_copy = pltpu.make_async_copy(live_in_ref, live_ref, live_arrived)
    live_copy.start()
    for c in range(9):
        source_t[c * channels : (c + 1) * channels, :] = source_ref[c].T
        target_t[c * channels : (c + 1) * channels, :] = target_ref[c].T
    near = near_ref[...].astype(F32).astype(BF16)
    classes = class_ref[...].astype(F32).astype(BF16)
    scale = 1.0 / math.sqrt(fanout)

    def chunk_step(chunk, carry):
        start = pl.multiple_of(chunk * CHUNK, CHUNK)
        here = pl.ds(start, CHUNK)
        edge = lax.broadcasted_iota(jnp.int32, (atoms, CHUNK), 1) + start
        atom = lax.broadcasted_iota(jnp.int32, (atoms, CHUNK), 0)
        repeat = (edge // fanout == atom).astype(F32).astype(BF16)
        edge8 = lax.broadcasted_iota(jnp.int32, (fanout, CHUNK), 1) + start
        lane8 = lax.broadcasted_iota(jnp.int32, (fanout, CHUNK), 0)
        picked = jnp.where(edge8 % fanout == lane8, nn(near, repeat), 0.0)
        near_row = jnp.sum(picked, axis=0, keepdims=True)
        class_row = nn(classes, repeat)
        edge_ref[0:1, here] = near_row
        edge_ref[1:2, here] = class_row
        slot = lax.broadcasted_iota(jnp.int32, (slots, CHUNK), 0).astype(F32)
        pick = (slot == near_row).astype(F32).astype(BF16)
        moved[...] = nn(source_t[...], pick)
        spread[...] = nn(target_t[...], repeat)

        def sub_step(sub, inner):
            at = pl.multiple_of(sub * SUB, SUB)

            def turn(field, write):
                def part(c):
                    return field[pl.ds(c * channels + at, SUB), :]

                write(0, zero_ref[0:1, here] * part(0))
                values = [part(c) for c in (1, 2, 3)]
                for a in range(3):
                    total = one_ref[a, 0:1, here] * values[0]
                    for b in range(1, 3):
                        total += one_ref[a, b : b + 1, here] * values[b]
                    write(1 + a, total)
                values = [part(c) for c in (4, 5, 6, 7, 8)]
                for a in range(1, 4):
                    total = two_ref[a, 0:1, here] * values[0]
                    for b in range(1, 5):
                        total += two_ref[a, b : b + 1, here] * values[b]
                    write(4 + a, total)

            def write_rotated(c, value):
                rotated[pl.ds(SLOT[c] * channels + at, SUB), here] = value.astype(BF16)

            def write_pulled(c, value):
                pulled_ref[pl.ds(SLOT[c] * channels + at, SUB), here] = (value * scale).astype(BF16)

            turn(moved, write_rotated)
            turn(spread, write_pulled)
            return inner

        lax.fori_loop(0, channels // SUB, sub_step, 0)
        return carry

    lax.fori_loop(0, edges // CHUNK, chunk_step, 0)
    live_copy.wait()
    edge_row = lax.broadcasted_iota(jnp.int32, (1, edges), 1)
    edge_ref[1:2, :] = jnp.where(edge_row < live_ref[0] * LIVE_BLOCK * fanout, edge_ref[1:2, :], -1.0)
    zw, pw = 3 * channels, 2 * channels
    first = zw * zw // 128
    second = first + pw * pw // 128
    own = lax.rem(lax.axis_index("gx"), 2).astype(F32)
    for out_refs, wanted in ((other_refs, 1.0 - own), ((own_ref,), own)):
        mask = (edge_ref[1:2, :] == wanted).astype(F32).astype(BF16)
        qz = pulled_ref[0:zw, :] * mask
        qp = pulled_ref[zw : zw + pw, :] * mask
        qn = pulled_ref[zw + pw : zw + 2 * pw, :] * mask
        z, p, n = rotated[0:zw, :], rotated[zw : zw + pw, :], rotated[zw + pw : zw + 2 * pw, :]
        whole = nt(z, qz)
        for j in range(zw // 128):
            grads[pl.ds(j, zw, stride=zw // 128), :] = whole[:, j * 128 : (j + 1) * 128]
        coupled = nt(p, qp) + nt(n, qn)
        crossed = nt(p, qn) - nt(n, qp)
        for j in range(pw // 128):
            grads[pl.ds(first + j, pw, stride=pw // 128), :] = coupled[:, j * 128 : (j + 1) * 128]
            grads[pl.ds(second + j, pw, stride=pw // 128), :] = crossed[:, j * 128 : (j + 1) * 128]
        height = out_refs[0].shape[0]
        for index, out_ref in enumerate(out_refs):
            per = max(len(out_refs) // 4, 1)
            at = (lax.axis_index("yz") ^ (index // per)) * per * height + index % per * height
            at = pl.multiple_of(at, 16) if len(out_refs) > 1 else 0
            out_ref[...] = grads[pl.ds(at, height), :].astype(BF16)


def features(live, near, classes, zero, one, two, source, target, rows, fanout, cuts):
    slots, channels = source.shape[1:]
    atoms = target.shape[1]
    edges = atoms * fanout
    shape = jax.ShapeDtypeStruct
    return pl.pallas_call(
        functools.partial(features_kernel, fanout=fanout, cuts=cuts),
        in_specs=[HBM] + [VMEM] * 7,
        out_specs=[VMEM] * (cuts + 3),
        out_shape=[
            *[shape((rows // cuts, 128), BF16)] * cuts,
            shape((rows, 128), BF16),
            shape((7 * channels, edges), BF16),
            shape((8, edges), F32),
        ],
        scratch_shapes=[
            pltpu.VMEM((9 * channels, slots), BF16),
            pltpu.VMEM((9 * channels, atoms), BF16),
            pltpu.VMEM((9 * channels, CHUNK), F32),
            pltpu.VMEM((9 * channels, CHUNK), F32),
            pltpu.VMEM((7 * channels, edges), BF16),
            pltpu.VMEM((rows, 128), F32),
            pltpu.SMEM((1,), jnp.int32),
            pltpu.SemaphoreType.DMA,
        ],
        compiler_params=limits(24),
        cost_estimate=cost(9 * 10**9, 7 * 10**6),
        name="features",
    )(live, near, classes, zero, one, two, source, target)


def back_kernel(
    edge_ref, zero_ref, one_ref, two_ref, pulled_ref, *rest, pieces, members, atoms, face, places,
):
    piece_refs = rest[:pieces]
    own_ref, *ghost_refs = rest[pieces : pieces + 5]
    flat, weight_zero, weight_pair, field, turned, pick_all = rest[pieces + 5 :]
    rows = flat.shape[1]
    channels = own_ref.shape[2]
    slots = pick_all.shape[0]
    edges = pulled_ref.shape[1]
    zw, pw = 3 * channels, 2 * channels
    first = zw * zw // 128
    second = first + pw * pw // 128
    placed = [(piece, index) for piece in piece_refs for index in range(piece.shape[0])]
    for (piece, index), place in zip(placed, places()):
        height = piece.shape[2]
        at = pl.ds(pl.multiple_of(place, 16), height)
        for k in range(members):
            flat[k, at, :] = piece[index, k].astype(F32)
    for k in range(members):
        for j in range(zw // 128):
            weight_zero[:, k * zw + j * 128 : k * zw + (j + 1) * 128] = flat[
                k, pl.ds(j, zw, stride=zw // 128), :
            ].astype(BF16)
        for j in range(pw // 128):
            at = k * 2 * pw + j * 128
            weight_pair[:, at : at + 128] = flat[k, pl.ds(first + j, pw, stride=pw // 128), :].astype(BF16)
            weight_pair[:, at + pw : at + pw + 128] = flat[
                k, pl.ds(second + j, pw, stride=pw // 128), :
            ].astype(BF16)

    def chunk_step(chunk, carry):
        start = pl.multiple_of(chunk * CHUNK, CHUNK)
        here = pl.ds(start, CHUNK)
        slot = lax.broadcasted_iota(jnp.int32, (slots, CHUNK), 0).astype(F32)
        pick_all[:, here] = (slot == edge_ref[0:1, here]).astype(F32).astype(BF16)
        qz, qpn, qnp = [], [], []
        for k in range(members):
            mask = (edge_ref[1:2, here] == float(k)).astype(F32).astype(BF16)
            qz.append(pulled_ref[0:zw, here] * mask)
            qp = pulled_ref[zw : zw + pw, here] * mask
            qn = pulled_ref[zw + pw : zw + 2 * pw, here] * mask
            qpn += [qp, qn]
            qnp += [qn, -qp]
        field[0:zw, :] = nn(weight_zero[...], jnp.concatenate(qz, axis=0))
        field[zw : zw + pw, :] = nn(weight_pair[...], jnp.concatenate(qpn, axis=0))
        field[zw + pw : zw + 2 * pw, :] = nn(weight_pair[...], jnp.concatenate(qnp, axis=0))

        def sub_step(sub, inner):
            at = pl.multiple_of(sub * SUB, SUB)

            def part(c):
                return field[pl.ds(SLOT[c] * channels + at, SUB), :]

            def write(c, value):
                turned[pl.ds(c * channels + at, SUB), here] = value.astype(BF16)

            write(0, zero_ref[0:1, here] * part(0))
            values = [part(c) for c in (1, 2, 3)]
            for b in range(3):
                total = one_ref[0, b : b + 1, here] * values[0]
                for a in range(1, 3):
                    total += one_ref[a, b : b + 1, here] * values[a]
                write(1 + b, total)
            values = [part(c) for c in (5, 6, 7)]
            for b in range(5):
                total = two_ref[1, b : b + 1, here] * values[0]
                for a in range(2, 4):
                    total += two_ref[a, b : b + 1, here] * values[a - 1]
                write(4 + b, total)
            return inner

        lax.fori_loop(0, channels // SUB, sub_step, 0)
        return carry

    lax.fori_loop(0, edges // CHUNK, chunk_step, 0)
    for c in range(9):
        summed = nt(pick_all[...], turned[c * channels : (c + 1) * channels, :])
        own_ref[c] = summed[:atoms]
        blocks = [summed[atoms + block * face : atoms + (block + 1) * face] for block in range(4)]
        for side in range(2):
            even = lax.rem(lax.axis_index(("gx", "yz")[side]), 2) == 0
            low, high = blocks[2 * side], blocks[2 * side + 1]
            ghost_refs[3 - side][c] = jnp.where(even, high, low).astype(BF16)
            ghost_refs[1 - side][c] = jnp.where(even, low, high).astype(BF16)


def back(edge, zero, one, two, pulled, pieces, places, rows, atoms, slots, face):
    members = pieces[0].shape[1]
    edges = pulled.shape[1]
    channels = pulled.shape[0] // 7
    shape = jax.ShapeDtypeStruct
    return pl.pallas_call(
        functools.partial(
            back_kernel, pieces=len(pieces), members=members, atoms=atoms, face=face, places=places
        ),
        in_specs=[VMEM] * (5 + len(pieces)),
        out_specs=[VMEM] * 5,
        out_shape=[shape((9, atoms, channels), F32), *[shape((9, face, channels), BF16)] * 4],
        scratch_shapes=[
            pltpu.VMEM((members, rows, 128), F32),
            pltpu.VMEM((3 * channels, members * 3 * channels), BF16),
            pltpu.VMEM((2 * channels, members * 4 * channels), BF16),
            pltpu.VMEM((7 * channels, CHUNK), F32),
            pltpu.VMEM((9 * channels, edges), BF16),
            pltpu.VMEM((slots, edges), BF16),
        ],
        compiler_params=limits(24),
        cost_estimate=cost(9 * 10**9, 7 * 10**6),
        name="back",
    )(edge, zero, one, two, pulled, *pieces)


def pair_kernel(own_ref, *refs, cuts):
    came_refs, out_refs = refs[:cuts], refs[cuts:]
    row = lax.axis_index("yz")
    per = cuts // len(out_refs)
    height = came_refs[0].shape[0]
    for index, came_ref in enumerate(came_refs):
        at = pl.multiple_of((row ^ (index // per)) * per * height + index % per * height, 16)
        total = own_ref[pl.ds(at, height), :].astype(F32) + came_ref[...].astype(F32)
        out_refs[index // per][pl.ds(index % per * height, height), :] = total.astype(BF16)


def pair_sum(own, came, count):
    height = own.shape[0] // count
    return pl.pallas_call(
        functools.partial(pair_kernel, cuts=len(came)),
        in_specs=[VMEM] * (1 + len(came)),
        out_specs=[VMEM] * count,
        out_shape=[jax.ShapeDtypeStruct((height, 128), BF16)] * count,
        compiler_params=limits(6),
        cost_estimate=cost(10**6, 2 * 10**6),
        name="pair_sum",
    )(own, *came)


def total_kernel(*refs):
    total = refs[0][...].astype(F32)
    for ref in refs[1:-1]:
        total += ref[...].astype(F32)
    refs[-1][...] = total.astype(BF16)


def total_sum(parts):
    return pl.pallas_call(
        total_kernel,
        in_specs=[VMEM] * len(parts),
        out_specs=VMEM,
        out_shape=jax.ShapeDtypeStruct(parts[0].shape, BF16),
        compiler_params=limits(6),
        cost_estimate=cost(10**6, 10**6),
        name="total_sum",
    )(*parts)


def pack_kernel(*refs):
    for index, ref in enumerate(refs[:-1]):
        refs[-1][index] = ref[...]


def pack(pieces):
    return pl.pallas_call(
        pack_kernel,
        in_specs=[VMEM] * len(pieces),
        out_specs=VMEM,
        out_shape=jax.ShapeDtypeStruct((len(pieces), *pieces[0].shape), pieces[0].dtype),
        compiler_params=limits(6),
        cost_estimate=cost(10**5, 10**6),
        name="pack",
    )(*pieces)


def expert_kernel(coef_ref, *refs, scale):
    sums, out_ref, summed, staged, written = refs[:-4], *refs[-4:]
    owned = out_ref.shape[0]
    place = lax.axis_index("gx")
    row = lax.broadcasted_iota(jnp.int32, (owned, coef_ref.shape[1]), 0)
    col = lax.broadcasted_iota(jnp.int32, (owned, coef_ref.shape[1]), 1)
    chosen = col == row + place * owned
    picked = [
        jnp.sum(jnp.where(chosen, coef_ref[k : k + 1, :], 0.0), axis=1, keepdims=True) * scale for k in range(2)
    ]
    even = lax.rem(place, 2) == 0
    first = jnp.broadcast_to(jnp.where(even, picked[0], picked[1]), (owned, 128))
    second = jnp.broadcast_to(jnp.where(even, picked[1], picked[0]), (owned, 128))
    half = len(sums) // 2
    for side in range(2):
        total = sums[side * half][...].astype(F32)
        for ref in sums[side * half + 1 : (side + 1) * half]:
            total += ref[...].astype(F32)
        summed[side] = total
    rows = summed.shape[1]
    stripes = written.shape[0]
    copies = []
    for stripe in range(stripes):
        low, high = rows * stripe // stripes, rows * (stripe + 1) // stripes
        for row in range(low, high):
            staged[:, row * 128 : (row + 1) * 128] = (
                first * summed[0, row : row + 1, :] + second * summed[1, row : row + 1, :]
            )
        span = pl.ds(low * 128, (high - low) * 128)
        copies.append(pltpu.make_async_copy(staged.at[:, span], out_ref.at[:, span], written.at[stripe]))
        copies[-1].start()
    for copy in copies:
        copy.wait()


def expert_product(coef, sums, owned, scale):
    rows = sums[0].shape[0]
    return pl.pallas_call(
        functools.partial(expert_kernel, scale=scale),
        in_specs=[VMEM] * (1 + len(sums)),
        out_specs=HBM,
        out_shape=jax.ShapeDtypeStruct((owned, rows * 128), F32),
        scratch_shapes=[
            pltpu.VMEM((2, rows, 128), F32),
            pltpu.VMEM((owned, rows * 128), F32),
            pltpu.SemaphoreType.DMA((4,)),
        ],
        compiler_params=limits(8),
        cost_estimate=cost(10**6, 4 * 10**6),
        name="expert_product",
    )(coef, *sums)


def finish_kernel(send_ref, own_ref, a_ref, b_ref, c_ref, d_ref, out_ref):
    atoms = own_ref.shape[1]
    face = send_ref.shape[1]
    row = lax.broadcasted_iota(jnp.int32, (atoms, face), 0)
    picks = []
    for side in range(2):
        even = lax.rem(lax.axis_index(("gx", "yz")[side]), 2) == 0
        below, above = send_ref[2 * side : 2 * side + 1, :], send_ref[2 * side + 1 : 2 * side + 2, :]
        for faces in (jnp.where(even, above, below), jnp.where(even, below, above)):
            picks.append((row == faces).astype(F32).astype(BF16))
    picks = [picks[3], picks[1], picks[2], picks[0]]
    for c in range(9):
        total = own_ref[c]
        for pick, ref in zip(picks, (a_ref, b_ref, c_ref, d_ref)):
            total += nn(pick, ref[c])
        out_ref[c] = total.astype(BF16)


def finish(send, own, returned):
    return pl.pallas_call(
        finish_kernel,
        in_specs=[VMEM] * 6,
        out_specs=VMEM,
        out_shape=jax.ShapeDtypeStruct(own.shape, BF16),
        compiler_params=limits(6),
        cost_estimate=cost(10**8, 2 * 10**6),
        name="finish",
    )(send, own, *returned)


def swap(value, axis, bit):
    return lax.ppermute(value, axis, [(i, i ^ bit) for i in range(lax.axis_size(axis))])


def neighbour_pairs(value, axis, first):
    count = lax.axis_size(axis)
    moves = []
    for low in range(first, count, 2):
        high = (low + 1) % count
        moves += [(low, high), (high, low)]
    return lax.ppermute(value, axis, moves)


def local(
    saved_input, cotangent, neighbours, rot_zero, rot_one, rot_two, send_index, atom_class, live_blocks,
    merge_coef, experts,
):
    atoms, fanout = neighbours.shape
    slots = saved_input.shape[0]
    channels = cotangent.shape[2]
    face = send_index.shape[1]
    count_yz, count_gx = lax.axis_size("yz"), lax.axis_size("gx")
    row, column = lax.axis_index("yz"), lax.axis_index("gx")
    core = column % 2
    height = experts.shape[1] // 128
    rows = height * count_yz
    direct = height % 32 == 0 and count_yz == 4 and count_gx == 4
    cuts = 4 if direct else 1

    zero = rot_zero.reshape(1, -1)
    source = jnp.transpose(saved_input, (1, 0, 2))
    target = jnp.transpose(cotangent, (1, 0, 2))

    if direct:
        half = height // 2
        mine = merge(merge_coef, experts, 2)
        held = [mine] + [swap(mine, "yz", k) for k in (2, 1, 3)]
        source, target, mine = lax.optimization_barrier((source, target, mine))

        def places():
            here, side = lax.axis_index("yz"), lax.rem(lax.axis_index("gx"), 2)
            starts = [(here ^ k) * height for k in (0, 2, 1, 3)]
            return [at + side * half for at in starts] + [at + (1 - side) * half for at in starts]
    else:
        part = jnp.dot(merge_coef, experts.astype(F32), precision=lax.Precision.HIGHEST).astype(BF16)
        merged = lax.all_gather(part, "yz", axis=1, tiled=True)
        pieces = [merged.reshape(1, merged.shape[0], rows, 128)]

        def places():
            return [0]

    *other, own, pulled, edge = features(
        live_blocks, neighbours.T, atom_class.reshape(1, -1), zero, rot_one, rot_two, source, target, rows, fanout, cuts
    )
    if direct:
        came = [swap(piece, "gx", 1) for piece in other]
        received = lax.optimization_barrier((*came, *held))
        came, held = received[:cuts], received[cuts:]
        parts = pair_sum(own, came, count_yz)
        gathered = [parts[0]] + [swap(parts[k], "yz", k) for k in (3, 1, 2)]
        held = pack(held)
        pieces = [held, swap(held, "gx", 1)]
    grad_own, *ghosts = back(edge, zero, rot_one, rot_two, pulled, pieces, places, rows, atoms, slots, face)
    returned = [
        neighbour_pairs(ghost, axis, first)
        for ghost, axis, first in zip(ghosts, ("yz", "gx", "yz", "gx"), (1, 1, 0, 0))
    ]
    if direct:
        grad_own, *gathered = lax.optimization_barrier((grad_own, *gathered))
        summed, *returned = lax.optimization_barrier((total_sum(gathered), *returned))
        across = swap(summed, "gx", 2)
        input_grad = finish(send_index, grad_own, returned)
        across, input_grad = lax.optimization_barrier((across, input_grad))
        sums = [summed, across, swap(summed, "gx", 1), swap(across, "gx", 1)]
    else:
        mixed = jnp.stack([own, other[0]]).astype(F32)
        mixed = jnp.where(core == 0, mixed, mixed[::-1])
        whole = lax.psum(mixed, ("yz", "gx"))
        piece = lax.dynamic_slice_in_dim(whole, row * height, height, 1)
        piece = jnp.where(core == 0, piece, piece[::-1])
        sums = [piece[0], piece[1]]
        input_grad = finish(send_index, grad_own, returned)
    grad_scale = math.sqrt(fanout / (atoms * count_yz * count_gx))
    expert_grad = expert_product(merge_coef, sums, merge_coef.shape[1] // count_gx, grad_scale)
    return (jnp.transpose(input_grad, (1, 0, 2)), expert_grad)


def solution(mesh):
    tiles = ("rep", "yz", "gx")
    in_specs = (
        P(tiles, None, None),
        P(tiles, None, None),
        P(tiles, None),
        P(tiles),
        P(None, None, tiles),
        P(None, None, tiles),
        P(tiles, None),
        P(tiles),
        P(tiles),
        P(),
        P(None, "yz"),
    )
    out_specs = (P(tiles, None, None), P(("rep", "gx"), "yz"))
    return jax.shard_map(local, mesh=mesh, in_specs=in_specs, out_specs=out_specs, check_vma=False)
```

```python
import functools
import math

import jax
import jax.numpy as jnp
from jax import lax
from jax.experimental import pallas as pl
from jax.experimental.pallas import tpu as pltpu
from jax.sharding import PartitionSpec as P

LIVE_BLOCK = 64
CHUNK = 512
SUB = 32
F32 = jnp.float32
BF16 = jnp.bfloat16

STACK = (0, 2, 6, 3, 7, 1, 5)
SLOT = {component: place for place, component in enumerate(STACK)}

VMEM = pl.BlockSpec(memory_space=pltpu.VMEM)
HBM = pl.BlockSpec(memory_space=pltpu.HBM)


def limits(mebibytes):
    return pltpu.CompilerParams(vmem_limit_bytes=mebibytes * 1024 * 1024)


def cost(flops, moved):
    return pl.CostEstimate(flops=flops, bytes_accessed=moved, transcendentals=0)


def nn(left, right):
    return lax.dot_general(left, right, (((1,), (0,)), ((), ())), preferred_element_type=F32)


def nt(left, right):
    return lax.dot_general(left, right, (((1,), (1,)), ((), ())), preferred_element_type=F32)


def split3(value):
    high = value.astype(BF16)
    rest = value - high.astype(F32)
    middle = rest.astype(BF16)
    low = (rest - middle.astype(F32)).astype(BF16)
    return high, middle, low


def merge_kernel(coef_in_ref, experts_ref, out_ref, held, coef_ref, arrived, coef_arrived):
    members, experts = coef_in_ref.shape
    rows = out_ref.shape[1]
    start = pl.multiple_of(lax.rem(lax.axis_index("gx"), 2) * rows * 128, 128)
    stripes = arrived.shape[0]
    blocks = rows // 16
    edges = [blocks * stripe // stripes for stripe in range(stripes + 1)]
    copies = []
    for stripe in range(stripes):
        at, wide = edges[stripe] * 2048, (edges[stripe + 1] - edges[stripe]) * 2048
        copies.append(
            pltpu.make_async_copy(
                experts_ref.at[:, pl.ds(start + at, wide)], held.at[:, pl.ds(at, wide)], arrived.at[stripe]
            )
        )
        copies[-1].start()
    coef_copy = pltpu.make_async_copy(coef_in_ref, coef_ref, coef_arrived)
    coef_copy.start()
    coef_copy.wait()
    wide = 8 * experts
    row = lax.broadcasted_iota(jnp.int32, (8, wide), 0)
    col = lax.broadcasted_iota(jnp.int32, (8, wide), 1)
    diagonal = row == col // experts
    source = lax.broadcasted_iota(jnp.int32, (experts, wide), 0)
    target = lax.broadcasted_iota(jnp.int32, (experts, wide), 1)
    tile = (source == target % experts).astype(F32).astype(BF16)
    lefts = []
    for term in split3(coef_ref[...]):
        tiled = nn(term, tile)
        for member in range(members):
            lefts.append(jnp.where(diagonal, tiled[member : member + 1, :], 0.0).astype(BF16))
    lefts = jnp.concatenate(lefts, axis=0)
    height = 8 * members
    for block in range(blocks):
        if block in edges:
            copies[edges.index(block)].wait()
        halves = []
        for half in range(2):
            first = block * 16 + half * 8
            groups = [held[:, (first + g) * 128 : (first + g + 1) * 128] for g in range(8)]
            halves.append(jnp.concatenate(groups, axis=0))
        product = nn(lefts, jnp.concatenate(halves, axis=1))
        total = product[:height] + product[height : 2 * height] + product[2 * height :]
        for member in range(members):
            part = total[member * 8 : member * 8 + 8]
            out_ref[member, block * 16 : block * 16 + 16, :] = jnp.concatenate(
                [part[:, :128], part[:, 128:]], axis=0
            ).astype(BF16)


def merge(coef, experts, parts):
    members, count = coef.shape
    columns = experts.shape[1] // parts
    rows = columns // 128
    return pl.pallas_call(
        merge_kernel,
        in_specs=[HBM, HBM],
        out_specs=VMEM,
        out_shape=jax.ShapeDtypeStruct((members, rows, 128), BF16),
        scratch_shapes=[
            pltpu.VMEM((count, columns), BF16),
            pltpu.VMEM((members, count), F32),
            pltpu.SemaphoreType.DMA((2,)),
            pltpu.SemaphoreType.DMA,
        ],
        compiler_params=limits(52),
        cost_estimate=cost(96 * 16 * columns, 2 * count * columns),
        name="merge",
    )(coef, experts)


def features_kernel(
    live_in_ref, near_ref, class_ref, zero_ref, one_ref, two_ref, source_ref, target_ref,
    *refs, fanout, cuts,
):
    other_refs, own_ref, pulled_ref, edge_ref = refs[:cuts], *refs[cuts : cuts + 3]
    source_t, target_t, moved, spread, rotated, grads, live_ref, live_arrived = refs[cuts + 3 :]
    slots, channels = source_ref.shape[1:]
    atoms = target_ref.shape[1]
    edges = atoms * fanout
    live_copy = pltpu.make_async_copy(live_in_ref, live_ref, live_arrived)
    live_copy.start()
    for c in range(9):
        source_t[c * channels : (c + 1) * channels, :] = source_ref[c].T
        target_t[c * channels : (c + 1) * channels, :] = target_ref[c].T
    near = near_ref[...].astype(F32).astype(BF16)
    classes = class_ref[...].astype(F32).astype(BF16)
    scale = 1.0 / math.sqrt(fanout)

    def chunk_step(chunk, carry):
        start = pl.multiple_of(chunk * CHUNK, CHUNK)
        here = pl.ds(start, CHUNK)
        edge = lax.broadcasted_iota(jnp.int32, (atoms, CHUNK), 1) + start
        atom = lax.broadcasted_iota(jnp.int32, (atoms, CHUNK), 0)
        repeat = (edge // fanout == atom).astype(F32).astype(BF16)
        edge8 = lax.broadcasted_iota(jnp.int32, (fanout, CHUNK), 1) + start
        lane8 = lax.broadcasted_iota(jnp.int32, (fanout, CHUNK), 0)
        picked = jnp.where(edge8 % fanout == lane8, nn(near, repeat), 0.0)
        near_row = jnp.sum(picked, axis=0, keepdims=True)
        class_row = nn(classes, repeat)
        edge_ref[0:1, here] = near_row
        edge_ref[1:2, here] = class_row
        slot = lax.broadcasted_iota(jnp.int32, (slots, CHUNK), 0).astype(F32)
        pick = (slot == near_row).astype(F32).astype(BF16)
        moved[...] = nn(source_t[...], pick)
        spread[...] = nn(target_t[...], repeat)

        def sub_step(sub, inner):
            at = pl.multiple_of(sub * SUB, SUB)

            def turn(field, write):
                def part(c):
                    return field[pl.ds(c * channels + at, SUB), :]

                write(0, zero_ref[0:1, here] * part(0))
                values = [part(c) for c in (1, 2, 3)]
                for a in range(3):
                    total = one_ref[a, 0:1, here] * values[0]
                    for b in range(1, 3):
                        total += one_ref[a, b : b + 1, here] * values[b]
                    write(1 + a, total)
                values = [part(c) for c in (4, 5, 6, 7, 8)]
                for a in range(1, 4):
                    total = two_ref[a, 0:1, here] * values[0]
                    for b in range(1, 5):
                        total += two_ref[a, b : b + 1, here] * values[b]
                    write(4 + a, total)

            def write_rotated(c, value):
                rotated[pl.ds(SLOT[c] * channels + at, SUB), here] = value.astype(BF16)

            def write_pulled(c, value):
                pulled_ref[pl.ds(SLOT[c] * channels + at, SUB), here] = (value * scale).astype(BF16)

            turn(moved, write_rotated)
            turn(spread, write_pulled)
            return inner

        lax.fori_loop(0, channels // SUB, sub_step, 0)
        return carry

    lax.fori_loop(0, edges // CHUNK, chunk_step, 0)
    live_copy.wait()
    edge_row = lax.broadcasted_iota(jnp.int32, (1, edges), 1)
    edge_ref[1:2, :] = jnp.where(edge_row < live_ref[0] * LIVE_BLOCK * fanout, edge_ref[1:2, :], -1.0)
    zw, pw = 3 * channels, 2 * channels
    first = zw * zw // 128
    second = first + pw * pw // 128
    own = lax.rem(lax.axis_index("gx"), 2).astype(F32)
    for out_refs, wanted in ((other_refs, 1.0 - own), ((own_ref,), own)):
        mask = (edge_ref[1:2, :] == wanted).astype(F32).astype(BF16)
        qz = pulled_ref[0:zw, :] * mask
        qp = pulled_ref[zw : zw + pw, :] * mask
        qn = pulled_ref[zw + pw : zw + 2 * pw, :] * mask
        z, p, n = rotated[0:zw, :], rotated[zw : zw + pw, :], rotated[zw + pw : zw + 2 * pw, :]
        whole = nt(z, qz)
        for j in range(zw // 128):
            grads[pl.ds(j, zw, stride=zw // 128), :] = whole[:, j * 128 : (j + 1) * 128]
        coupled = nt(p, qp) + nt(n, qn)
        crossed = nt(p, qn) - nt(n, qp)
        for j in range(pw // 128):
            grads[pl.ds(first + j, pw, stride=pw // 128), :] = coupled[:, j * 128 : (j + 1) * 128]
            grads[pl.ds(second + j, pw, stride=pw // 128), :] = crossed[:, j * 128 : (j + 1) * 128]
        height = out_refs[0].shape[0]
        for index, out_ref in enumerate(out_refs):
            per = max(len(out_refs) // 4, 1)
            at = (lax.axis_index("yz") ^ (index // per)) * per * height + index % per * height
            at = pl.multiple_of(at, 16) if len(out_refs) > 1 else 0
            out_ref[...] = grads[pl.ds(at, height), :].astype(BF16)


def features(live, near, classes, zero, one, two, source, target, rows, fanout, cuts):
    slots, channels = source.shape[1:]
    atoms = target.shape[1]
    edges = atoms * fanout
    shape = jax.ShapeDtypeStruct
    return pl.pallas_call(
        functools.partial(features_kernel, fanout=fanout, cuts=cuts),
        in_specs=[HBM] + [VMEM] * 7,
        out_specs=[VMEM] * (cuts + 3),
        out_shape=[
            *[shape((rows // cuts, 128), BF16)] * cuts,
            shape((rows, 128), BF16),
            shape((7 * channels, edges), BF16),
            shape((8, edges), F32),
        ],
        scratch_shapes=[
            pltpu.VMEM((9 * channels, slots), BF16),
            pltpu.VMEM((9 * channels, atoms), BF16),
            pltpu.VMEM((9 * channels, CHUNK), F32),
            pltpu.VMEM((9 * channels, CHUNK), F32),
            pltpu.VMEM((7 * channels, edges), BF16),
            pltpu.VMEM((rows, 128), F32),
            pltpu.SMEM((1,), jnp.int32),
            pltpu.SemaphoreType.DMA,
        ],
        compiler_params=limits(24),
        cost_estimate=cost(9 * 10**9, 7 * 10**6),
        name="features",
    )(live, near, classes, zero, one, two, source, target)


def back_kernel(
    edge_ref, zero_ref, one_ref, two_ref, pulled_ref, *rest, pieces, members, atoms, face, places,
):
    piece_refs = rest[:pieces]
    own_ref, *ghost_refs = rest[pieces : pieces + 5]
    flat, weight_zero, weight_pair, field, turned, pick_all = rest[pieces + 5 :]
    rows = flat.shape[1]
    channels = own_ref.shape[2]
    slots = pick_all.shape[0]
    edges = pulled_ref.shape[1]
    zw, pw = 3 * channels, 2 * channels
    first = zw * zw // 128
    second = first + pw * pw // 128
    placed = [(piece, index) for piece in piece_refs for index in range(piece.shape[0])]
    for (piece, index), place in zip(placed, places()):
        height = piece.shape[2]
        at = pl.ds(pl.multiple_of(place, 16), height)
        for k in range(members):
            flat[k, at, :] = piece[index, k].astype(F32)
    for k in range(members):
        for j in range(zw // 128):
            weight_zero[:, k * zw + j * 128 : k * zw + (j + 1) * 128] = flat[
                k, pl.ds(j, zw, stride=zw // 128), :
            ].astype(BF16)
        for j in range(pw // 128):
            at = k * 2 * pw + j * 128
            weight_pair[:, at : at + 128] = flat[k, pl.ds(first + j, pw, stride=pw // 128), :].astype(BF16)
            weight_pair[:, at + pw : at + pw + 128] = flat[
                k, pl.ds(second + j, pw, stride=pw // 128), :
            ].astype(BF16)

    def chunk_step(chunk, carry):
        start = pl.multiple_of(chunk * CHUNK, CHUNK)
        here = pl.ds(start, CHUNK)
        slot = lax.broadcasted_iota(jnp.int32, (slots, CHUNK), 0).astype(F32)
        pick_all[:, here] = (slot == edge_ref[0:1, here]).astype(F32).astype(BF16)
        qz, qpn, qnp = [], [], []
        for k in range(members):
            mask = (edge_ref[1:2, here] == float(k)).astype(F32).astype(BF16)
            qz.append(pulled_ref[0:zw, here] * mask)
            qp = pulled_ref[zw : zw + pw, here] * mask
            qn = pulled_ref[zw + pw : zw + 2 * pw, here] * mask
            qpn += [qp, qn]
            qnp += [qn, -qp]
        field[0:zw, :] = nn(weight_zero[...], jnp.concatenate(qz, axis=0))
        field[zw : zw + pw, :] = nn(weight_pair[...], jnp.concatenate(qpn, axis=0))
        field[zw + pw : zw + 2 * pw, :] = nn(weight_pair[...], jnp.concatenate(qnp, axis=0))

        def sub_step(sub, inner):
            at = pl.multiple_of(sub * SUB, SUB)

            def part(c):
                return field[pl.ds(SLOT[c] * channels + at, SUB), :]

            def write(c, value):
                turned[pl.ds(c * channels + at, SUB), here] = value.astype(BF16)

            write(0, zero_ref[0:1, here] * part(0))
            values = [part(c) for c in (1, 2, 3)]
            for b in range(3):
                total = one_ref[0, b : b + 1, here] * values[0]
                for a in range(1, 3):
                    total += one_ref[a, b : b + 1, here] * values[a]
                write(1 + b, total)
            values = [part(c) for c in (5, 6, 7)]
            for b in range(5):
                total = two_ref[1, b : b + 1, here] * values[0]
                for a in range(2, 4):
                    total += two_ref[a, b : b + 1, here] * values[a - 1]
                write(4 + b, total)
            return inner

        lax.fori_loop(0, channels // SUB, sub_step, 0)
        return carry

    lax.fori_loop(0, edges // CHUNK, chunk_step, 0)
    for c in range(9):
        summed = nt(pick_all[...], turned[c * channels : (c + 1) * channels, :])
        own_ref[c] = summed[:atoms]
        blocks = [summed[atoms + block * face : atoms + (block + 1) * face] for block in range(4)]
        for side in range(2):
            even = lax.rem(lax.axis_index(("gx", "yz")[side]), 2) == 0
            low, high = blocks[2 * side], blocks[2 * side + 1]
            ghost_refs[3 - 2 * side][c] = jnp.where(even, high, low).astype(BF16)
            ghost_refs[2 - 2 * side][c] = jnp.where(even, low, high).astype(BF16)


def back(edge, zero, one, two, pulled, pieces, places, rows, atoms, slots, face):
    members = pieces[0].shape[1]
    edges = pulled.shape[1]
    channels = pulled.shape[0] // 7
    shape = jax.ShapeDtypeStruct
    return pl.pallas_call(
        functools.partial(
            back_kernel, pieces=len(pieces), members=members, atoms=atoms, face=face, places=places
        ),
        in_specs=[VMEM] * (5 + len(pieces)),
        out_specs=[VMEM] * 5,
        out_shape=[shape((9, atoms, channels), F32), *[shape((9, face, channels), BF16)] * 4],
        scratch_shapes=[
            pltpu.VMEM((members, rows, 128), F32),
            pltpu.VMEM((3 * channels, members * 3 * channels), BF16),
            pltpu.VMEM((2 * channels, members * 4 * channels), BF16),
            pltpu.VMEM((7 * channels, CHUNK), F32),
            pltpu.VMEM((9 * channels, edges), BF16),
            pltpu.VMEM((slots, edges), BF16),
        ],
        compiler_params=limits(24),
        cost_estimate=cost(9 * 10**9, 7 * 10**6),
        name="back",
    )(edge, zero, one, two, pulled, *pieces)


def pair_kernel(own_ref, *refs, cuts):
    came_refs, out_refs = refs[:cuts], refs[cuts:]
    row = lax.axis_index("yz")
    per = cuts // len(out_refs)
    height = came_refs[0].shape[0]
    for index, came_ref in enumerate(came_refs):
        at = pl.multiple_of((row ^ (index // per)) * per * height + index % per * height, 16)
        total = own_ref[pl.ds(at, height), :].astype(F32) + came_ref[...].astype(F32)
        out_refs[index // per][pl.ds(index % per * height, height), :] = total.astype(BF16)


def pair_sum(own, came, count):
    height = own.shape[0] // count
    return pl.pallas_call(
        functools.partial(pair_kernel, cuts=len(came)),
        in_specs=[VMEM] * (1 + len(came)),
        out_specs=[VMEM] * count,
        out_shape=[jax.ShapeDtypeStruct((height, 128), BF16)] * count,
        compiler_params=limits(6),
        cost_estimate=cost(10**6, 2 * 10**6),
        name="pair_sum",
    )(own, *came)


def total_kernel(*refs):
    total = refs[0][...].astype(F32)
    for ref in refs[1:-1]:
        total += ref[...].astype(F32)
    refs[-1][...] = total.astype(BF16)


def total_sum(parts):
    return pl.pallas_call(
        total_kernel,
        in_specs=[VMEM] * len(parts),
        out_specs=VMEM,
        out_shape=jax.ShapeDtypeStruct(parts[0].shape, BF16),
        compiler_params=limits(6),
        cost_estimate=cost(10**6, 10**6),
        name="total_sum",
    )(*parts)


def pack_kernel(*refs):
    for index, ref in enumerate(refs[:-1]):
        refs[-1][index] = ref[...]


def pack(pieces):
    return pl.pallas_call(
        pack_kernel,
        in_specs=[VMEM] * len(pieces),
        out_specs=VMEM,
        out_shape=jax.ShapeDtypeStruct((len(pieces), *pieces[0].shape), pieces[0].dtype),
        compiler_params=limits(6),
        cost_estimate=cost(10**5, 10**6),
        name="pack",
    )(*pieces)


def expert_kernel(coef_ref, *refs, scale):
    sums, out_ref, summed, staged, written = refs[:-4], *refs[-4:]
    owned = out_ref.shape[0]
    place = lax.axis_index("gx")
    row = lax.broadcasted_iota(jnp.int32, (owned, coef_ref.shape[1]), 0)
    col = lax.broadcasted_iota(jnp.int32, (owned, coef_ref.shape[1]), 1)
    chosen = col == row + place * owned
    picked = [
        jnp.sum(jnp.where(chosen, coef_ref[k : k + 1, :], 0.0), axis=1, keepdims=True) * scale for k in range(2)
    ]
    even = lax.rem(place, 2) == 0
    first = jnp.broadcast_to(jnp.where(even, picked[0], picked[1]), (owned, 128))
    second = jnp.broadcast_to(jnp.where(even, picked[1], picked[0]), (owned, 128))
    half = len(sums) // 2
    for side in range(2):
        total = sums[side * half][...].astype(F32)
        for ref in sums[side * half + 1 : (side + 1) * half]:
            total += ref[...].astype(F32)
        summed[side] = total
    rows = summed.shape[1]
    stripes = written.shape[0]
    copies = []
    for stripe in range(stripes):
        low, high = rows * stripe // stripes, rows * (stripe + 1) // stripes
        for row in range(low, high):
            staged[:, row * 128 : (row + 1) * 128] = (
                first * summed[0, row : row + 1, :] + second * summed[1, row : row + 1, :]
            )
        span = pl.ds(low * 128, (high - low) * 128)
        copies.append(pltpu.make_async_copy(staged.at[:, span], out_ref.at[:, span], written.at[stripe]))
        copies[-1].start()
    for copy in copies:
        copy.wait()


def expert_product(coef, sums, owned, scale):
    rows = sums[0].shape[0]
    return pl.pallas_call(
        functools.partial(expert_kernel, scale=scale),
        in_specs=[VMEM] * (1 + len(sums)),
        out_specs=HBM,
        out_shape=jax.ShapeDtypeStruct((owned, rows * 128), F32),
        scratch_shapes=[
            pltpu.VMEM((2, rows, 128), F32),
            pltpu.VMEM((owned, rows * 128), F32),
            pltpu.SemaphoreType.DMA((4,)),
        ],
        compiler_params=limits(8),
        cost_estimate=cost(10**6, 4 * 10**6),
        name="expert_product",
    )(coef, *sums)


def finish_kernel(send_ref, own_ref, a_ref, b_ref, c_ref, d_ref, out_ref):
    atoms = own_ref.shape[1]
    face = send_ref.shape[1]
    row = lax.broadcasted_iota(jnp.int32, (atoms, face), 0)
    picks = []
    for side in range(2):
        even = lax.rem(lax.axis_index(("gx", "yz")[side]), 2) == 0
        below, above = send_ref[2 * side : 2 * side + 1, :], send_ref[2 * side + 1 : 2 * side + 2, :]
        for faces in (jnp.where(even, above, below), jnp.where(even, below, above)):
            picks.append((row == faces).astype(F32).astype(BF16))
    picks = [picks[3], picks[2], picks[1], picks[0]]
    for c in range(9):
        total = own_ref[c]
        for pick, ref in zip(picks, (a_ref, b_ref, c_ref, d_ref)):
            total += nn(pick, ref[c])
        out_ref[c] = total.astype(BF16)


def finish(send, own, returned):
    return pl.pallas_call(
        finish_kernel,
        in_specs=[VMEM] * 6,
        out_specs=VMEM,
        out_shape=jax.ShapeDtypeStruct(own.shape, BF16),
        compiler_params=limits(6),
        cost_estimate=cost(10**8, 2 * 10**6),
        name="finish",
    )(send, own, *returned)


def swap(value, axis, bit):
    return lax.ppermute(value, axis, [(i, i ^ bit) for i in range(lax.axis_size(axis))])


def neighbour_pairs(value, axis, first):
    count = lax.axis_size(axis)
    moves = []
    for low in range(first, count, 2):
        high = (low + 1) % count
        moves += [(low, high), (high, low)]
    return lax.ppermute(value, axis, moves)


def local(
    saved_input, cotangent, neighbours, rot_zero, rot_one, rot_two, send_index, atom_class, live_blocks,
    merge_coef, experts,
):
    atoms, fanout = neighbours.shape
    slots = saved_input.shape[0]
    channels = cotangent.shape[2]
    face = send_index.shape[1]
    count_yz, count_gx = lax.axis_size("yz"), lax.axis_size("gx")
    row, column = lax.axis_index("yz"), lax.axis_index("gx")
    core = column % 2
    height = experts.shape[1] // 128
    rows = height * count_yz
    direct = height % 32 == 0 and count_yz == 4 and count_gx == 4
    cuts = 4 if direct else 1

    zero = rot_zero.reshape(1, -1)
    source = jnp.transpose(saved_input, (1, 0, 2))
    target = jnp.transpose(cotangent, (1, 0, 2))

    if direct:
        half = height // 2
        mine = merge(merge_coef, experts, 2)
        held = [mine] + [swap(mine, "yz", k) for k in (2, 1, 3)]
        source, target, mine = lax.optimization_barrier((source, target, mine))

        def places():
            here, side = lax.axis_index("yz"), lax.rem(lax.axis_index("gx"), 2)
            starts = [(here ^ k) * height for k in (0, 2, 1, 3)]
            return [at + side * half for at in starts] + [at + (1 - side) * half for at in starts]
    else:
        part = jnp.dot(merge_coef, experts.astype(F32), precision=lax.Precision.HIGHEST).astype(BF16)
        merged = lax.all_gather(part, "yz", axis=1, tiled=True)
        pieces = [merged.reshape(1, merged.shape[0], rows, 128)]

        def places():
            return [0]

    *other, own, pulled, edge = features(
        live_blocks, neighbours.T, atom_class.reshape(1, -1), zero, rot_one, rot_two, source, target, rows, fanout, cuts
    )
    if direct:
        came = [swap(piece, "gx", 1) for piece in other]
        received = lax.optimization_barrier((*came, *held))
        came, held = received[:cuts], received[cuts:]
        parts = pair_sum(own, came, count_yz)
        gathered = [parts[0]] + [swap(parts[k], "yz", k) for k in (3, 1, 2)]
        held = pack(held)
        pieces = [held, swap(held, "gx", 1)]
    grad_own, *ghosts = back(edge, zero, rot_one, rot_two, pulled, pieces, places, rows, atoms, slots, face)
    returned = [
        neighbour_pairs(ghost, axis, first)
        for ghost, axis, first in zip(ghosts, ("yz", "yz", "gx", "gx"), (1, 0, 1, 0))
    ]
    if direct:
        grad_own, *gathered = lax.optimization_barrier((grad_own, *gathered))
        summed, *returned = lax.optimization_barrier((total_sum(gathered), *returned))
        across = swap(summed, "gx", 2)
        input_grad = finish(send_index, grad_own, returned)
        across, input_grad = lax.optimization_barrier((across, input_grad))
        sums = [summed, across, swap(summed, "gx", 1), swap(across, "gx", 1)]
    else:
        mixed = jnp.stack([own, other[0]]).astype(F32)
        mixed = jnp.where(core == 0, mixed, mixed[::-1])
        whole = lax.psum(mixed, ("yz", "gx"))
        piece = lax.dynamic_slice_in_dim(whole, row * height, height, 1)
        piece = jnp.where(core == 0, piece, piece[::-1])
        sums = [piece[0], piece[1]]
        input_grad = finish(send_index, grad_own, returned)
    grad_scale = math.sqrt(fanout / (atoms * count_yz * count_gx))
    expert_grad = expert_product(merge_coef, sums, merge_coef.shape[1] // count_gx, grad_scale)
    return (jnp.transpose(input_grad, (1, 0, 2)), expert_grad)


def solution(mesh):
    tiles = ("rep", "yz", "gx")
    in_specs = (
        P(tiles, None, None),
        P(tiles, None, None),
        P(tiles, None),
        P(tiles),
        P(None, None, tiles),
        P(None, None, tiles),
        P(tiles, None),
        P(tiles),
        P(tiles),
        P(),
        P(None, "yz"),
    )
    out_specs = (P(tiles, None, None), P(("rep", "gx"), "yz"))
    return jax.shard_map(local, mesh=mesh, in_specs=in_specs, out_specs=out_specs, check_vma=False)
```

```python
import functools
import math

import jax
import jax.numpy as jnp
from jax import lax
from jax.experimental import pallas as pl
from jax.experimental.pallas import tpu as pltpu
from jax.sharding import PartitionSpec as P

LIVE_BLOCK = 64
CHUNK = 1024
SUB = 32
F32 = jnp.float32
BF16 = jnp.bfloat16

STACK = (0, 2, 6, 3, 7, 1, 5)
SLOT = {component: place for place, component in enumerate(STACK)}

VMEM = pl.BlockSpec(memory_space=pltpu.VMEM)
HBM = pl.BlockSpec(memory_space=pltpu.HBM)


def limits(mebibytes):
    return pltpu.CompilerParams(vmem_limit_bytes=mebibytes * 1024 * 1024)


def cost(flops, moved):
    return pl.CostEstimate(flops=flops, bytes_accessed=moved, transcendentals=0)


def nn(left, right):
    return lax.dot_general(left, right, (((1,), (0,)), ((), ())), preferred_element_type=F32)


def nt(left, right):
    return lax.dot_general(left, right, (((1,), (1,)), ((), ())), preferred_element_type=F32)


def split3(value):
    high = value.astype(BF16)
    rest = value - high.astype(F32)
    middle = rest.astype(BF16)
    low = (rest - middle.astype(F32)).astype(BF16)
    return high, middle, low


def merge_kernel(coef_in_ref, experts_ref, out_ref, held, coef_ref, arrived, coef_arrived):
    members, experts = coef_in_ref.shape
    rows = out_ref.shape[1]
    start = pl.multiple_of(lax.rem(lax.axis_index("gx"), 2) * rows * 128, 128)
    stripes = arrived.shape[0]
    blocks = rows // 16
    edges = [blocks * stripe // stripes for stripe in range(stripes + 1)]
    copies = []
    for stripe in range(stripes):
        at, wide = edges[stripe] * 2048, (edges[stripe + 1] - edges[stripe]) * 2048
        copies.append(
            pltpu.make_async_copy(
                experts_ref.at[:, pl.ds(start + at, wide)], held.at[:, pl.ds(at, wide)], arrived.at[stripe]
            )
        )
        copies[-1].start()
    coef_copy = pltpu.make_async_copy(coef_in_ref, coef_ref, coef_arrived)
    coef_copy.start()
    coef_copy.wait()
    wide = 8 * experts
    row = lax.broadcasted_iota(jnp.int32, (8, wide), 0)
    col = lax.broadcasted_iota(jnp.int32, (8, wide), 1)
    diagonal = row == col // experts
    source = lax.broadcasted_iota(jnp.int32, (experts, wide), 0)
    target = lax.broadcasted_iota(jnp.int32, (experts, wide), 1)
    tile = (source == target % experts).astype(F32).astype(BF16)
    lefts = []
    for term in split3(coef_ref[...]):
        tiled = nn(term, tile)
        for member in range(members):
            lefts.append(jnp.where(diagonal, tiled[member : member + 1, :], 0.0).astype(BF16))
    lefts = jnp.concatenate(lefts, axis=0)
    height = 8 * members
    for block in range(blocks):
        if block in edges:
            copies[edges.index(block)].wait()
        halves = []
        for half in range(2):
            first = block * 16 + half * 8
            groups = [held[:, (first + g) * 128 : (first + g + 1) * 128] for g in range(8)]
            halves.append(jnp.concatenate(groups, axis=0))
        product = nn(lefts, jnp.concatenate(halves, axis=1))
        total = product[:height] + product[height : 2 * height] + product[2 * height :]
        for member in range(members):
            part = total[member * 8 : member * 8 + 8]
            out_ref[member, block * 16 : block * 16 + 16, :] = jnp.concatenate(
                [part[:, :128], part[:, 128:]], axis=0
            ).astype(BF16)


def merge(coef, experts, parts):
    members, count = coef.shape
    columns = experts.shape[1] // parts
    rows = columns // 128
    return pl.pallas_call(
        merge_kernel,
        in_specs=[HBM, HBM],
        out_specs=VMEM,
        out_shape=jax.ShapeDtypeStruct((members, rows, 128), BF16),
        scratch_shapes=[
            pltpu.VMEM((count, columns), BF16),
            pltpu.VMEM((members, count), F32),
            pltpu.SemaphoreType.DMA((2,)),
            pltpu.SemaphoreType.DMA,
        ],
        compiler_params=limits(52),
        cost_estimate=cost(96 * 16 * columns, 2 * count * columns),
        name="merge",
    )(coef, experts)


def features_kernel(
    live_in_ref, near_ref, class_ref, zero_ref, one_ref, two_ref, source_ref, target_ref,
    *refs, fanout, cuts,
):
    other_refs, own_ref, pulled_ref, edge_ref = refs[:cuts], *refs[cuts : cuts + 3]
    source_t, target_t, moved, spread, rotated, grads, live_ref, live_arrived = refs[cuts + 3 :]
    slots, channels = source_ref.shape[1:]
    atoms = target_ref.shape[1]
    edges = atoms * fanout
    live_copy = pltpu.make_async_copy(live_in_ref, live_ref, live_arrived)
    live_copy.start()
    for c in range(9):
        source_t[c * channels : (c + 1) * channels, :] = source_ref[c].T
        target_t[c * channels : (c + 1) * channels, :] = target_ref[c].T
    near = near_ref[...].astype(F32).astype(BF16)
    classes = class_ref[...].astype(F32).astype(BF16)
    scale = 1.0 / math.sqrt(fanout)

    def chunk_step(chunk, carry):
        start = pl.multiple_of(chunk * CHUNK, CHUNK)
        here = pl.ds(start, CHUNK)
        edge = lax.broadcasted_iota(jnp.int32, (atoms, CHUNK), 1) + start
        atom = lax.broadcasted_iota(jnp.int32, (atoms, CHUNK), 0)
        repeat = (edge // fanout == atom).astype(F32).astype(BF16)
        edge8 = lax.broadcasted_iota(jnp.int32, (fanout, CHUNK), 1) + start
        lane8 = lax.broadcasted_iota(jnp.int32, (fanout, CHUNK), 0)
        picked = jnp.where(edge8 % fanout == lane8, nn(near, repeat), 0.0)
        near_row = jnp.sum(picked, axis=0, keepdims=True)
        class_row = nn(classes, repeat)
        edge_ref[0:1, here] = near_row
        edge_ref[1:2, here] = class_row
        slot = lax.broadcasted_iota(jnp.int32, (slots, CHUNK), 0).astype(F32)
        pick = (slot == near_row).astype(F32).astype(BF16)
        moved[...] = nn(source_t[...], pick)
        spread[...] = nn(target_t[...], repeat)

        def sub_step(sub, inner):
            at = pl.multiple_of(sub * SUB, SUB)

            def turn(field, write):
                def part(c):
                    return field[pl.ds(c * channels + at, SUB), :]

                write(0, zero_ref[0:1, here] * part(0))
                values = [part(c) for c in (1, 2, 3)]
                for a in range(3):
                    total = one_ref[a, 0:1, here] * values[0]
                    for b in range(1, 3):
                        total += one_ref[a, b : b + 1, here] * values[b]
                    write(1 + a, total)
                values = [part(c) for c in (4, 5, 6, 7, 8)]
                for a in range(1, 4):
                    total = two_ref[a, 0:1, here] * values[0]
                    for b in range(1, 5):
                        total += two_ref[a, b : b + 1, here] * values[b]
                    write(4 + a, total)

            def write_rotated(c, value):
                rotated[pl.ds(SLOT[c] * channels + at, SUB), here] = value.astype(BF16)

            def write_pulled(c, value):
                pulled_ref[pl.ds(SLOT[c] * channels + at, SUB), here] = (value * scale).astype(BF16)

            turn(moved, write_rotated)
            turn(spread, write_pulled)
            return inner

        lax.fori_loop(0, channels // SUB, sub_step, 0)
        return carry

    lax.fori_loop(0, edges // CHUNK, chunk_step, 0)
    live_copy.wait()
    edge_row = lax.broadcasted_iota(jnp.int32, (1, edges), 1)
    edge_ref[1:2, :] = jnp.where(edge_row < live_ref[0] * LIVE_BLOCK * fanout, edge_ref[1:2, :], -1.0)
    zw, pw = 3 * channels, 2 * channels
    first = zw * zw // 128
    second = first + pw * pw // 128
    own = lax.rem(lax.axis_index("gx"), 2).astype(F32)
    for out_refs, wanted in ((other_refs, 1.0 - own), ((own_ref,), own)):
        mask = (edge_ref[1:2, :] == wanted).astype(F32).astype(BF16)
        qz = pulled_ref[0:zw, :] * mask
        qp = pulled_ref[zw : zw + pw, :] * mask
        qn = pulled_ref[zw + pw : zw + 2 * pw, :] * mask
        z, p, n = rotated[0:zw, :], rotated[zw : zw + pw, :], rotated[zw + pw : zw + 2 * pw, :]
        whole = nt(z, qz)
        for j in range(zw // 128):
            grads[pl.ds(j, zw, stride=zw // 128), :] = whole[:, j * 128 : (j + 1) * 128]
        coupled = nt(p, qp) + nt(n, qn)
        crossed = nt(p, qn) - nt(n, qp)
        for j in range(pw // 128):
            grads[pl.ds(first + j, pw, stride=pw // 128), :] = coupled[:, j * 128 : (j + 1) * 128]
            grads[pl.ds(second + j, pw, stride=pw // 128), :] = crossed[:, j * 128 : (j + 1) * 128]
        height = out_refs[0].shape[0]
        for index, out_ref in enumerate(out_refs):
            per = max(len(out_refs) // 4, 1)
            at = (lax.axis_index("yz") ^ (index // per)) * per * height + index % per * height
            at = pl.multiple_of(at, 16) if len(out_refs) > 1 else 0
            out_ref[...] = grads[pl.ds(at, height), :].astype(BF16)


def features(live, near, classes, zero, one, two, source, target, rows, fanout, cuts):
    slots, channels = source.shape[1:]
    atoms = target.shape[1]
    edges = atoms * fanout
    shape = jax.ShapeDtypeStruct
    return pl.pallas_call(
        functools.partial(features_kernel, fanout=fanout, cuts=cuts),
        in_specs=[HBM] + [VMEM] * 7,
        out_specs=[VMEM] * (cuts + 3),
        out_shape=[
            *[shape((rows // cuts, 128), BF16)] * cuts,
            shape((rows, 128), BF16),
            shape((7 * channels, edges), BF16),
            shape((8, edges), F32),
        ],
        scratch_shapes=[
            pltpu.VMEM((9 * channels, slots), BF16),
            pltpu.VMEM((9 * channels, atoms), BF16),
            pltpu.VMEM((9 * channels, CHUNK), F32),
            pltpu.VMEM((9 * channels, CHUNK), F32),
            pltpu.VMEM((7 * channels, edges), BF16),
            pltpu.VMEM((rows, 128), F32),
            pltpu.SMEM((1,), jnp.int32),
            pltpu.SemaphoreType.DMA,
        ],
        compiler_params=limits(24),
        cost_estimate=cost(9 * 10**9, 7 * 10**6),
        name="features",
    )(live, near, classes, zero, one, two, source, target)


def back_kernel(
    edge_ref, zero_ref, one_ref, two_ref, pulled_ref, *rest, pieces, members, atoms, face, places,
):
    piece_refs = rest[:pieces]
    own_ref, *ghost_refs = rest[pieces : pieces + 5]
    flat, weight_zero, weight_pair, field, turned, pick_all = rest[pieces + 5 :]
    rows = flat.shape[1]
    channels = own_ref.shape[2]
    slots = pick_all.shape[0]
    edges = pulled_ref.shape[1]
    zw, pw = 3 * channels, 2 * channels
    first = zw * zw // 128
    second = first + pw * pw // 128
    placed = [(piece, index) for piece in piece_refs for index in range(piece.shape[0])]
    for (piece, index), place in zip(placed, places()):
        height = piece.shape[2]
        at = pl.ds(pl.multiple_of(place, 16), height)
        for k in range(members):
            flat[k, at, :] = piece[index, k].astype(F32)
    for k in range(members):
        for j in range(zw // 128):
            weight_zero[:, k * zw + j * 128 : k * zw + (j + 1) * 128] = flat[
                k, pl.ds(j, zw, stride=zw // 128), :
            ].astype(BF16)
        for j in range(pw // 128):
            at = k * 2 * pw + j * 128
            weight_pair[:, at : at + 128] = flat[k, pl.ds(first + j, pw, stride=pw // 128), :].astype(BF16)
            weight_pair[:, at + pw : at + pw + 128] = flat[
                k, pl.ds(second + j, pw, stride=pw // 128), :
            ].astype(BF16)

    def chunk_step(chunk, carry):
        start = pl.multiple_of(chunk * CHUNK, CHUNK)
        here = pl.ds(start, CHUNK)
        slot = lax.broadcasted_iota(jnp.int32, (slots, CHUNK), 0).astype(F32)
        pick_all[:, here] = (slot == edge_ref[0:1, here]).astype(F32).astype(BF16)
        qz, qpn, qnp = [], [], []
        for k in range(members):
            mask = (edge_ref[1:2, here] == float(k)).astype(F32).astype(BF16)
            qz.append(pulled_ref[0:zw, here] * mask)
            qp = pulled_ref[zw : zw + pw, here] * mask
            qn = pulled_ref[zw + pw : zw + 2 * pw, here] * mask
            qpn += [qp, qn]
            qnp += [qn, -qp]
        field[0:zw, :] = nn(weight_zero[...], jnp.concatenate(qz, axis=0))
        field[zw : zw + pw, :] = nn(weight_pair[...], jnp.concatenate(qpn, axis=0))
        field[zw + pw : zw + 2 * pw, :] = nn(weight_pair[...], jnp.concatenate(qnp, axis=0))

        def sub_step(sub, inner):
            at = pl.multiple_of(sub * SUB, SUB)

            def part(c):
                return field[pl.ds(SLOT[c] * channels + at, SUB), :]

            def write(c, value):
                turned[pl.ds(c * channels + at, SUB), here] = value.astype(BF16)

            write(0, zero_ref[0:1, here] * part(0))
            values = [part(c) for c in (1, 2, 3)]
            for b in range(3):
                total = one_ref[0, b : b + 1, here] * values[0]
                for a in range(1, 3):
                    total += one_ref[a, b : b + 1, here] * values[a]
                write(1 + b, total)
            values = [part(c) for c in (5, 6, 7)]
            for b in range(5):
                total = two_ref[1, b : b + 1, here] * values[0]
                for a in range(2, 4):
                    total += two_ref[a, b : b + 1, here] * values[a - 1]
                write(4 + b, total)
            return inner

        lax.fori_loop(0, channels // SUB, sub_step, 0)
        return carry

    lax.fori_loop(0, edges // CHUNK, chunk_step, 0)
    for c in range(9):
        summed = nt(pick_all[...], turned[c * channels : (c + 1) * channels, :])
        own_ref[c] = summed[:atoms]
        blocks = [summed[atoms + block * face : atoms + (block + 1) * face] for block in range(4)]
        for side in range(2):
            even = lax.rem(lax.axis_index(("gx", "yz")[side]), 2) == 0
            low, high = blocks[2 * side], blocks[2 * side + 1]
            ghost_refs[3 - 2 * side][c] = jnp.where(even, high, low).astype(BF16)
            ghost_refs[2 - 2 * side][c] = jnp.where(even, low, high).astype(BF16)


def back(edge, zero, one, two, pulled, pieces, places, rows, atoms, slots, face):
    members = pieces[0].shape[1]
    edges = pulled.shape[1]
    channels = pulled.shape[0] // 7
    shape = jax.ShapeDtypeStruct
    return pl.pallas_call(
        functools.partial(
            back_kernel, pieces=len(pieces), members=members, atoms=atoms, face=face, places=places
        ),
        in_specs=[VMEM] * (5 + len(pieces)),
        out_specs=[VMEM] * 5,
        out_shape=[shape((9, atoms, channels), F32), *[shape((9, face, channels), BF16)] * 4],
        scratch_shapes=[
            pltpu.VMEM((members, rows, 128), F32),
            pltpu.VMEM((3 * channels, members * 3 * channels), BF16),
            pltpu.VMEM((2 * channels, members * 4 * channels), BF16),
            pltpu.VMEM((7 * channels, CHUNK), F32),
            pltpu.VMEM((9 * channels, edges), BF16),
            pltpu.VMEM((slots, edges), BF16),
        ],
        compiler_params=limits(24),
        cost_estimate=cost(9 * 10**9, 7 * 10**6),
        name="back",
    )(edge, zero, one, two, pulled, *pieces)


def pair_kernel(own_ref, *refs, cuts):
    came_refs, out_refs = refs[:cuts], refs[cuts:]
    row = lax.axis_index("yz")
    per = cuts // len(out_refs)
    height = came_refs[0].shape[0]
    for index, came_ref in enumerate(came_refs):
        at = pl.multiple_of((row ^ (index // per)) * per * height + index % per * height, 16)
        total = own_ref[pl.ds(at, height), :].astype(F32) + came_ref[...].astype(F32)
        out_refs[index // per][pl.ds(index % per * height, height), :] = total.astype(BF16)


def pair_sum(own, came, count):
    height = own.shape[0] // count
    return pl.pallas_call(
        functools.partial(pair_kernel, cuts=len(came)),
        in_specs=[VMEM] * (1 + len(came)),
        out_specs=[VMEM] * count,
        out_shape=[jax.ShapeDtypeStruct((height, 128), BF16)] * count,
        compiler_params=limits(6),
        cost_estimate=cost(10**6, 2 * 10**6),
        name="pair_sum",
    )(own, *came)


def total_kernel(*refs):
    total = refs[0][...].astype(F32)
    for ref in refs[1:-1]:
        total += ref[...].astype(F32)
    refs[-1][...] = total.astype(BF16)


def total_sum(parts):
    return pl.pallas_call(
        total_kernel,
        in_specs=[VMEM] * len(parts),
        out_specs=VMEM,
        out_shape=jax.ShapeDtypeStruct(parts[0].shape, BF16),
        compiler_params=limits(6),
        cost_estimate=cost(10**6, 10**6),
        name="total_sum",
    )(*parts)


def pack_kernel(*refs):
    for index, ref in enumerate(refs[:-1]):
        refs[-1][index] = ref[...]


def pack(pieces):
    return pl.pallas_call(
        pack_kernel,
        in_specs=[VMEM] * len(pieces),
        out_specs=VMEM,
        out_shape=jax.ShapeDtypeStruct((len(pieces), *pieces[0].shape), pieces[0].dtype),
        compiler_params=limits(6),
        cost_estimate=cost(10**5, 10**6),
        name="pack",
    )(*pieces)


def expert_kernel(coef_ref, *refs, scale):
    sums, out_ref, summed, staged, written = refs[:-4], *refs[-4:]
    owned = out_ref.shape[0]
    place = lax.axis_index("gx")
    row = lax.broadcasted_iota(jnp.int32, (owned, coef_ref.shape[1]), 0)
    col = lax.broadcasted_iota(jnp.int32, (owned, coef_ref.shape[1]), 1)
    chosen = col == row + place * owned
    picked = [
        jnp.sum(jnp.where(chosen, coef_ref[k : k + 1, :], 0.0), axis=1, keepdims=True) * scale for k in range(2)
    ]
    even = lax.rem(place, 2) == 0
    first = jnp.broadcast_to(jnp.where(even, picked[0], picked[1]), (owned, 128))
    second = jnp.broadcast_to(jnp.where(even, picked[1], picked[0]), (owned, 128))
    half = len(sums) // 2
    for side in range(2):
        total = sums[side * half][...].astype(F32)
        for ref in sums[side * half + 1 : (side + 1) * half]:
            total += ref[...].astype(F32)
        summed[side] = total
    rows = summed.shape[1]
    stripes = written.shape[0]
    copies = []
    for stripe in range(stripes):
        low, high = rows * stripe // stripes, rows * (stripe + 1) // stripes
        for row in range(low, high):
            staged[:, row * 128 : (row + 1) * 128] = (
                first * summed[0, row : row + 1, :] + second * summed[1, row : row + 1, :]
            )
        span = pl.ds(low * 128, (high - low) * 128)
        copies.append(pltpu.make_async_copy(staged.at[:, span], out_ref.at[:, span], written.at[stripe]))
        copies[-1].start()
    for copy in copies:
        copy.wait()


def expert_product(coef, sums, owned, scale):
    rows = sums[0].shape[0]
    return pl.pallas_call(
        functools.partial(expert_kernel, scale=scale),
        in_specs=[VMEM] * (1 + len(sums)),
        out_specs=HBM,
        out_shape=jax.ShapeDtypeStruct((owned, rows * 128), F32),
        scratch_shapes=[
            pltpu.VMEM((2, rows, 128), F32),
            pltpu.VMEM((owned, rows * 128), F32),
            pltpu.SemaphoreType.DMA((4,)),
        ],
        compiler_params=limits(8),
        cost_estimate=cost(10**6, 4 * 10**6),
        name="expert_product",
    )(coef, *sums)


def finish_kernel(send_ref, own_ref, a_ref, b_ref, c_ref, d_ref, out_ref):
    atoms = own_ref.shape[1]
    face = send_ref.shape[1]
    row = lax.broadcasted_iota(jnp.int32, (atoms, face), 0)
    picks = []
    for side in range(2):
        even = lax.rem(lax.axis_index(("gx", "yz")[side]), 2) == 0
        below, above = send_ref[2 * side : 2 * side + 1, :], send_ref[2 * side + 1 : 2 * side + 2, :]
        for faces in (jnp.where(even, above, below), jnp.where(even, below, above)):
            picks.append((row == faces).astype(F32).astype(BF16))
    picks = [picks[3], picks[2], picks[1], picks[0]]
    for c in range(9):
        total = own_ref[c]
        for pick, ref in zip(picks, (a_ref, b_ref, c_ref, d_ref)):
            total += nn(pick, ref[c])
        out_ref[c] = total.astype(BF16)


def finish(send, own, returned):
    return pl.pallas_call(
        finish_kernel,
        in_specs=[VMEM] * 6,
        out_specs=VMEM,
        out_shape=jax.ShapeDtypeStruct(own.shape, BF16),
        compiler_params=limits(6),
        cost_estimate=cost(10**8, 2 * 10**6),
        name="finish",
    )(send, own, *returned)


def swap(value, axis, bit):
    return lax.ppermute(value, axis, [(i, i ^ bit) for i in range(lax.axis_size(axis))])


def neighbour_pairs(value, axis, first):
    count = lax.axis_size(axis)
    moves = []
    for low in range(first, count, 2):
        high = (low + 1) % count
        moves += [(low, high), (high, low)]
    return lax.ppermute(value, axis, moves)


def local(
    saved_input, cotangent, neighbours, rot_zero, rot_one, rot_two, send_index, atom_class, live_blocks,
    merge_coef, experts,
):
    atoms, fanout = neighbours.shape
    slots = saved_input.shape[0]
    channels = cotangent.shape[2]
    face = send_index.shape[1]
    count_yz, count_gx = lax.axis_size("yz"), lax.axis_size("gx")
    row, column = lax.axis_index("yz"), lax.axis_index("gx")
    core = column % 2
    height = experts.shape[1] // 128
    rows = height * count_yz
    direct = height % 32 == 0 and count_yz == 4 and count_gx == 4
    cuts = 4 if direct else 1

    zero = rot_zero.reshape(1, -1)
    source = jnp.transpose(saved_input, (1, 0, 2))
    target = jnp.transpose(cotangent, (1, 0, 2))

    if direct:
        half = height // 2
        mine = merge(merge_coef, experts, 2)
        held = [mine] + [swap(mine, "yz", k) for k in (2, 1, 3)]
        source, target, mine = lax.optimization_barrier((source, target, mine))

        def places():
            here, side = lax.axis_index("yz"), lax.rem(lax.axis_index("gx"), 2)
            starts = [(here ^ k) * height for k in (0, 2, 1, 3)]
            return [at + side * half for at in starts] + [at + (1 - side) * half for at in starts]
    else:
        part = jnp.dot(merge_coef, experts.astype(F32), precision=lax.Precision.HIGHEST).astype(BF16)
        merged = lax.all_gather(part, "yz", axis=1, tiled=True)
        pieces = [merged.reshape(1, merged.shape[0], rows, 128)]

        def places():
            return [0]

    *other, own, pulled, edge = features(
        live_blocks, neighbours.T, atom_class.reshape(1, -1), zero, rot_one, rot_two, source, target, rows, fanout, cuts
    )
    if direct:
        came = [swap(piece, "gx", 1) for piece in other]
        received = lax.optimization_barrier((*came, *held))
        came, held = received[:cuts], received[cuts:]
        parts = pair_sum(own, came, count_yz)
        gathered = [parts[0]] + [swap(parts[k], "yz", k) for k in (3, 1, 2)]
        held = pack(held)
        pieces = [held, swap(held, "gx", 1)]
    grad_own, *ghosts = back(edge, zero, rot_one, rot_two, pulled, pieces, places, rows, atoms, slots, face)
    returned = [
        neighbour_pairs(ghost, axis, first)
        for ghost, axis, first in zip(ghosts, ("yz", "yz", "gx", "gx"), (1, 0, 1, 0))
    ]
    if direct:
        grad_own, *gathered = lax.optimization_barrier((grad_own, *gathered))
        summed, *returned = lax.optimization_barrier((total_sum(gathered), *returned))
        across = swap(summed, "gx", 2)
        input_grad = finish(send_index, grad_own, returned)
        across, input_grad = lax.optimization_barrier((across, input_grad))
        sums = [summed, across, swap(summed, "gx", 1), swap(across, "gx", 1)]
    else:
        mixed = jnp.stack([own, other[0]]).astype(F32)
        mixed = jnp.where(core == 0, mixed, mixed[::-1])
        whole = lax.psum(mixed, ("yz", "gx"))
        piece = lax.dynamic_slice_in_dim(whole, row * height, height, 1)
        piece = jnp.where(core == 0, piece, piece[::-1])
        sums = [piece[0], piece[1]]
        input_grad = finish(send_index, grad_own, returned)
    grad_scale = math.sqrt(fanout / (atoms * count_yz * count_gx))
    expert_grad = expert_product(merge_coef, sums, merge_coef.shape[1] // count_gx, grad_scale)
    return (jnp.transpose(input_grad, (1, 0, 2)), expert_grad)


def solution(mesh):
    tiles = ("rep", "yz", "gx")
    in_specs = (
        P(tiles, None, None),
        P(tiles, None, None),
        P(tiles, None),
        P(tiles),
        P(None, None, tiles),
        P(None, None, tiles),
        P(tiles, None),
        P(tiles),
        P(tiles),
        P(),
        P(None, "yz"),
    )
    out_specs = (P(tiles, None, None), P(("rep", "gx"), "yz"))
    return jax.shard_map(local, mesh=mesh, in_specs=in_specs, out_specs=out_specs, check_vma=False)
```
